32 devices in a mesh: pb: 8 (over y, x, core), pa: 4 (over z).
Axes of the slice: x: 2, y: 2, z: 4, core: 2. Of those that a mesh axis runs over, the one named last changes fastest.
Arguments:
- hidden: bfloat16 [32, 128, 768], P(('pb', 'pa')), may hold values from -6 to 6
- encoder: bfloat16 [32, 4, 384, 768], P('pb', 'pa'), may hold values from -6 to 6
- lengths: int32 [32, 4], P('pb', 'pa'), may hold values from 1 to 384, 1152 in all within a row
- w_sq: bfloat16 [768, 768], replicated, may hold values from -0.21875 to 0.21875
- w_sk: bfloat16 [768, 768], replicated, may hold values from -0.21875 to 0.21875
- w_sv: bfloat16 [768, 768], replicated, may hold values from -0.21875 to 0.21875
- w_so: bfloat16 [768, 768], replicated, may hold values from -1.75 to 1.75
- w_cq: bfloat16 [768, 768], replicated, may hold values from -0.21875 to 0.21875
- w_ck: bfloat16 [768, 768], replicated, may hold values from -0.21875 to 0.21875
- w_cv: bfloat16 [768, 768], replicated, may hold values from -0.21875 to 0.21875
- w_co: bfloat16 [768, 768], replicated, may hold values from -6 to 6
- w_in: bfloat16 [768, 3072], replicated, may hold values from -0.21875 to 0.21875
- w_out: bfloat16 [3072, 768], replicated, may hold values from -0.109375 to 0.109375
- gain_self: float32 [768], replicated, may hold values from 0.5 to 1.5
- gain_cross: float32 [768], replicated, may hold values from 0.5 to 1.5
- gain_ffn: float32 [768], replicated, may hold values from 0.5 to 1.5
- cotangent: bfloat16 [32, 128, 768], P(('pb', 'pa')), may hold values from -6 to 6
Outputs:
- out: bfloat16 [32, 128, 768], P(('pb', 'pa'))
- grad_hidden: bfloat16 [32, 128, 768], P(('pb', 'pa'))
- grad_encoder: bfloat16 [32, 4, 384, 768], P('pb', 'pa')
- grad_w_sq: float32 [768, 768], P('pa')
- grad_w_sk: float32 [768, 768], P('pa')
- grad_w_sv: float32 [768, 768], P('pa')
- grad_w_so: float32 [768, 768], P('pa')
- grad_w_cq: float32 [768, 768], P('pa')
- grad_w_ck: float32 [768, 768], P('pa')
- grad_w_cv: float32 [768, 768], P('pa')
- grad_w_co: float32 [768, 768], P('pa')
- grad_w_in: float32 [768, 3072], P('pa')
- grad_w_out: float32 [3072, 768], P('pa')
- grad_gain_self: float32 [768], P('pa')
- grad_gain_cross: float32 [768], P('pa')
- grad_gain_ffn: float32 [768], P('pa')
The draws below stay inside these ranges and needn't reach their ends.
Inputs may be any that keep to these rules, and one draw needn't show every extreme that they name: Every passage has at least one true token and each question has a passage of exactly 384 true tokens; the lengths of a question sum to 1152.
All inputs are finite; a program needn't handle non-finite values. No bound on the sum of `lengths` on one device may be relied on, other than what follows from the above.
Results may differ from the reference program's by a relative error of at most 0.02.
Values may be sent and summed in bfloat16 or wider, within the bound.
No kernel may reach another device: no remote copies, remote signals or barrier semaphores. Data moves between devices by JAX's collectives and lax.ppermute only.
A program may use at most 192 MiB of HBM per device.

```python
import math
import jax
import jax.numpy as jnp
import numpy as np
from jax import lax

D = 768
HEADS = 12
HD = 64
FF = 3072
DEC = 128
PLEN = 384
PASSAGES = 4
NQ = 32


def block_levels(rng, dims, shards, smallest, top_value):
    loudness, own = 1.0, jax.random.fold_in(rng, 6)
    for axis_at, shards_of in shards:
        draws = jnp.exp(jax.random.uniform(jax.random.fold_in(own, axis_at), (shards_of,), jnp.float32, smallest / len(shards), top_value / len(shards)))
        loudness = loudness * jnp.repeat(draws, dims[axis_at] // shards_of).reshape([-1 if axis == axis_at else 1 for axis in range(len(dims))])
    return loudness


def split_up(count, total, bound, skew):
    portions = [(1 << 20) // math.isqrt(rank ** skew) + 1 for rank in range(2, count + 1)]
    spare, given = total - bound - (count - 1), [1] * (count - 1)
    while spare > 0:
        candidates = [i for i in range(count - 1) if given[i] < bound]
        pool, remaining = sum([portions[i] for i in candidates]), spare
        for i in candidates:
            addition = min(bound - given[i], max(1, remaining * portions[i] // pool), spare)
            given[i] = given[i] + addition
            spare = spare - addition
    return np.array([bound] + given)


def ragged_sizes(rng, number_of, total, limit, slope):
    if number_of == 2:
        one = jax.random.randint(rng, (), max(1, total - limit), min(limit, total - 1) + 1)
        return jnp.stack([one, total - one])
    sizes = jnp.asarray(split_up(number_of, total, limit, slope), jnp.int32)
    couples = (number_of - 1) // 2
    giver, receiver = sizes[1:1 + 2 * couples:2], sizes[2:2 + 2 * couples:2]
    room = jnp.minimum(giver - 1, limit - receiver)
    shifted = jax.random.randint(jax.random.fold_in(rng, 1), (couples,), 0, 1 << 20) % (room + 1)
    sizes = sizes.at[1:1 + 2 * couples:2].set(giver - shifted).at[2:2 + 2 * couples:2].set(receiver + shifted)
    return sizes[jax.random.permutation(jax.random.fold_in(rng, 2), number_of)]


def normal_values(rng, extent, width, bound, shards=(), kind=jnp.bfloat16):
    drawn = jax.random.normal(rng, extent, jnp.float32) * width
    if len(shards) > 0:
        drawn = block_levels(rng, extent, shards, -0.22, 0.18) * drawn
    return jnp.clip(drawn, min=-bound, max=bound).astype(kind)


def setup_inputs(seed: int = 0) -> dict:
    keys = jax.random.split(jax.random.key(seed), 18)
    hidden = normal_values(keys[0], (NQ, DEC, D), 1.0, 6.0, ((0, 32),))
    encoder = normal_values(keys[1], (NQ, PASSAGES, PLEN, D), 1.0, 6.0, ((0, 8), (1, 4)))
    lengths = jax.vmap(lambda own: ragged_sizes(own, PASSAGES, PASSAGES * PLEN * 3 // 4, PLEN, 1))(jax.random.split(keys[2], NQ)).reshape((NQ, PASSAGES)).astype(jnp.int32)
    w_sq = normal_values(keys[3], (D, D), D ** -0.5, 0.21875)
    w_sk = normal_values(keys[4], (D, D), D ** -0.5, 0.21875)
    w_sv = normal_values(keys[5], (D, D), D ** -0.5, 0.21875)
    w_so = normal_values(keys[6], (D, D), (max(1, 2 * D // DEC)) ** -0.5, 1.75)
    w_cq = normal_values(keys[7], (D, D), D ** -0.5, 0.21875)
    w_ck = normal_values(keys[8], (D, D), D ** -0.5, 0.21875)
    w_cv = normal_values(keys[9], (D, D), D ** -0.5, 0.21875)
    w_co = normal_values(keys[10], (D, D), (max(1, 2 * D // (PASSAGES * PLEN))) ** -0.5, 6.0)
    w_in = normal_values(keys[11], (D, FF), D ** -0.5, 0.21875)
    w_out = normal_values(keys[12], (FF, D), FF ** -0.5, 0.109375)
    gain_self = jnp.clip(1.0 + 0.1 * jax.random.normal(keys[13], (D,), jnp.float32), 0.5, 1.5)
    gain_cross = jnp.clip(1.0 + 0.1 * jax.random.normal(keys[14], (D,), jnp.float32), 0.5, 1.5)
    gain_ffn = jnp.clip(1.0 + 0.1 * jax.random.normal(keys[15], (D,), jnp.float32), 0.5, 1.5)
    cotangent = normal_values(keys[16], (NQ, DEC, D), 1.0, 6.0, ((0, 32),))
    return {"hidden": hidden, "encoder": encoder, "lengths": lengths, "w_sq": w_sq, "w_sk": w_sk, "w_sv": w_sv, "w_so": w_so, "w_cq": w_cq, "w_ck": w_ck, "w_cv": w_cv, "w_co": w_co, "w_in": w_in, "w_out": w_out, "gain_self": gain_self, "gain_cross": gain_cross, "gain_ffn": gain_ffn, "cotangent": cotangent}


EPS = 1e-06
NEG = -1000000000.0

@jax.custom_vjp
def low(v):
    return lax.optimization_barrier(v.astype(jnp.bfloat16)).astype(jnp.float32)

@jax.custom_vjp
def low_back(v):
    return v

def low_keep(v):
    return (low(v), None)

def low_pass(kept, grad):
    return (grad,)

def back_keep(v):
    return (v, None)

def back_low(kept, grad):
    return (low(grad),)
low.defvjp(low_keep, low_pass)
low_back.defvjp(back_keep, back_low)

def highest(left, right):
    return jnp.dot(left, right, precision=lax.Precision.HIGHEST)

def rms_gain(stream, gain):
    return stream * lax.rsqrt(lax.optimization_barrier(jnp.mean(stream * stream, axis=-1, keepdims=True)) + EPS) * gain

def attend(queries, key_rows, value_rows, allowed):
    q_heads = queries.reshape(queries.shape[0], HEADS, HD)
    k_heads = key_rows.reshape(key_rows.shape[0], HEADS, HD)
    v_heads = value_rows.reshape(value_rows.shape[0], HEADS, HD)
    scores = jnp.einsum('thd,shd->hts', q_heads, k_heads, precision=lax.Precision.HIGHEST) * HD ** (-0.5)
    scores = low_back(scores)
    scores = jnp.where(allowed[None], scores, NEG)
    row_max = lax.optimization_barrier(jnp.max(scores, axis=-1, keepdims=True))
    weights = jnp.exp(scores - row_max)
    attn_probs = low(weights / lax.optimization_barrier(jnp.sum(weights, axis=-1, keepdims=True)))
    mixture = jnp.einsum('hts,shd->thd', attn_probs, v_heads, precision=lax.Precision.HIGHEST)
    return mixture.reshape(queries.shape[0], HEADS * HD)

def question(stream, enc_rows, passage_len, params):
    w_sq, w_sk, w_sv, w_so, w_cq, w_ck, w_cv, w_co, w_in, w_out, gain_self, gain_cross, gain_ffn = params
    x_self = low(rms_gain(stream, gain_self))
    self_q = low_back(low(highest(x_self, w_sq)))
    self_k = low_back(low(highest(x_self, w_sk)))
    self_v = low_back(low(highest(x_self, w_sv)))
    causal = jnp.arange(DEC)[:, None] >= jnp.arange(DEC)[None, :]
    self_mix = low_back(low(attend(self_q, self_k, self_v, causal)))
    after_self = stream + low_back(highest(self_mix, w_so))
    x_cross = low(rms_gain(after_self, gain_cross))
    cross_q = low_back(low(highest(x_cross, w_cq)))
    enc_flat = enc_rows.reshape(PASSAGES * PLEN, D)
    cross_k = low_back(low(highest(enc_flat, w_ck)))
    cross_v = low_back(low(highest(enc_flat, w_cv)))
    key_valid = (jnp.arange(PLEN)[None, :] < passage_len[:, None]).reshape(PASSAGES * PLEN)
    allowed = jnp.broadcast_to(key_valid[None, :], (DEC, PASSAGES * PLEN))
    cross_mix = low_back(low(attend(cross_q, cross_k, cross_v, allowed)))
    after_cross = after_self + low_back(highest(cross_mix, w_co))
    x_ffn = low(rms_gain(after_cross, gain_ffn))
    preact = low_back(highest(x_ffn, w_in))
    activated = low(jax.nn.gelu(preact))
    return after_cross + low_back(highest(activated, w_out))

def reference(hidden, encoder, lengths, w_sq, w_sk, w_sv, w_so, w_cq, w_ck, w_cv, w_co, w_in, w_out, gain_self, gain_cross, gain_ffn, cotangent):

    def whole_layer(stream, enc_all, *params):

        def one_question(items):
            return question(items[0], items[1], items[2], params)
        return lax.map(jax.checkpoint(one_question), (stream, enc_all, lengths))
    inputs = (hidden, encoder, w_sq, w_sk, w_sv, w_so, w_cq, w_ck, w_cv, w_co, w_in, w_out, gain_self, gain_cross, gain_ffn)
    primals = tuple((item.astype(jnp.float32) for item in inputs))
    result, pullback = jax.vjp(whole_layer, *primals)
    grads = pullback(cotangent.astype(jnp.float32))
    return (result.astype(jnp.bfloat16), grads[0].astype(jnp.bfloat16), grads[1].astype(jnp.bfloat16), grads[2], grads[3], grads[4], grads[5], grads[6], grads[7], grads[8], grads[9], grads[10], grads[11], grads[12], grads[13], grads[14])
```

```python
import functools

import jax
import jax.numpy as jnp
from jax import lax
from jax.experimental import pallas as pl
from jax.experimental.pallas import tpu as pltpu
from jax.sharding import PartitionSpec as P

HEADS = 12
EPS = 1e-06
NEG = -1000000000.0
F32 = jnp.float32
BF = jnp.bfloat16
ROWS = 16
MIB = 1 << 20


def dot(left, right, left_dim, right_dim, precision=None):
    return lax.dot_general(
        left,
        right,
        (((left_dim,), (right_dim,)), ((), ())),
        precision=precision,
        preferred_element_type=F32,
    )


def nn(left, right):
    return dot(left, right, 1, 0)


def nt(left, right):
    return dot(left, right, 1, 1)


def tn(left, right):
    return dot(left, right, 0, 0)


def low(values):
    return values.astype(BF)


def inverse_rms(values):
    return lax.rsqrt(jnp.mean(values * values, axis=-1, keepdims=True) + EPS)


def norm_back(grad, values, gain):
    inv = inverse_rms(values)
    scaled = gain * grad
    inner = jnp.mean(values * scaled, axis=-1, keepdims=True)
    grad_values = inv * scaled - values * (inv * inv * inv * inner)
    grad_gain = jnp.sum(grad * values * inv, axis=0, keepdims=True)
    return grad_values, grad_gain


def head_matrix(width):
    row = lax.broadcasted_iota(jnp.int32, (ROWS, width), 0)
    lane = lax.broadcasted_iota(jnp.int32, (ROWS, width), 1)
    return jnp.where(lane // (width // HEADS) == row, 1.0, 0.0).astype(F32)


def spread(per_head, heads):
    return dot(per_head, heads, 0, 0, lax.Precision.HIGHEST)


def gather_heads(values, heads):
    return dot(heads, values, 1, 1, lax.Precision.HIGHEST)


def split_three(values):
    first = low(values)
    rest = values - first.astype(F32)
    second = low(rest)
    third = low(rest - second.astype(F32))
    return first, second, third


def joined(parts):
    return (parts[0].astype(F32) + parts[1].astype(F32)) + parts[2].astype(F32)


def two_heads(block):
    lane = lax.broadcasted_iota(jnp.int32, block.shape, 1)
    first = lane < block.shape[1] // 2
    zero = jnp.zeros_like(block)
    return jnp.concatenate([jnp.where(first, block, zero), jnp.where(first, zero, block)], 0)


def fold_heads(block):
    half = block.shape[0] // 2
    lane = lax.broadcasted_iota(jnp.int32, (half, block.shape[1]), 1)
    return jnp.where(lane < block.shape[1] // 2, block[:half], block[half:])


def pair_rows(per_head, pair):
    return jnp.concatenate([per_head[2 * pair : 2 * pair + 1], per_head[2 * pair + 1 : 2 * pair + 2]], 1)


def attend_pair(queries, keys, values, valid):
    scores = jnp.where(valid, nt(keys, two_heads(queries)), NEG)
    top = jnp.max(scores, axis=0, keepdims=True)
    weights = jnp.exp(scores - top)
    total = jnp.sum(weights, axis=0, keepdims=True)
    probs = low(weights * (1.0 / total))
    return fold_heads(tn(probs, values)), top + jnp.log(total)


def attend_pair_back(queries, keys, values, grad_mix, valid, log_row, dot_row):
    scaled = two_heads(queries)
    grad_two = two_heads(grad_mix)
    scores = jnp.where(valid, nt(keys, scaled), NEG)
    probs = jnp.exp(scores - log_row)
    grad_probs = nt(values, grad_two)
    grad_scores = low(probs * (grad_probs - dot_row))
    grad_values = nn(low(probs), grad_two)
    grad_keys = nn(grad_scores, scaled)
    grad_queries = fold_heads(tn(grad_scores, keys))
    return grad_queries, grad_keys, grad_values


def causal_mask(tokens):
    key = lax.broadcasted_iota(jnp.int32, (tokens, 2 * tokens), 0)
    token = lax.broadcasted_iota(jnp.int32, (tokens, 2 * tokens), 1)
    return key <= jnp.where(token >= tokens, token - tokens, token)


def params(mib, **more):
    return pltpu.CompilerParams(vmem_limit_bytes=mib * MIB, **more)


def self_forward_kernel(
    hidden, gain_self, gain_cross, w_sq, w_sk, w_sv, w_so, w_cq,
    x_self_out, q_out, k_out, v_out, mixture_out, log_out, mix_out, after_out, x_cross_out, cross_q_out,
):
    stream = hidden[...].astype(F32)
    tokens, width = stream.shape
    factor = (width // HEADS) ** -0.5
    x_self = low(stream * inverse_rms(stream) * gain_self[...])
    x_self_out[...] = x_self
    queries = low(nn(x_self, w_sq[...]))
    keys = low(nn(x_self, w_sk[...]))
    values = low(nn(x_self, w_sv[...]))
    q_out[...] = queries
    k_out[...] = keys
    v_out[...] = values
    valid = causal_mask(tokens)
    pair_width = 2 * width // HEADS
    log_out[...] = jnp.zeros_like(log_out)
    mixtures = []
    for pair in range(HEADS // 2):
        part = slice(pair * pair_width, (pair + 1) * pair_width)
        mixture, log_total = attend_pair(queries[:, part] * factor, keys[:, part], values[:, part], valid)
        mixtures.append(mixture)
        log_out[2 * pair : 2 * pair + 1] = log_total[:, :tokens]
        log_out[2 * pair + 1 : 2 * pair + 2] = log_total[:, tokens:]
    mixture = jnp.concatenate(mixtures, 1)
    mixture_out[...] = mixture
    mix = low(mixture)
    mix_out[...] = mix
    after_self = stream + nn(mix, w_so[...])
    after_out[...] = after_self
    x_cross = low(after_self * inverse_rms(after_self) * gain_cross[...])
    x_cross_out[...] = x_cross
    cross_q_out[...] = low(nn(x_cross, w_cq[...]))


def self_forward(hidden, gain_self, gain_cross, w_sq, w_sk, w_sv, w_so, w_cq):
    tokens, width = hidden.shape
    bf = jax.ShapeDtypeStruct((tokens, width), BF)
    f32 = jax.ShapeDtypeStruct((tokens, width), F32)
    logs = jax.ShapeDtypeStruct((ROWS, tokens), F32)
    return pl.pallas_call(
        self_forward_kernel,
        out_shape=(bf, bf, bf, bf, f32, logs, bf, f32, bf, bf),
        compiler_params=params(40),
        cost_estimate=pl.CostEstimate(flops=10 * tokens * width * width, bytes_accessed=12 * width * width, transcendentals=0),
        name="self_forward",
    )(hidden, gain_self, gain_cross, w_sq, w_sk, w_sv, w_so, w_cq)


def cross_forward_kernel(place, lengths, queries, keys, values, *outs):
    step = pl.program_id(0)
    count = len(outs)
    question = lax.rem(place[0] + step, count)
    tokens, width = queries.shape[1:]
    key_count = keys.shape[0]
    factor = (width // HEADS) ** -0.5
    valid = lax.broadcasted_iota(jnp.int32, (key_count, 2 * tokens), 0) < lengths[question]
    pair_width = 2 * width // HEADS
    mixtures, logs = [], []
    for pair in range(HEADS // 2):
        part = slice(pair * pair_width, (pair + 1) * pair_width)
        mixture, log_total = attend_pair(
            queries[0, :, part] * factor, keys[:, part], values[:, part], valid
        )
        mixtures.append(low(mixture))
        logs += [log_total[:, :tokens], log_total[:, tokens:]]
    logs.append(jnp.zeros((ROWS - HEADS, tokens), F32))
    parts = list(split_three(jnp.concatenate(logs, 0)))
    extra = parts + [jnp.zeros((ROWS, width - 3 * tokens), BF)]
    packed = jnp.concatenate([jnp.concatenate(mixtures, 1), jnp.concatenate(extra, 1)], 0)
    for index, out in enumerate(outs):

        @pl.when(step == index)
        def _():
            out[...] = packed


def cross_forward(place, lengths, queries, keys, values):
    count, tokens, width = queries.shape
    key_count = keys.shape[0] // count
    whose = lambda step, place, lengths: lax.rem(place[0] + step, count)
    grid = pltpu.PrefetchScalarGridSpec(
        num_scalar_prefetch=2,
        grid=(count,),
        in_specs=[
            pl.BlockSpec((1, tokens, width), lambda s, p, n: (whose(s, p, n), 0, 0)),
            pl.BlockSpec((key_count, width), lambda s, p, n: (whose(s, p, n), 0)),
            pl.BlockSpec((key_count, width), lambda s, p, n: (whose(s, p, n), 0)),
        ],
        out_specs=[pl.BlockSpec((tokens + ROWS, width), lambda s, p, n: (0, 0))] * count,
    )
    return pl.pallas_call(
        cross_forward_kernel,
        grid_spec=grid,
        out_shape=[jax.ShapeDtypeStruct((tokens + ROWS, width), BF)] * count,
        compiler_params=params(48),
        cost_estimate=pl.CostEstimate(
            flops=16 * count * tokens * key_count * width, bytes_accessed=4 * count * key_count * width, transcendentals=0
        ),
        name="cross_forward",
    )(place, lengths, queries, keys, values)


def feed_forward_kernel(
    after_self, cotangent, gain_ffn, w_co, w_in, w_out, *refs, count, chunks
):
    packed = refs[:count]
    (mix_out, x_ffn_out, act_out, grad_pre_out, result_out, grad_after_out,
     g_cross_out, send_out, grad_gain_out) = refs[count:]
    tokens, width = after_self.shape
    hidden_units = w_in.shape[1]
    heads = head_matrix(width)
    logs = [
        joined([part[tokens:, i * tokens : (i + 1) * tokens] for i in range(3)]) for part in packed
    ]
    top = functools.reduce(jnp.maximum, logs)
    log_total = top + jnp.log(sum(jnp.exp(item - top) for item in logs))
    mixture = sum(
        spread(jnp.exp(item - log_total), heads) * part[:tokens].astype(F32)
        for item, part in zip(logs, packed)
    )
    mix = low(mixture)
    mix_out[...] = mix
    after_cross = after_self[...] + nn(mix, w_co[...])
    x_ffn = low(after_cross * inverse_rms(after_cross) * gain_ffn[...])
    x_ffn_out[...] = x_ffn
    grad_low = cotangent[...]
    span = hidden_units // chunks
    result = after_cross
    grad_x = jnp.zeros((tokens, width), F32)
    slope = (2.0 / 3.141592653589793) ** 0.5
    for chunk in range(chunks):
        part = slice(chunk * span, (chunk + 1) * span)
        pre = nn(x_ffn, w_in[:, part])
        bent = jnp.tanh(slope * (pre + 0.044715 * (pre * pre * pre)))
        act = low(0.5 * pre * (1.0 + bent))
        act_out[:, part] = act
        result = result + nn(act, w_out[part, :])
        grad_act = nt(grad_low, w_out[part, :])
        bend = 0.5 * (1.0 + bent) + (0.5 * slope) * pre * (1.0 - bent * bent) * (1.0 + (3 * 0.044715) * (pre * pre))
        grad_pre = low(grad_act * bend)
        grad_pre_out[:, part] = grad_pre
        grad_x = grad_x + nt(grad_pre, w_in[:, part])
    result_out[...] = low(result)
    grad_values, grad_gain = norm_back(grad_x, after_cross, gain_ffn[...])
    grad_gain_out[...] = grad_gain
    grad_after = grad_low.astype(F32) + grad_values
    grad_after_out[...] = grad_after
    g_cross = low(grad_after)
    g_cross_out[...] = g_cross
    grad_mix = low(nt(g_cross, w_co[...]))
    delta = gather_heads(grad_mix.astype(F32) * mixture, heads)
    extra = list(split_three(log_total)) + list(split_three(delta))
    rest = width - 6 * tokens
    if rest:
        extra.append(jnp.zeros((ROWS, rest), BF))
    send_out[:tokens] = grad_mix
    send_out[tokens:] = jnp.concatenate(extra, 1)


def feed_forward(after_self, cotangent, gain_ffn, w_co, w_in, w_out, packed):
    tokens, width = after_self.shape
    hidden_units = w_in.shape[1]
    bf = jax.ShapeDtypeStruct((tokens, width), BF)
    f32 = jax.ShapeDtypeStruct((tokens, width), F32)
    wide = jax.ShapeDtypeStruct((tokens, hidden_units), BF)
    return pl.pallas_call(
        functools.partial(feed_forward_kernel, count=len(packed), chunks=4),
        out_shape=(
            bf, bf, wide, wide, bf, f32, bf,
            jax.ShapeDtypeStruct((tokens + ROWS, width), BF),
            jax.ShapeDtypeStruct((1, width), F32),
        ),
        compiler_params=params(48),
        cost_estimate=pl.CostEstimate(
            flops=8 * tokens * width * hidden_units, bytes_accessed=5 * width * hidden_units, transcendentals=0
        ),
        name="feed_forward",
    )(after_self, cotangent, gain_ffn, w_co, w_in, w_out, *packed)


def cross_backward_kernel(place, lengths, queries, grads, keys, values, grad_keys, grad_values, *outs):
    step = pl.program_id(0)
    count = len(outs)
    question = lax.rem(place[0] + step, count)
    tokens, width = queries.shape[1:]
    key_count = keys.shape[0]
    factor = (width // HEADS) ** -0.5
    valid = lax.broadcasted_iota(jnp.int32, (key_count, 2 * tokens), 0) < lengths[question]
    pair_width = 2 * width // HEADS
    pieces = [grads[0, tokens:, i * tokens : (i + 1) * tokens] for i in range(6)]
    log_total, delta = joined(pieces[:3]), joined(pieces[3:])
    found = []
    for pair in range(HEADS // 2):
        part = slice(pair * pair_width, (pair + 1) * pair_width)
        grad_q, grad_k, grad_v = attend_pair_back(
            queries[0, :, part] * factor, keys[:, part], values[:, part], grads[0, :tokens, part],
            valid, pair_rows(log_total, pair), pair_rows(delta, pair),
        )
        found.append(low(grad_q * factor))
        grad_keys[:, part] = low(grad_k)
        grad_values[:, part] = low(grad_v)
    grad_queries = jnp.concatenate(found, 1)
    for index, out in enumerate(outs):

        @pl.when(step == index)
        def _():
            out[...] = grad_queries


def cross_backward(place, lengths, queries, grads, keys, values):
    count, tokens, width = queries.shape
    key_count = keys.shape[0] // count
    whose = lambda step, place: lax.rem(place[0] + step, count)
    key_spec = pl.BlockSpec((key_count, width), lambda s, p, n: (whose(s, p), 0))
    grid = pltpu.PrefetchScalarGridSpec(
        num_scalar_prefetch=2,
        grid=(count,),
        in_specs=[
            pl.BlockSpec((1, tokens, width), lambda s, p, n: (whose(s, p), 0, 0)),
            pl.BlockSpec((1, tokens + ROWS, width), lambda s, p, n: (whose(s, p), 0, 0)),
            key_spec,
            key_spec,
        ],
        out_specs=[key_spec, key_spec] + [pl.BlockSpec((tokens, width), lambda s, p, n: (0, 0))] * count,
    )
    return pl.pallas_call(
        cross_backward_kernel,
        grid_spec=grid,
        out_shape=[jax.ShapeDtypeStruct(keys.shape, BF)] * 2 + [jax.ShapeDtypeStruct((tokens, width), BF)] * count,
        compiler_params=params(48),
        cost_estimate=pl.CostEstimate(
            flops=40 * count * tokens * key_count * width, bytes_accessed=8 * count * key_count * width, transcendentals=0
        ),
        name="cross_backward",
    )(place, lengths, queries, grads, keys, values)


def self_backward_kernel(
    grad_after_cross, after_self, hidden, gain_self, gain_cross, self_q, self_k, self_v, mixture, logs,
    w_cq, w_so, w_sq, w_sk, w_sv, *refs, count
):
    partial = refs[:count]
    grad_cq_out, g_self_out, sq_out, sk_out, sv_out, hidden_out, gain_self_out, gain_cross_out = refs[count:]
    tokens, width = after_self.shape
    factor = (width // HEADS) ** -0.5
    heads = head_matrix(width)
    grad_cq = low(sum(item[...].astype(F32) for item in partial))
    grad_cq_out[...] = grad_cq
    grad_values, grad_gain = norm_back(nt(grad_cq, w_cq[...]), after_self[...], gain_cross[...])
    gain_cross_out[...] = grad_gain
    grad_after = grad_after_cross[...] + grad_values
    g_self = low(grad_after)
    g_self_out[...] = g_self
    grad_mix = low(nt(g_self, w_so[...]))
    delta = gather_heads(grad_mix.astype(F32) * mixture[...], heads)
    valid = causal_mask(tokens)
    pair_width = 2 * width // HEADS
    found = []
    for pair in range(HEADS // 2):
        part = slice(pair * pair_width, (pair + 1) * pair_width)
        grad_q, grad_k, grad_v = attend_pair_back(
            self_q[:, part] * factor, self_k[:, part], self_v[:, part], grad_mix[:, part],
            valid, pair_rows(logs[...], pair), pair_rows(delta, pair),
        )
        found.append((low(grad_q * factor), low(grad_k), low(grad_v)))
    grad_q, grad_k, grad_v = (jnp.concatenate([item[i] for item in found], 1) for i in range(3))
    sq_out[...] = grad_q
    sk_out[...] = grad_k
    sv_out[...] = grad_v
    grad_x = nt(grad_q, w_sq[...]) + nt(grad_k, w_sk[...]) + nt(grad_v, w_sv[...])
    grad_values, grad_gain = norm_back(grad_x, hidden[...].astype(F32), gain_self[...])
    gain_self_out[...] = grad_gain
    hidden_out[...] = low(grad_after + grad_values)


def self_backward(first, weights, partial):
    tokens, width = first[1].shape
    bf = jax.ShapeDtypeStruct((tokens, width), BF)
    row = jax.ShapeDtypeStruct((1, width), F32)
    return pl.pallas_call(
        functools.partial(self_backward_kernel, count=len(partial)),
        out_shape=(bf, bf, bf, bf, bf, bf, row, row),
        compiler_params=params(48),
        cost_estimate=pl.CostEstimate(flops=12 * tokens * width * width, bytes_accessed=12 * width * width, transcendentals=0),
        name="self_backward",
    )(*first, *weights, *partial)


def swap(values, axis, by):
    peers = lax.axis_size(axis)
    return lax.ppermute(values, axis, [(i, i ^ by) for i in range(peers)])


def shift(values, axis, by):
    peers = lax.axis_size(axis)
    return lax.ppermute(values, axis, [(i, (i + by) % peers) for i in range(peers)])


def pick(values, index):
    return lax.dynamic_index_in_dim(values, index, 0, keepdims=False)


def total(parts):
    return sum(item.astype(F32) for item in parts)


def body(
    hidden, encoder, lengths, w_sq, w_sk, w_sv, w_so, w_cq, w_ck, w_cv, w_co, w_in, w_out,
    gain_self, gain_cross, gain_ffn, cotangent,
):
    _, tokens, width = hidden.shape
    questions, _, passage_len, _ = encoder.shape
    units = w_in.shape[1]
    ring = lax.axis_size("pa")
    chips = lax.axis_size("pb") // 2
    place = lax.axis_index("pa")
    chip = lax.axis_index("pb") // 2
    core = lax.axis_index("pb") % 2
    rows = width // ring
    half = rows // 2
    gain_self, gain_cross, gain_ffn = (gain.reshape(1, width) for gain in (gain_self, gain_cross, gain_ffn))
    where_now = jnp.reshape(place, (1,)).astype(jnp.int32)
    true_len = lengths.reshape(questions)
    hidden2 = hidden.reshape(tokens, width)
    cot = cotangent.reshape(tokens, width)
    enc = encoder.reshape(questions * passage_len, width)

    def to_chips(make):
        found = [make(chip)]
        for by in range(1, chips):
            found.append(swap(make(chip ^ by), "pb", 2 * by))
        return found

    def to_ring(make):
        found = [make(place)]
        for by in range(1, ring):
            found.append(shift(make((place + by) % ring), "pa", by))
        return found

    x_self, self_q, self_k, self_v, mixture, logs, self_mix, after_self, x_cross, cross_q = self_forward(
        hidden2, gain_self, gain_cross, w_sq, w_sk, w_sv, w_so, w_cq
    )
    queries = lax.all_gather(cross_q, "pa")
    four = 4 * width // chips
    two = 2 * width // chips

    def early(index):
        first = jnp.where(index * 4 // chips == 3, self_mix, x_self)
        return jnp.concatenate([first, cot], 1)

    early_parts = to_chips(early)
    keys = low(nn(enc, w_ck))
    values = low(nn(enc, w_cv))
    partial = cross_forward(where_now, true_len, queries, keys, values)
    packed = [partial[0]] + [shift(partial[by], "pa", by) for by in range(1, ring)]
    (cross_mix, x_ffn, activated, grad_pre, result, grad_after_cross, g_cross, sent, grad_gain_ffn) = feed_forward(
        after_self, cot, gain_ffn, w_co, w_in, w_out, packed
    )
    grads = lax.all_gather(sent, "pa")
    act_chips = jnp.transpose(
        activated.reshape(tokens, ring, chips, units // (ring * chips)), (2, 0, 1, 3)
    ).reshape(chips, tokens, units // chips)

    def middle(index):
        first = jnp.where(index * 2 // chips == 0, cross_mix, x_cross)
        span = units // chips
        return jnp.concatenate(
            [x_ffn, first, pick(act_chips, index), lax.dynamic_slice_in_dim(grad_pre, index * span, span, 1)], 1
        )

    middle_parts = to_chips(middle)
    back = cross_backward(where_now, true_len, queries, grads, keys, values)
    grad_keys, grad_values, partial = back[0], back[1], back[2:]
    partial = [partial[0]] + [shift(partial[by], "pa", by) for by in range(1, ring)]
    grad_encoder = low(nt(grad_keys, w_ck) + nt(grad_values, w_cv)).reshape(encoder.shape)
    early_all = jnp.concatenate(early_parts, 0)
    middle_all = jnp.concatenate(middle_parts, 0)
    span = units // chips
    grad_in = low(tn(middle_all[:, :width], middle_all[:, 2 * width + span :]))
    grad_out = low(tn(middle_all[:, 2 * width : 2 * width + span], early_all[:, width:]))
    ffn_rows = grad_in.reshape(ring, 2, half, span)
    out_rows = grad_out.reshape(ring, 2, half * span // width, width)
    kv = jnp.concatenate([low(tn(enc, grad_keys)), low(tn(enc, grad_values))], 1).reshape(ring, 2, half, 2 * width)

    def core_sum(values, axis):
        keep = lax.dynamic_index_in_dim(values, core, axis, keepdims=False)
        give = lax.dynamic_index_in_dim(values, 1 - core, axis, keepdims=False)
        return low(total([keep, swap(give, "pb", 1)]))

    ffn_sum = core_sum(ffn_rows, 1)
    out_sum = core_sum(out_rows, 1)
    kv_core = core_sum(kv, 1)
    kv_sum = low(total(to_chips(lambda index: lax.dynamic_slice_in_dim(kv_core, index * two, two, 2))))

    flat = lambda item: item.reshape(ring, -1)
    first_all = jnp.concatenate([flat(ffn_sum), flat(out_sum), flat(kv_sum)], 1)
    first_sum = low(total(to_ring(lambda index: pick(first_all, index))))

    grad_cq, g_self, grad_sq, grad_sk, grad_sv, grad_hidden, grad_gain_self, grad_gain_cross = self_backward(
        (grad_after_cross, after_self, hidden2, gain_self, gain_cross, self_q, self_k, self_v, mixture, logs),
        (w_cq, w_so, w_sq, w_sk, w_sv),
        partial,
    )
    gains = jnp.concatenate([grad_gain_self, grad_gain_cross, grad_gain_ffn], 0)

    def gain_rows(values):
        big = lax.reduce_precision(values, 8, 7)
        return jnp.concatenate([low(big), low(values - big)], 0)

    def gain_total(parts):
        both = total(parts)
        return both[:3] + both[3:]

    tail_stack = jnp.stack([grad_sq, grad_sk, grad_sv, g_self], 0)
    tail_stack = tail_stack.reshape(4, tokens, chips // 4, four)
    tail_stack = jnp.transpose(tail_stack, (0, 2, 1, 3)).reshape(chips, tokens, four)
    co_stack = jnp.stack([g_cross, grad_cq], 0).reshape(2, tokens, chips // 2, two)
    co_stack = jnp.transpose(co_stack, (0, 2, 1, 3)).reshape(chips, tokens, two)
    gain_pad = jnp.pad(gain_rows(gains), ((0, ROWS - 6), (0, four + two - width if four + two > width else 0)))

    def late(index):
        top = jnp.concatenate([pick(tail_stack, index), pick(co_stack, index)], 1)
        return jnp.concatenate([top, gain_pad[:, : four + two]], 0)

    late_parts = to_chips(late) if four + two >= width else to_chips(
        lambda index: jnp.concatenate([pick(tail_stack, index), pick(co_stack, index)], 1)
    )
    late_all = jnp.concatenate([item[:tokens] for item in late_parts], 0)
    if four + two >= width:
        gain_sum = gain_total([item[tokens : tokens + 6, :width] for item in late_parts])
    else:
        gain_sum = gains + sum(swap(gains, "pb", 2 * by) for by in range(1, chips))
    gain_sum = gain_total([gain_rows(gain_sum), swap(gain_rows(gain_sum), "pb", 1)])
    grad_tail = low(tn(early_all[:, :width], late_all[:, :four]))
    grad_co = low(tn(middle_all[:, width : 2 * width], late_all[:, four:]))
    tail_sum = core_sum(jnp.concatenate([grad_tail, grad_co], 1).reshape(ring, 2, half, four + two), 1)
    gain_flat = gain_rows(gain_sum).reshape(6 * width)

    def last(index):
        return jnp.concatenate([pick(tail_sum, index).reshape(-1), gain_flat])

    last_parts = to_ring(last)
    split_at = half * (four + two)
    last_sum = low(total([item[:split_at] for item in last_parts]))
    gain_sum = gain_total([item[split_at:].reshape(6, width) for item in last_parts])
    gain_mine = lax.dynamic_slice_in_dim(gain_sum, place * rows, rows, 1)

    def everyone(values):
        found = jnp.zeros((chips,) + values.shape, BF)
        for by in range(chips):
            piece = values if by == 0 else swap(values, "pb", 2 * by)
            found = lax.dynamic_update_index_in_dim(found, piece, chip ^ by, 0)
        other = swap(found, "pb", 1)
        return jnp.where(core == 0, jnp.stack([found, other], 1), jnp.stack([other, found], 1))

    first_all = everyone(first_sum)
    cut_in = half * span
    cut_out = cut_in + half * span
    piece_in = first_all[:, :, :cut_in].reshape(chips, 2, half, span)
    piece_out = first_all[:, :, cut_in:cut_out].reshape(chips, 2, half * span // width, width)
    piece_kv = first_all[:, :, cut_out:].reshape(chips, 2, half, two)
    last_all = everyone(last_sum).reshape(chips, 2, half, four + two)

    def columns(pieces):
        return jnp.transpose(pieces, (1, 2, 0, 3)).reshape(rows, -1).astype(F32)

    quarter = chips // 4
    self_pieces = [columns(last_all[i * quarter : (i + 1) * quarter, :, :, :four]) for i in range(4)]
    mid = chips // 2
    grad_w_co = columns(last_all[:mid, :, :, four:])
    grad_w_cq = columns(last_all[mid:, :, :, four:])
    grad_w_ck = columns(piece_kv[:mid])
    grad_w_cv = columns(piece_kv[mid:])
    grad_w_in = columns(piece_in)
    grad_w_out = piece_out.reshape(units // ring, width).astype(F32)
    return (
        result.reshape(hidden.shape),
        grad_hidden.reshape(hidden.shape),
        grad_encoder,
        self_pieces[0],
        self_pieces[1],
        self_pieces[2],
        self_pieces[3],
        grad_w_cq,
        grad_w_ck,
        grad_w_cv,
        grad_w_co,
        grad_w_in,
        grad_w_out,
        gain_mine[0],
        gain_mine[1],
        gain_mine[2],
    )


def solution(mesh):
    split = P(("pb", "pa"), None, None)
    passages = P("pb", "pa", None, None)
    return jax.shard_map(
        body,
        mesh=mesh,
        in_specs=(split, passages, P("pb", "pa")) + (P(),) * 13 + (split,),
        out_specs=(split, split, passages) + (P("pa", None),) * 10 + (P("pa"),) * 3,
        check_vma=False,
    )
```

```python
import functools

import jax
import jax.numpy as jnp
from jax import lax
from jax.experimental import pallas as pl
from jax.experimental.pallas import tpu as pltpu
from jax.sharding import PartitionSpec as P

HEADS = 12
EPS = 1e-06
NEG = -1000000000.0
F32 = jnp.float32
BF = jnp.bfloat16
SLOTS = 8
LANES = 128
EXTRA_ROWS = 16
MIB = 1 << 20


def dot(left, right, left_dim, right_dim, precision=None):
    return lax.dot_general(
        left,
        right,
        (((left_dim,), (right_dim,)), ((), ())),
        precision=precision,
        preferred_element_type=F32,
    )


def nn(left, right):
    return dot(left, right, 1, 0)


def nt(left, right):
    return dot(left, right, 1, 1)


def tn(left, right):
    return dot(left, right, 0, 0)


def low(values):
    return values.astype(BF)


def inverse_rms(values):
    return lax.rsqrt(jnp.mean(values * values, axis=-1, keepdims=True) + EPS)


def norm_back(grad, values, gain):
    inv = inverse_rms(values)
    scaled = gain * grad
    inner = jnp.mean(values * scaled, axis=-1, keepdims=True)
    grad_values = inv * scaled - values * (inv * inv * inv * inner)
    grad_gain = jnp.sum(grad * values * inv, axis=0, keepdims=True)
    return grad_values, grad_gain


def lanes_of(shape):
    return lax.broadcasted_iota(jnp.int32, shape, len(shape) - 1)


def rows_of(shape):
    return lax.broadcasted_iota(jnp.int32, shape, len(shape) - 2)


def ones_where(condition):
    return jnp.where(condition, 1.0, 0.0).astype(BF)


def spread_matrix(width):
    slot, lane = rows_of((LANES, width)), lanes_of((LANES, width))
    return ones_where((slot // SLOTS == lane // (width // HEADS)) & (slot % SLOTS < 3))


def compact_matrix():
    slot, lane = rows_of((LANES, LANES)), lanes_of((LANES, LANES))
    return ones_where((slot // SLOTS == lane // SLOTS) & (slot % SLOTS < 3))


def gather_matrix(width):
    feature, lane = rows_of((width, LANES)), lanes_of((width, LANES))
    return ones_where(feature // (width // HEADS) == lane // SLOTS)


def split_three(values):
    first = low(values).astype(F32)
    rest = values - first
    second = low(rest).astype(F32)
    third = low(rest - second).astype(F32)
    return first, second, third


def in_slots(values, start=0):
    first, second, third = split_three(values)
    slot = lanes_of(values.shape) % SLOTS - start
    return jnp.where(slot == 0, first, jnp.where(slot == 1, second, jnp.where(slot == 2, third, 0.0)))


def head_sums(values, matrix):
    first, second, third = split_three(values)
    return nn(low(first), matrix) + nn(low(second), matrix) + nn(low(third), matrix)


def two_heads(block):
    first = lanes_of(block.shape) < block.shape[1] // 2
    zero = jnp.zeros_like(block)
    return jnp.concatenate([jnp.where(first, block, zero), jnp.where(first, zero, block)], 0)


def fold_heads(block):
    half = block.shape[0] // 2
    lane = lanes_of((half, block.shape[1]))
    return jnp.where(lane < block.shape[1] // 2, block[:half], block[half:])


def pair_of_slots(extra, pair, start, more=None):
    lane = lanes_of(extra.shape)
    slot = lane % SLOTS
    wanted = (slot >= start) & (slot < start + 3)
    halves = [
        jnp.where(wanted & (lane // SLOTS == 2 * pair + i), extra, jnp.zeros_like(extra)) for i in range(2)
    ]
    block = jnp.concatenate(halves, 0)
    return block if more is None else block + more


def last_lane(rows, value):
    return jnp.where(lanes_of((rows, LANES)) == LANES - 1, value, 0.0).astype(BF)


def attend_pair(queries, keys, values, valid=None):
    scores = nt(keys, queries)
    if valid is not None:
        scores = jnp.where(valid, scores, NEG)
    top = jnp.max(scores, axis=0, keepdims=True)
    weights = low(jnp.exp(scores - top))
    both = tn(weights, values)
    split = both.shape[1] - LANES
    mixture = fold_heads(both[:, :split]) * (1.0 / fold_heads(both[:, split:]))
    return mixture, both[:, split:], top


def log_totals(sums, tops):
    tokens = tops[0].shape[1] // 2
    lane = lanes_of((tokens, LANES)) // SLOTS
    found = jnp.ones((tokens, LANES), F32)
    rows = []
    for pair, (both, top) in enumerate(zip(sums, tops)):
        found = jnp.where(lane == 2 * pair, both[:tokens], jnp.where(lane == 2 * pair + 1, both[tokens:], found))
        rows += [jnp.broadcast_to(top[:, :tokens], (SLOTS, tokens)), jnp.broadcast_to(top[:, tokens:], (SLOTS, tokens))]
    rows.append(jnp.zeros((LANES - HEADS * SLOTS, tokens), F32))
    return jnp.transpose(jnp.concatenate(rows, 0)) + jnp.log(found)


def attend_pair_back(queries, keys, values, grad_mix, query_more, key_more, grad_more, value_more, valid=None):
    scaled = two_heads(queries)
    grad_two = two_heads(grad_mix)
    scores = nt(jnp.concatenate([keys, key_more], 1), jnp.concatenate([scaled, query_more], 1))
    probs = jnp.exp(scores)
    if valid is not None:
        probs = jnp.where(valid, probs, 0.0)
    grad_probs = nt(jnp.concatenate([values, value_more], 1), jnp.concatenate([grad_two, grad_more], 1))
    grad_scores = low(probs * grad_probs)
    grad_values = nn(low(probs), grad_two)
    grad_keys = nn(grad_scores, scaled)
    grad_queries = fold_heads(tn(grad_scores, keys))
    return grad_queries, grad_keys, grad_values


def minus_slots(rows, start):
    slot = lanes_of((rows, LANES)) % SLOTS
    return jnp.where((slot >= start) & (slot < start + 3), -1.0, 0.0)


def causal_mask(tokens):
    key = rows_of((tokens, 2 * tokens))
    token = lanes_of((tokens, 2 * tokens))
    return key <= jnp.where(token >= tokens, token - tokens, token)


def call(kernel, name, outs, args, mib, scratch=(), places=None):
    kinds = {"s": pltpu.SMEM, "h": pltpu.HBM, "v": pltpu.VMEM}
    specs = [pl.BlockSpec(memory_space=kinds[letter]) for letter in places]
    return pl.pallas_call(
        kernel,
        out_shape=outs,
        in_specs=specs,
        out_specs=jax.tree.map(lambda _: pl.BlockSpec(memory_space=pltpu.VMEM), outs),
        scratch_shapes=scratch,
        compiler_params=pltpu.CompilerParams(vmem_limit_bytes=mib * MIB),
        cost_estimate=pl.CostEstimate(flops=1000, bytes_accessed=1000, transcendentals=0),
        name=name,
    )(*args)


def shape(*dims):
    return jax.ShapeDtypeStruct(dims, BF)


def shape32(*dims):
    return jax.ShapeDtypeStruct(dims, F32)


def fetch(copies):
    for item in copies:
        item.start()
    return copies


def self_forward_kernel(ids, hidden, cot, gain_self, gain_cross, *refs, chips):
    weights, refs = refs[:5], refs[5:]
    (q_out, k_out, v_out, mixture_out, logs_out, mix_out, after_out, x_cross_out, cross_q_out) = refs[:9]
    early, held, sems = refs[9 : 9 + chips], refs[9 + chips], refs[10 + chips]
    copies = fetch([pltpu.make_async_copy(w, held.at[i], sems.at[i]) for i, w in enumerate(weights)])
    stream = hidden[...].astype(F32)
    tokens, width = stream.shape
    factor = (width // HEADS) ** -0.5
    x_self = low(stream * inverse_rms(stream) * gain_self[...])
    found = []
    for i, out in enumerate((q_out, k_out, v_out)):
        copies[i].wait()
        found.append(low(nn(x_self, held[i])))
        out[...] = found[i]
    queries, keys, values = found
    valid = causal_mask(tokens)
    pair_width = 2 * width // HEADS
    ones = jnp.ones((tokens, LANES), BF)
    mixtures, sums, tops = [], [], []
    for pair in range(HEADS // 2):
        part = slice(pair * pair_width, (pair + 1) * pair_width)
        mixture, both, top = attend_pair(
            two_heads(queries[:, part] * factor), keys[:, part], jnp.concatenate([values[:, part], ones], 1), valid
        )
        mixtures.append(mixture)
        sums.append(both)
        tops.append(top)
    logs_out[...] = log_totals(sums, tops)
    mixture = jnp.concatenate(mixtures, 1)
    mixture_out[...] = mixture
    mix = low(mixture)
    mix_out[...] = mix
    copies[3].wait()
    after_self = stream + nn(mix, held[3])
    after_out[...] = after_self
    x_cross = low(after_self * inverse_rms(after_self) * gain_cross[...])
    x_cross_out[...] = x_cross
    copies[4].wait()
    cross_q_out[...] = low(nn(x_cross, held[4]))
    chip = ids[1]
    for by, out in enumerate(early):
        out[:, width:] = cot[...]
        last = lax.div((chip ^ by) * 4, chips) == 3

        @pl.when(last)
        def _():
            out[:, :width] = mix

        @pl.when(jnp.logical_not(last))
        def _():
            out[:, :width] = x_self


def self_forward(ids, hidden, cot, gain_self, gain_cross, weights, chips):
    tokens, width = hidden.shape
    low_one = shape(tokens, width)
    return call(
        functools.partial(self_forward_kernel, chips=chips),
        "self_forward",
        (low_one, low_one, low_one, shape32(tokens, width), shape32(tokens, LANES), low_one,
         shape32(tokens, width), low_one, low_one) + (shape(tokens, 2 * width),) * chips,
        (ids, hidden, cot, gain_self, gain_cross) + tuple(weights),
        20,
        [pltpu.VMEM((5, width, width), BF), pltpu.SemaphoreType.DMA((5,))],
        "svvvv" + "h" * 5,
    )


def question_of(step, ids, count):
    return lax.rem(ids[0] + count - step, count)


def cross_forward_kernel(ids, lengths, keys, values, *refs):
    count = (len(refs) - 1) // 2
    asked, outs, queries = refs[:count], refs[count : 2 * count], refs[-1]
    step = pl.program_id(0)
    tokens, width = queries.shape
    for index, item in enumerate(asked):

        @pl.when(step == index)
        def _():
            queries[...] = item[...]

    key_count = keys.shape[0]
    factor = (width // HEADS) ** -0.5
    size = (key_count, LANES)
    hidden_key = jnp.where(rows_of(size) < lengths[question_of(step, ids, count)], 0.0, NEG)
    key_more = jnp.where(lanes_of(size) == LANES - 1, hidden_key, 0.0).astype(BF)
    query_more = last_lane(2 * tokens, 1.0)
    ones = jnp.ones(size, BF)
    pair_width = 2 * width // HEADS
    mixtures, sums, tops = [], [], []
    for pair in range(HEADS // 2):
        part = slice(pair * pair_width, (pair + 1) * pair_width)
        mixture, both, top = attend_pair(
            jnp.concatenate([two_heads(queries[:, part] * factor), query_more], 1),
            jnp.concatenate([keys[:, part], key_more], 1),
            jnp.concatenate([values[:, part], ones], 1),
        )
        mixtures.append(low(mixture))
        sums.append(both)
        tops.append(top)
    packed = jnp.concatenate(mixtures + [low(in_slots(log_totals(sums, tops)))], 1)
    for index, out in enumerate(outs):

        @pl.when(step == index)
        def _():
            out[...] = packed


def cross_forward(ids, lengths, asked, keys, values):
    count = len(asked)
    tokens, width = asked[0].shape
    key_spec = pl.BlockSpec((keys.shape[0] // count, width), lambda s, ids, n: (question_of(s, ids, count), 0))
    whole = lambda lanes: pl.BlockSpec((tokens, lanes), lambda s, ids, n: (0, 0))
    return pl.pallas_call(
        cross_forward_kernel,
        grid_spec=pltpu.PrefetchScalarGridSpec(
            num_scalar_prefetch=2,
            grid=(count,),
            in_specs=[key_spec, key_spec] + [whole(width)] * count,
            out_specs=[whole(width + LANES)] * count,
            scratch_shapes=[pltpu.VMEM((tokens, width), BF)],
        ),
        out_shape=[shape(tokens, width + LANES)] * count,
        compiler_params=pltpu.CompilerParams(vmem_limit_bytes=20 * MIB),
        cost_estimate=pl.CostEstimate(flops=1000, bytes_accessed=1000, transcendentals=0),
        name="cross_forward",
    )(ids, lengths, keys, values, *asked)


def feed_forward_kernel(
    ids, after_self, cotangent, x_cross, gain_ffn, w_co_far, w_in_far, w_out_far, *refs, count, chips, chunks
):
    packed, refs = refs[:count], refs[count:]
    result_out, grad_after_out, g_cross_out, send_out, grad_gain_out = refs[:5]
    middle = refs[5 : 5 + chips]
    w_co, w_in, w_out, acts, grad_pres, sems = refs[5 + chips :]
    tokens, width = after_self.shape
    units = w_in.shape[1]
    wide = units // chunks
    first = pltpu.make_async_copy(w_co_far, w_co, sems.at[0])
    first.start()
    copies = []
    for chunk in range(chunks):
        part = pl.ds(chunk * wide, wide)
        copies.append(
            fetch([
                pltpu.make_async_copy(w_in_far.at[:, part], w_in.at[:, part], sems.at[1 + 2 * chunk]),
                pltpu.make_async_copy(w_out_far.at[part], w_out.at[part], sems.at[2 + 2 * chunk]),
            ])
        )
    compact, spread = compact_matrix(), spread_matrix(width)
    logs = [nn(part[:, width:], compact) for part in packed]
    top = functools.reduce(jnp.maximum, logs)
    log_total = top + jnp.log(sum(jnp.exp(item - top) for item in logs))
    mixture = sum(
        nn(low(in_slots(jnp.exp(item - log_total))), spread) * part[:, :width].astype(F32)
        for item, part in zip(logs, packed)
    )
    mix = low(mixture)
    first.wait()
    after_cross = after_self[...] + nn(mix, w_co[...])
    x_ffn = low(after_cross * inverse_rms(after_cross) * gain_ffn[...])
    grad_low = cotangent[...]
    result = after_cross
    grad_x = jnp.zeros((tokens, width), F32)
    slope = (2.0 / 3.141592653589793) ** 0.5
    span = units // chips
    piece = units // (count * chips)
    for chunk in range(chunks):
        part = slice(chunk * wide, (chunk + 1) * wide)
        for item in copies[chunk]:
            item.wait()
        pre = nn(x_ffn, w_in[:, part])
        square = pre * pre
        bent = jnp.tanh(pre * (slope + (0.044715 * slope) * square))
        act = low(0.5 * pre * (1.0 + bent))
        result = result + nn(act, w_out[part, :])
        grad_act = nt(grad_low, w_out[part, :])
        bend = 0.5 * (1.0 + bent) + 0.5 * pre * (1.0 - bent * bent) * (slope + (3 * 0.044715 * slope) * square)
        grad_pre = low(grad_act * bend)
        grad_x = grad_x + nt(grad_pre, w_in[:, part])
        for at in range(0, wide, piece):
            which = (chunk * wide + at) // piece
            slot = which // chips * piece
            acts[which % chips, :, slot : slot + piece] = act[:, at : at + piece]
        for at in range(0, wide, span):
            grad_pres[(chunk * wide + at) // span] = grad_pre[:, at : at + span]
    result_out[...] = low(result)
    grad_values, grad_gain = norm_back(grad_x, after_cross, gain_ffn[...])
    grad_gain_out[...] = grad_gain
    grad_after = grad_low.astype(F32) + grad_values
    grad_after_out[...] = grad_after
    g_cross = low(grad_after)
    g_cross_out[...] = g_cross
    grad_mix = low(nt(g_cross, w_co[...]))
    delta = head_sums(grad_mix.astype(F32) * mixture, gather_matrix(width))
    send_out[:, :width] = grad_mix
    send_out[:, width:] = low(in_slots(log_total) + in_slots(delta, 3))
    chip = ids[1]
    for by, out in enumerate(middle):
        index = chip ^ by
        out[:, :width] = x_ffn
        out[:, 2 * width : 2 * width + span] = acts[index]
        out[:, 2 * width + span :] = grad_pres[index]
        early = lax.div(index * 2, chips) == 0

        @pl.when(early)
        def _():
            out[:, width : 2 * width] = mix

        @pl.when(jnp.logical_not(early))
        def _():
            out[:, width : 2 * width] = x_cross[...]


def feed_forward(ids, after_self, cotangent, x_cross, gain_ffn, w_co, w_in, w_out, packed, chips):
    tokens, width = after_self.shape
    units = w_in.shape[1]
    span, chunks = units // chips, 4
    return call(
        functools.partial(feed_forward_kernel, count=len(packed), chips=chips, chunks=chunks),
        "feed_forward",
        (shape(tokens, width), shape32(tokens, width), shape(tokens, width), shape(tokens, width + LANES),
         shape32(1, width)) + (shape(tokens, 2 * width + 2 * span),) * chips,
        (ids, after_self, cotangent, x_cross, gain_ffn, w_co, w_in, w_out) + tuple(packed),
        32,
        [
            pltpu.VMEM(w_co.shape, BF),
            pltpu.VMEM(w_in.shape, BF),
            pltpu.VMEM(w_out.shape, BF),
            pltpu.VMEM((chips, tokens, span), BF),
            pltpu.VMEM((chips, tokens, span), BF),
            pltpu.SemaphoreType.DMA((1 + 2 * chunks,)),
        ],
        "svvvvhhh" + "v" * len(packed),
    )


def cross_backward_kernel(ids, lengths, keys, values, *refs):
    count = (len(refs) - 4) // 3
    asked, given = refs[:count], refs[count : 2 * count]
    grad_keys, grad_values = refs[2 * count : 2 * count + 2]
    outs = refs[2 * count + 2 : 3 * count + 2]
    queries, grads = refs[3 * count + 2 :]
    step = pl.program_id(0)
    tokens, width = queries.shape
    for index in range(count):

        @pl.when(step == index)
        def _():
            queries[...] = asked[index][...]
            grads[...] = given[index][...]

    key_count = keys.shape[0]
    factor = (width // HEADS) ** -0.5
    size = (key_count, LANES)
    hidden_key = jnp.where(rows_of(size) < lengths[question_of(step, ids, count)], 0.0, NEG)
    key_more = jnp.where(lanes_of(size) == LANES - 1, hidden_key, minus_slots(key_count, 0)).astype(BF)
    value_more = minus_slots(key_count, 3).astype(BF)
    extra = grads[:, width:]
    one = last_lane(2 * tokens, 1.0)
    pair_width = 2 * width // HEADS
    found = []
    for pair in range(HEADS // 2):
        part = slice(pair * pair_width, (pair + 1) * pair_width)
        grad_q, grad_k, grad_v = attend_pair_back(
            queries[:, part] * factor, keys[:, part], values[:, part], grads[:, part],
            pair_of_slots(extra, pair, 0, one), key_more, pair_of_slots(extra, pair, 3), value_more,
        )
        found.append(low(grad_q * factor))
        grad_keys[:, part] = low(grad_k)
        grad_values[:, part] = low(grad_v)
    grad_queries = jnp.concatenate(found, 1)
    for index, out in enumerate(outs):

        @pl.when(step == index)
        def _():
            out[...] = grad_queries


def cross_backward(ids, lengths, asked, given, keys, values):
    count = len(asked)
    tokens, width = asked[0].shape
    key_spec = pl.BlockSpec((keys.shape[0] // count, width), lambda s, ids, n: (question_of(s, ids, count), 0))
    whole = lambda lanes: pl.BlockSpec((tokens, lanes), lambda s, ids, n: (0, 0))
    return pl.pallas_call(
        cross_backward_kernel,
        grid_spec=pltpu.PrefetchScalarGridSpec(
            num_scalar_prefetch=2,
            grid=(count,),
            in_specs=[key_spec, key_spec] + [whole(width)] * count + [whole(width + LANES)] * count,
            out_specs=[key_spec, key_spec] + [whole(width)] * count,
            scratch_shapes=[pltpu.VMEM((tokens, width), BF), pltpu.VMEM((tokens, width + LANES), BF)],
        ),
        out_shape=[jax.ShapeDtypeStruct(keys.shape, BF)] * 2 + [shape(tokens, width)] * count,
        compiler_params=pltpu.CompilerParams(vmem_limit_bytes=24 * MIB),
        cost_estimate=pl.CostEstimate(flops=1000, bytes_accessed=1000, transcendentals=0),
        name="cross_backward",
    )(ids, lengths, keys, values, *asked, *given)


def gain_block(gains, four, width_out):
    count = gains.shape[1] // four
    high = low(gains).astype(F32)
    rows = [part[i : i + 1, v * four : (v + 1) * four] for part in (high, gains - high) for i in range(3) for v in range(count)]
    block = jnp.concatenate(rows + [jnp.zeros((EXTRA_ROWS - len(rows), four), F32)], 0)
    return low(jnp.concatenate([block, jnp.zeros((EXTRA_ROWS, width_out - four), F32)], 1))


def gain_values(block, four, width):
    count = width // four
    rows = []
    for i in range(3):
        pieces = [
            block[i * count + v : i * count + v + 1, :four] + block[(3 + i) * count + v : (3 + i) * count + v + 1, :four]
            for v in range(count)
        ]
        rows.append(jnp.concatenate(pieces, 1))
    return jnp.concatenate(rows, 0)


def self_backward_kernel(
    ids, grad_after_cross, after_self, hidden, gain_self, gain_cross, grad_gain_ffn, g_cross,
    self_q, self_k, self_v, mixture, logs, *refs, count, chips
):
    weights, partial, refs = refs[:5], refs[5 : 5 + count], refs[5 + count :]
    hidden_out, late = refs[0], refs[1 : 1 + chips]
    held, fours, twos, sems = refs[1 + chips :]
    copies = fetch([pltpu.make_async_copy(w, held.at[i], sems.at[i]) for i, w in enumerate(weights)])
    tokens, width = after_self.shape
    factor = (width // HEADS) ** -0.5
    four, two = 4 * width // chips, 2 * width // chips
    grad_cq = low(sum(item[...].astype(F32) for item in partial))
    copies[0].wait()
    grad_values, grad_gain_cross = norm_back(nt(grad_cq, held[0]), after_self[...], gain_cross[...])
    grad_after = grad_after_cross[...] + grad_values
    g_self = low(grad_after)
    copies[1].wait()
    grad_mix = low(nt(g_self, held[1]))
    delta = head_sums(grad_mix.astype(F32) * mixture[...], gather_matrix(width))
    extra = low(in_slots(logs[...]) + in_slots(delta, 3))
    valid = causal_mask(tokens)
    key_more = minus_slots(tokens, 0).astype(BF)
    value_more = minus_slots(tokens, 3).astype(BF)
    pair_width = 2 * width // HEADS
    found = []
    for pair in range(HEADS // 2):
        part = slice(pair * pair_width, (pair + 1) * pair_width)
        grad_q, grad_k, grad_v = attend_pair_back(
            self_q[:, part] * factor, self_k[:, part], self_v[:, part], grad_mix[:, part],
            pair_of_slots(extra, pair, 0), key_more, pair_of_slots(extra, pair, 3), value_more, valid,
        )
        found.append((low(grad_q * factor), low(grad_k), low(grad_v)))
    grads = [jnp.concatenate([item[i] for item in found], 1) for i in range(3)]
    grad_x = jnp.zeros((tokens, width), F32)
    for i in range(3):
        copies[2 + i].wait()
        grad_x = grad_x + nt(grads[i], held[2 + i])
    grad_values, grad_gain_self = norm_back(grad_x, hidden[...].astype(F32), gain_self[...])
    hidden_out[...] = low(grad_after + grad_values)
    gains = jnp.concatenate([grad_gain_self, grad_gain_cross, grad_gain_ffn[...]], 0)
    block = gain_block(gains, four, four + two)
    for i, item in enumerate(grads + [g_self]):
        for v in range(width // four):
            fours[i * (width // four) + v] = item[:, v * four : (v + 1) * four]
    for i, item in enumerate((g_cross[...], grad_cq)):
        for v in range(width // two):
            twos[i * (width // two) + v] = item[:, v * two : (v + 1) * two]
    chip = ids[1]
    for by, out in enumerate(late):
        out[:tokens, :four] = fours[chip ^ by]
        out[:tokens, four:] = twos[chip ^ by]
        out[tokens:] = block


def self_backward(ids, first, weights, partial, chips):
    tokens, width = first[1].shape
    four, two = 4 * width // chips, 2 * width // chips
    return call(
        functools.partial(self_backward_kernel, count=len(partial), chips=chips),
        "self_backward",
        (shape(tokens, width),) + (shape(tokens + EXTRA_ROWS, four + two),) * chips,
        (ids,) + tuple(first) + tuple(weights) + tuple(partial),
        24,
        [
            pltpu.VMEM((5, width, width), BF),
            pltpu.VMEM((chips, tokens, four), BF),
            pltpu.VMEM((chips, tokens, two), BF),
            pltpu.SemaphoreType.DMA((5,)),
        ],
        "s" + "v" * len(first) + "h" * 5 + "v" * len(partial),
    )


def stacked(refs, rows, lanes):
    return jnp.concatenate([item[rows, lanes] for item in refs], 0)


def hand_out(ids, held, keep, give):
    core = ids[2]
    keep[...] = held[core]
    give[...] = held[1 - core]


def ffn_grads_kernel(ids, *refs, chips):
    early, middle, (keep, give, held) = refs[:chips], refs[chips : 2 * chips], refs[2 * chips :]
    _, ring, half, both = held.shape
    span = both // 2
    width = early[0].shape[1] // 2
    every = slice(None)
    grad_in = low(
        tn(stacked(middle, every, slice(0, width)), stacked(middle, every, slice(2 * width + span, 2 * width + 2 * span)))
    )
    for z in range(ring):
        for c in range(2):
            at = (2 * z + c) * half
            held[c, z, :, :span] = grad_in[at : at + half]
    grad_out = low(
        tn(stacked(middle, every, slice(2 * width, 2 * width + span)), stacked(early, every, slice(width, 2 * width)))
    )
    few = span // (2 * ring)
    for z in range(ring):
        for c in range(2):
            at = (2 * z + c) * few
            block = grad_out[at : at + few]
            held[c, z, :, span:] = jnp.concatenate([block[:, v : v + span] for v in range(0, width, span)], 0)
    hand_out(ids, held, keep, give)


def ffn_grads(ids, early, middle, ring, units):
    chips = len(early)
    width = early[0].shape[1] // 2
    part = (ring, width // (2 * ring), 2 * units // chips)
    return call(
        functools.partial(ffn_grads_kernel, chips=chips), "ffn_grads", (shape(*part),) * 2,
        (ids,) + tuple(early) + tuple(middle), 36, [pltpu.VMEM((2,) + part, BF)], "s" + "v" * (2 * chips),
    )


def key_grads_kernel(ids, encoder, grad_keys, grad_values, keep, give, held):
    _, ring, half, both = held.shape
    width = both // 2
    for i, item in enumerate((grad_keys, grad_values)):
        grad = low(tn(encoder[...], item[...]))
        for z in range(ring):
            for c in range(2):
                at = (2 * z + c) * half
                held[c, z, :, i * width : (i + 1) * width] = grad[at : at + half]
    hand_out(ids, held, keep, give)


def key_grads(ids, encoder, grad_keys, grad_values, ring):
    width = encoder.shape[1]
    part = (ring, width // (2 * ring), 2 * width)
    return call(
        key_grads_kernel, "key_grads", (shape(*part),) * 2, (ids, encoder, grad_keys, grad_values), 36,
        [pltpu.VMEM((2,) + part, BF)], "svvv",
    )


def key_sum_kernel(ids, keep, came, *refs):
    outs, held = refs[:-1], refs[-1]
    chips, two = held.shape[0], held.shape[3]
    summed = low(keep[...].astype(F32) + came[...].astype(F32))
    for j in range(chips):
        held[j] = summed[:, :, j * two : (j + 1) * two]
    for by, out in enumerate(outs):
        out[...] = held[ids[1] ^ by]


def key_sum(ids, keep, came, chips):
    ring, half, both = keep.shape
    part = (ring, half, both // chips)
    return call(
        key_sum_kernel, "key_sum", (shape(*part),) * chips, (ids, keep, came), 20, [pltpu.VMEM((chips,) + part, BF)], "svv"
    )


def first_sum_kernel(ids, keep, came, *refs, chips):
    parts, outs = refs[:chips], refs[chips:]
    ring = len(outs)
    wide = keep.shape[2]
    for by, out in enumerate(outs):
        z = lax.rem(ids[0] + by, ring)
        out[:, :wide] = low(keep[z].astype(F32) + came[z].astype(F32))
        out[:, wide:] = low(sum(item[z].astype(F32) for item in parts))


def first_sum(ids, keep, came, parts):
    ring, half, wide = keep.shape
    out = shape(half, wide + parts[0].shape[2])
    return call(
        functools.partial(first_sum_kernel, chips=len(parts)), "first_sum", (out,) * ring,
        (ids, keep, came) + tuple(parts), 20, (), "svv" + "v" * len(parts),
    )


def tail_grads_kernel(ids, *refs, chips):
    early, middle, late = refs[:chips], refs[chips : 2 * chips], refs[2 * chips : 3 * chips]
    keep, give, held = refs[3 * chips :]
    _, ring, more, both = held.shape
    half = more - EXTRA_ROWS
    four = both // 3 * 2
    width = early[0].shape[1] // 2
    tokens = early[0].shape[0]
    every, rows = slice(None), slice(0, tokens)
    grads = (
        (low(tn(stacked(early, every, slice(0, width)), stacked(late, rows, slice(0, four)))), slice(0, four)),
        (low(tn(stacked(middle, every, slice(width, 2 * width)), stacked(late, rows, slice(four, both)))), slice(four, both)),
    )
    gains = sum(gain_values(item[tokens:].astype(F32), four, width) for item in late)
    block = gain_block(gains, four, both)
    for z in range(ring):
        for c in range(2):
            at = (2 * z + c) * half
            for grad, lanes in grads:
                held[c, z, :half, lanes] = grad[at : at + half]
            held[c, z, half:, :] = block
    hand_out(ids, held, keep, give)


def tail_grads(ids, early, middle, late, ring):
    chips = len(early)
    width = early[0].shape[1] // 2
    part = (ring, width // (2 * ring) + EXTRA_ROWS, late[0].shape[1])
    return call(
        functools.partial(tail_grads_kernel, chips=chips), "tail_grads", (shape(*part),) * 2,
        (ids,) + tuple(early) + tuple(middle) + tuple(late), 36, [pltpu.VMEM((2,) + part, BF)], "s" + "v" * (3 * chips),
    )


def tail_sum_kernel(ids, keep, came, *outs):
    ring = len(outs)
    half = keep.shape[1] - EXTRA_ROWS
    four = keep.shape[2] // 3 * 2
    width = half * 2 * ring
    gains = gain_values(keep[0, half:].astype(F32), four, width) + gain_values(came[0, half:].astype(F32), four, width)
    block = gain_block(gains, four, keep.shape[2])
    for by, out in enumerate(outs):
        z = lax.rem(ids[0] + by, ring)
        out[:half] = low(keep[z, :half].astype(F32) + came[z, :half].astype(F32))
        out[half:] = block


def tail_sum(ids, keep, came):
    ring, more, both = keep.shape
    return call(tail_sum_kernel, "tail_sum", (shape(more, both),) * ring, (ids, keep, came), 20, (), "svv")


def ring_sum_kernel(*refs):
    refs[-1][...] = low(sum(item[...].astype(F32) for item in refs[:-1]))


def ring_sum(parts):
    return call(ring_sum_kernel, "ring_sum", shape(*parts[0].shape), tuple(parts), 16, (), "v" * len(parts))


def last_sum_kernel(ids, *refs):
    parts, (out, gains_out, held) = refs[:-3], refs[-3:]
    half, both = out.shape
    ring, _, rows = held.shape
    four = both // 3 * 2
    out[...] = low(sum(item[:half].astype(F32) for item in parts))
    gains = sum(gain_values(item[half:].astype(F32), four, ring * rows) for item in parts)
    for z in range(ring):
        held[z] = gains[:, z * rows : (z + 1) * rows]
    gains_out[...] = held[ids[0]]


def last_sum(ids, parts, rows):
    more, both = parts[0].shape
    return call(
        last_sum_kernel, "last_sum", (shape(more - EXTRA_ROWS, both), shape32(3, rows)), (ids,) + tuple(parts), 16,
        [pltpu.VMEM((len(parts), 3, rows), F32)], "s" + "v" * len(parts),
    )


def place_pieces(ids, own, other, held):
    for by, (mine, theirs) in enumerate(zip(own, other)):
        held[ids[1] ^ by, ids[2]] = mine[...]
        held[ids[1] ^ by, 1 - ids[2]] = theirs[...]


def first_out_kernel(ids, *refs, chips, span):
    own, other, (in_out, out_out, ck_out, cv_out, held) = refs[:chips], refs[chips : 2 * chips], refs[2 * chips :]
    place_pieces(ids, own, other, held)
    half, wide = held.shape[2:]
    two = wide - 2 * span
    width = out_out.shape[1]
    few = half * span // width
    for j in range(chips):
        for c in range(2):
            rows = slice(c * half, (c + 1) * half)
            in_out[rows, j * span : (j + 1) * span] = held[j, c, :, :span].astype(F32)
            for v in range(width // span):
                at = (2 * j + c) * few
                out_out[at : at + few, v * span : (v + 1) * span] = held[
                    j, c, v * few : (v + 1) * few, span : 2 * span
                ].astype(F32)
            out = (ck_out, cv_out)[j * 2 // chips]
            at = j % (chips // 2) * two
            out[rows, at : at + two] = held[j, c, :, 2 * span :].astype(F32)


def first_out(ids, own, other, units, width):
    chips = len(own)
    half, wide = own[0].shape
    span = units // chips
    rows = 2 * half
    return call(
        functools.partial(first_out_kernel, chips=chips, span=span), "first_out",
        (shape32(rows, units), shape32(rows * units // width, width), shape32(rows, width), shape32(rows, width)),
        (ids,) + tuple(own) + tuple(other), 28, [pltpu.VMEM((chips, 2, half, wide), BF)], "s" + "v" * (2 * chips),
    )


def last_out_kernel(ids, *refs, chips):
    own, other, outs, held = refs[:chips], refs[chips : 2 * chips], refs[2 * chips : -1], refs[-1]
    place_pieces(ids, own, other, held)
    half, both = held.shape[2:]
    four, two = both // 3 * 2, both // 3
    for j in range(chips):
        for c in range(2):
            rows = slice(c * half, (c + 1) * half)
            at = j % (chips // 4) * four
            outs[j * 4 // chips][rows, at : at + four] = held[j, c, :, :four].astype(F32)
            at = j % (chips // 2) * two
            outs[4 + j * 2 // chips][rows, at : at + two] = held[j, c, :, four:].astype(F32)


def last_out(ids, own, other, width):
    chips = len(own)
    half, both = own[0].shape
    return call(
        functools.partial(last_out_kernel, chips=chips), "last_out", (shape32(2 * half, width),) * 6,
        (ids,) + tuple(own) + tuple(other), 28, [pltpu.VMEM((chips, 2, half, both), BF)], "s" + "v" * (2 * chips),
    )


def swap(values, axis, by):
    peers = lax.axis_size(axis)
    return lax.ppermute(values, axis, [(i, i ^ by) for i in range(peers)])


def shift(values, axis, by):
    peers = lax.axis_size(axis)
    return lax.ppermute(values, axis, [(i, (i + by) % peers) for i in range(peers)])


def over_chips(blocks):
    return [blocks[0]] + [swap(item, "pb", 2 * by) for by, item in enumerate(blocks) if by]


def over_ring(blocks, sign=1):
    return [blocks[0]] + [shift(item, "pa", sign * by) for by, item in enumerate(blocks) if by]


def over_core(blocks):
    return [swap(item, "pb", 1) for item in blocks]


def body(
    hidden, encoder, lengths, w_sq, w_sk, w_sv, w_so, w_cq, w_ck, w_cv, w_co, w_in, w_out,
    gain_self, gain_cross, gain_ffn, cotangent,
):
    _, tokens, width = hidden.shape
    questions, _, passage_len, _ = encoder.shape
    units = w_in.shape[1]
    ring = lax.axis_size("pa")
    chips = lax.axis_size("pb") // 2
    place, lane = lax.axis_index("pa"), lax.axis_index("pb")
    ids = jnp.stack([place, lane >> 1, lane & 1]).astype(jnp.int32)
    gain_self, gain_cross, gain_ffn = (gain.reshape(1, width) for gain in (gain_self, gain_cross, gain_ffn))
    true_len = lengths.reshape(questions)
    hidden2 = hidden.reshape(tokens, width)
    cot = cotangent.reshape(tokens, width)
    enc = encoder.reshape(questions * passage_len, width)

    found = self_forward(ids, hidden2, cot, gain_self, gain_cross, (w_sq, w_sk, w_sv, w_so, w_cq), chips)
    self_q, self_k, self_v, mixture, logs, _, after_self, x_cross, cross_q = found[:9]
    asked = over_ring([cross_q] * ring)
    early = over_chips(found[9:])
    keys = low(nn(enc, w_ck))
    values = low(nn(enc, w_cv))
    packed = over_ring(cross_forward(ids, true_len, asked, keys, values), -1)
    found = feed_forward(ids, after_self, cot, x_cross, gain_ffn, w_co, w_in, w_out, packed, chips)
    result, grad_after_cross, g_cross, sent, grad_gain_ffn = found[:5]
    given = over_ring([sent] * ring)
    middle = over_chips(found[5:])
    found = cross_backward(ids, true_len, asked, given, keys, values)
    grad_keys, grad_values = found[:2]
    partial = over_ring(found[2:], -1)
    keep, give = key_grads(ids, enc, grad_keys, grad_values, ring)
    key_parts = over_chips(key_sum(ids, keep, swap(give, "pb", 1), chips))
    keep, give = ffn_grads(ids, early, middle, ring, units)
    first = ring_sum(over_ring(first_sum(ids, keep, swap(give, "pb", 1), key_parts)))
    first = over_chips([first] * chips)
    grad_in, grad_out, grad_ck, grad_cv = first_out(ids, first, over_core(first), units, width)
    grad_encoder = low(nt(grad_keys, w_ck) + nt(grad_values, w_cv)).reshape(encoder.shape)
    found = self_backward(
        ids,
        (grad_after_cross, after_self, hidden2, gain_self, gain_cross, grad_gain_ffn, g_cross,
         self_q, self_k, self_v, mixture, logs),
        (w_cq, w_so, w_sq, w_sk, w_sv),
        partial,
        chips,
    )
    grad_hidden = found[0]
    late = over_chips(found[1:])
    keep, give = tail_grads(ids, early, middle, late, ring)
    last, gains = last_sum(ids, over_ring(tail_sum(ids, keep, swap(give, "pb", 1))), width // ring)
    last = over_chips([last] * chips)
    grad_sq, grad_sk, grad_sv, grad_so, grad_co, grad_cq = last_out(ids, last, over_core(last), width)
    return (
        result.reshape(hidden.shape),
        grad_hidden.reshape(hidden.shape),
        grad_encoder,
        grad_sq,
        grad_sk,
        grad_sv,
        grad_so,
        grad_cq,
        grad_ck,
        grad_cv,
        grad_co,
        grad_in,
        grad_out,
        gains[0],
        gains[1],
        gains[2],
    )


def solution(mesh):
    split = P(("pb", "pa"), None, None)
    passages = P("pb", "pa", None, None)
    return jax.shard_map(
        body,
        mesh=mesh,
        in_specs=(split, passages, P("pb", "pa")) + (P(),) * 13 + (split,),
        out_specs=(split, split, passages) + (P("pa", None),) * 10 + (P("pa"),) * 3,
        check_vma=False,
    )
```

```python
import functools

import jax
import jax.numpy as jnp
from jax import lax
from jax.experimental import pallas as pl
from jax.experimental.pallas import tpu as pltpu
from jax.sharding import PartitionSpec as P

HEADS = 12
EPS = 1e-06
NEG = -1000000000.0
F32 = jnp.float32
BF = jnp.bfloat16
SLOTS = 8
LANES = 128
MIB = 1 << 20


def dot(left, right, left_dim, right_dim, precision=None):
    return lax.dot_general(
        left,
        right,
        (((left_dim,), (right_dim,)), ((), ())),
        precision=precision,
        preferred_element_type=F32,
    )


def nn(left, right):
    return dot(left, right, 1, 0)


def nt(left, right):
    return dot(left, right, 1, 1)


def tn(left, right):
    return dot(left, right, 0, 0)


def low(values):
    return values.astype(BF)


def inverse_rms(values):
    return lax.rsqrt(jnp.mean(values * values, axis=-1, keepdims=True) + EPS)


def norm_back(grad, values, gain):
    inv = inverse_rms(values)
    scaled = gain * grad
    inner = jnp.mean(values * scaled, axis=-1, keepdims=True)
    grad_values = inv * scaled - values * (inv * inv * inv * inner)
    grad_gain = jnp.sum(grad * values * inv, axis=0, keepdims=True)
    return grad_values, grad_gain


def lanes_of(shape):
    return lax.broadcasted_iota(jnp.int32, shape, len(shape) - 1)


def rows_of(shape):
    return lax.broadcasted_iota(jnp.int32, shape, len(shape) - 2)


def ones_where(condition):
    return jnp.where(condition, 1.0, 0.0).astype(BF)


def spread_matrix(width):
    slot, lane = rows_of((LANES, width)), lanes_of((LANES, width))
    return ones_where((slot // SLOTS == lane // (width // HEADS)) & (slot % SLOTS < 3))


def compact_matrix():
    slot, lane = rows_of((LANES, LANES)), lanes_of((LANES, LANES))
    return ones_where((slot // SLOTS == lane // SLOTS) & (slot % SLOTS < 3))


def gather_matrix(width):
    feature, lane = rows_of((width, LANES)), lanes_of((width, LANES))
    return ones_where(feature // (width // HEADS) == lane // SLOTS)


def split_three(values):
    first = low(values).astype(F32)
    rest = values - first
    second = low(rest).astype(F32)
    third = low(rest - second).astype(F32)
    return first, second, third


def in_slots(values, start=0):
    first, second, third = split_three(values)
    slot = lanes_of(values.shape) % SLOTS - start
    return jnp.where(slot == 0, first, jnp.where(slot == 1, second, jnp.where(slot == 2, third, 0.0)))


def head_sums(values, matrix):
    first, second, third = split_three(values)
    return nn(low(first), matrix) + nn(low(second), matrix) + nn(low(third), matrix)


def two_heads(block):
    first = lanes_of(block.shape) < block.shape[1] // 2
    zero = jnp.zeros_like(block)
    return jnp.concatenate([jnp.where(first, block, zero), jnp.where(first, zero, block)], 0)


def fold_heads(block):
    half = block.shape[0] // 2
    lane = lanes_of((half, block.shape[1]))
    return jnp.where(lane < block.shape[1] // 2, block[:half], block[half:])


def pair_of_slots(extra, pair, start, more=None):
    lane = lanes_of(extra.shape)
    slot = lane % SLOTS
    wanted = (slot >= start) & (slot < start + 3)
    halves = [
        jnp.where(wanted & (lane // SLOTS == 2 * pair + i), extra, jnp.zeros_like(extra)) for i in range(2)
    ]
    block = jnp.concatenate(halves, 0)
    return block if more is None else block + more


def last_lane(rows, value):
    return jnp.where(lanes_of((rows, LANES)) == LANES - 1, value, 0.0).astype(BF)


def attend_pair(queries, keys, values, valid=None):
    scores = nt(keys, queries)
    if valid is not None:
        scores = jnp.where(valid, scores, NEG)
    top = jnp.max(scores, axis=0, keepdims=True)
    weights = low(jnp.exp(scores - top))
    both = tn(weights, values)
    split = both.shape[1] - LANES
    mixture = fold_heads(both[:, :split]) * (1.0 / fold_heads(both[:, split:]))
    return mixture, both[:, split:], top


def log_totals(sums, tops):
    tokens = tops[0].shape[1] // 2
    lane = lanes_of((tokens, LANES)) // SLOTS
    found = jnp.ones((tokens, LANES), F32)
    rows = []
    for pair, (both, top) in enumerate(zip(sums, tops)):
        found = jnp.where(lane == 2 * pair, both[:tokens], jnp.where(lane == 2 * pair + 1, both[tokens:], found))
        rows += [jnp.broadcast_to(top[:, :tokens], (SLOTS, tokens)), jnp.broadcast_to(top[:, tokens:], (SLOTS, tokens))]
    rows.append(jnp.zeros((LANES - HEADS * SLOTS, tokens), F32))
    return jnp.transpose(jnp.concatenate(rows, 0)) + jnp.log(found)


def attend_pair_back(queries, keys, values, grad_mix, query_more, key_more, grad_more, value_more, valid=None):
    scaled = two_heads(queries)
    grad_two = two_heads(grad_mix)
    scores = nt(jnp.concatenate([keys, key_more], 1), jnp.concatenate([scaled, query_more], 1))
    probs = jnp.exp(scores)
    if valid is not None:
        probs = jnp.where(valid, probs, 0.0)
    grad_probs = nt(jnp.concatenate([values, value_more], 1), jnp.concatenate([grad_two, grad_more], 1))
    grad_scores = low(probs * grad_probs)
    grad_values = nn(low(probs), grad_two)
    grad_keys = nn(grad_scores, scaled)
    grad_queries = fold_heads(tn(grad_scores, keys))
    return grad_queries, grad_keys, grad_values


def minus_slots(rows, start):
    slot = lanes_of((rows, LANES)) % SLOTS
    return jnp.where((slot >= start) & (slot < start + 3), -1.0, 0.0)


def causal_mask(tokens):
    key = rows_of((tokens, 2 * tokens))
    token = lanes_of((tokens, 2 * tokens))
    return key <= jnp.where(token >= tokens, token - tokens, token)


WEIGHTS = {
    "self_forward": 0,
    "key_values": 5,
    "cross_forward": 1,
    "feed_forward": 5,
    "cross_backward": 0,
    "key_grads": 6,
    "ffn_grads": 0,
    "first_sum": 0,
    "self_backward": 20,
    "encoder_grad": 0,
    "ring_sum": 0,
    "tail_grads": 0,
    "tail_sum": 0,
    "first_out": 0,
    "last_sum": 0,
    "last_out": 0,
    "meet": 0,
    "pack": 0,
    "hold": 0,
    "key_sum": 0,
    "key_add": 0,
    "first_add": 0,
}


class Line:
    def __init__(self):
        self.token = None

    def __call__(self, kernel, name, outs, args, mib, scratch=(), places="", after=(), weight=None):
        kinds = {"s": pltpu.SMEM, "h": pltpu.HBM, "v": pltpu.VMEM}
        placed = places[:1] == "i"
        specs = [pl.BlockSpec(memory_space=kinds[letter]) for letter in places[placed:]]
        count = len(args)
        single = not isinstance(outs, (tuple, list))
        outs = ((outs,) if single else tuple(outs)) + (shape32(SLOTS, LANES),)
        given = (() if self.token is None else (self.token,)) + tuple(after)
        homes = [pltpu.HBM if name == "self_forward" else pltpu.VMEM] * (len(outs) - 1) + [pltpu.VMEM]

        def run(*refs):
            at = count + len(given)
            made = refs[at : at + len(outs)]
            made[-1][...] = jnp.zeros((SLOTS, LANES), F32)
            here = ()
            if placed:
                lane = lax.axis_index("pb").astype(jnp.int32)
                here = ((lax.axis_index("pa").astype(jnp.int32), lane >> 1, lane & 1),)
            kernel(*here, *refs[:count], *made[:-1], *refs[at + len(outs) :])

        found = pl.pallas_call(
            run,
            out_shape=outs,
            in_specs=specs + [pl.BlockSpec(memory_space=pl.ANY)] * len(given),
            out_specs=[pl.BlockSpec(memory_space=home) for home in homes],
            scratch_shapes=scratch,
            compiler_params=pltpu.CompilerParams(vmem_limit_bytes=mib * MIB),
            cost_estimate=pl.CostEstimate(flops=int(1153000000 * (WEIGHTS[name] if weight is None else weight)), bytes_accessed=0, transcendentals=0),
            name=name,
        )(*args, *given)
        self.token = found[-1]
        return found[0] if single else found[:-1]

    def meet(self, weight, after=()):
        self(lambda *refs: None, "meet", (), (), 4, (), "", after, weight)


def shape(*dims):
    return jax.ShapeDtypeStruct(dims, BF)


def shape32(*dims):
    return jax.ShapeDtypeStruct(dims, F32)


def row(gain):
    return gain[...].reshape(1, gain.shape[0])


def self_forward_kernel(ids, *refs, chips):
    far, refs = refs[:9], refs[9:]
    outs, early = refs[:8], refs[8 : 8 + chips]
    held, made, mix_held, (sems, out_sems, early_sems) = (
        refs[8 + chips : 17 + chips], refs[17 + chips : 25 + chips], refs[25 + chips], refs[26 + chips :]
    )
    copies = [pltpu.make_async_copy(item, near, sems.at[i]) for i, (item, near) in enumerate(zip(far, held))]
    for item in copies:
        item.start()
    hidden, cot, gain_self, gain_cross = held[:4]
    weights = held[4:]
    q_out, k_out, v_out, mixture_out, logs_out, after_out, x_cross_out, cross_q_out = made
    x_held = mix_held.at[0]
    mixes = mix_held.at[1]
    pending = []

    def send(index):
        pending.append(pltpu.make_async_copy(made[index], outs[index], out_sems.at[index]))
        pending[-1].start()

    width = hidden.shape[1]
    tokens = hidden.shape[0]
    factor = (width // HEADS) ** -0.5
    copies[0].wait()
    copies[2].wait()
    stream = hidden[...].astype(F32)
    x_self = low(stream * inverse_rms(stream) * row(gain_self))
    x_held[...] = x_self
    for i in range(3):
        copies[4 + i].wait()
        made[i][...] = low(nn(x_self, weights[i][...]))
        send(i)
    queries, keys, values = (made[i][...] for i in range(3))
    copies[1].wait()
    for by, out in enumerate(early):
        pending.append(pltpu.make_async_copy(cot, out.at[:, pl.ds(width, width)], early_sems.at[2 * by]))
        pending[-1].start()
    valid = causal_mask(tokens)
    pair_width = 2 * width // HEADS
    ones = jnp.ones((tokens, LANES), BF)
    mixtures, sums, tops = [], [], []
    for pair in range(HEADS // 2):
        part = slice(pair * pair_width, (pair + 1) * pair_width)
        mixture, both, top = attend_pair(
            two_heads(queries[:, part] * factor), keys[:, part], jnp.concatenate([values[:, part], ones], 1), valid
        )
        mixtures.append(mixture)
        sums.append(both)
        tops.append(top)
    mixture = jnp.concatenate(mixtures, 1)
    mixture_out[...] = mixture
    send(3)
    logs_out[...] = log_totals(sums, tops)
    send(4)
    mix = low(mixture)
    mixes[...] = mix
    chip = ids[1]
    for by, out in enumerate(early):
        last = lax.div((chip ^ by) * 4, chips) == 3
        place = out.at[:, pl.ds(0, width)]

        @pl.when(last)
        def _():
            pltpu.make_async_copy(mixes, place, early_sems.at[2 * by + 1]).start()

        @pl.when(jnp.logical_not(last))
        def _():
            pltpu.make_async_copy(x_held, place, early_sems.at[2 * by + 1]).start()

        pending.append(pltpu.make_async_copy(x_held, place, early_sems.at[2 * by + 1]))
    copies[3].wait()
    copies[7].wait()
    after_self = stream + nn(mix, weights[3][...])
    after_out[...] = after_self
    send(5)
    x_cross = low(after_self * inverse_rms(after_self) * row(gain_cross))
    x_cross_out[...] = x_cross
    send(6)
    copies[8].wait()
    cross_q_out[...] = low(nn(x_cross, weights[4][...]))
    send(7)
    for item in pending:
        item.wait()


def self_forward(call, hidden, cot, gain_self, gain_cross, weights, chips):
    tokens, width = hidden.shape
    low_one = shape(tokens, width)
    args = (hidden, cot, gain_self, gain_cross) + tuple(weights)
    outs = (low_one, low_one, low_one, shape32(tokens, width), shape32(tokens, LANES),
            shape32(tokens, width), low_one, low_one)
    return call(
        functools.partial(self_forward_kernel, chips=chips),
        "self_forward",
        outs + (shape(tokens, 2 * width),) * chips,
        args,
        56,
        [pltpu.VMEM(item.shape, item.dtype) for item in args + outs]
        + [pltpu.VMEM((2, tokens, width), BF)]
        + [pltpu.SemaphoreType.DMA((size,)) for size in (len(args), len(outs), 2 * chips)],
        "i" + "h" * len(args),
    )


def key_values_kernel(encoder, w_ck, w_cv, keys, values, *, block):
    def step(index, carry):
        rows = pl.ds(pl.multiple_of(index * block, block), block)
        here = encoder[rows, :]
        keys[rows, :] = low(nn(here, w_ck[...]))
        values[rows, :] = low(nn(here, w_cv[...]))
        return carry

    lax.fori_loop(0, encoder.shape[0] // block, step, 0)


def key_values(call, encoder, w_ck, w_cv, block):
    return call(
        functools.partial(key_values_kernel, block=block), "key_values", (shape(*encoder.shape), shape(*encoder.shape)), (encoder, w_ck, w_cv), 24, (), "vvv"
    )


def key_rows(ids, count, step):
    key_count = count
    return pl.ds(pl.multiple_of((ids[0] ^ step) * key_count, LANES), key_count)


def cross_forward_kernel(ids, lengths, keys, values, queries, out, *, step, key_count):
    tokens, width = queries.shape
    factor = (width // HEADS) ** -0.5
    rows = key_rows(ids, key_count, step)
    size = (key_count, LANES)
    hidden_key = jnp.where(rows_of(size) < lengths[ids[0] ^ step], 0.0, NEG)
    key_more = jnp.where(lanes_of(size) == LANES - 1, hidden_key, 0.0).astype(BF)
    query_more = last_lane(2 * tokens, 1.0)
    ones = jnp.ones(size, BF)
    pair_width = 2 * width // HEADS
    sums, tops = [], []
    for pair in range(HEADS // 2):
        part = slice(pair * pair_width, (pair + 1) * pair_width)
        mixture, both, top = attend_pair(
            jnp.concatenate([two_heads(queries[:, part] * factor), query_more], 1),
            jnp.concatenate([keys[rows, part], key_more], 1),
            jnp.concatenate([values[rows, part], ones], 1),
        )
        out[:, part] = low(mixture)
        sums.append(both)
        tops.append(top)
    out[:, width:] = low(in_slots(log_totals(sums, tops)))


def cross_forward(call, lengths, queries, keys, values, step, after=(), weight=None):
    tokens, width = queries.shape
    key_count = keys.shape[0] // lengths.shape[0]
    return call(
        functools.partial(cross_forward_kernel, step=step, key_count=key_count),
        "cross_forward", shape(tokens, width + LANES), (lengths, keys, values, queries), 16, (), "isvvv",
        after, weight,
    )


def feed_forward_kernel(
    ids, after_self, cotangent, x_cross, gain_ffn, w_co, w_in, w_out, *refs, count, chips, chunks
):
    packed, refs = refs[:count], refs[count:]
    result_out, grad_after_out, g_cross_out, send_out, grad_gain_out = refs[:5]
    middle = refs[5 : 5 + chips]
    acts, grad_pres, act_held, grad_held = refs[5 + chips :]
    tokens, width = after_self.shape
    units = w_in.shape[1]
    wide = units // chunks
    compact, spread = compact_matrix(), spread_matrix(width)
    logs = [nn(part[:, width:], compact) for part in packed]
    top = functools.reduce(jnp.maximum, logs)
    log_total = top + jnp.log(sum(jnp.exp(item - top) for item in logs))
    mixture = sum(
        nn(low(in_slots(jnp.exp(item - log_total))), spread) * part[:, :width].astype(F32)
        for item, part in zip(logs, packed)
    )
    mix = low(mixture)
    after_cross = after_self[...] + nn(mix, w_co[...])
    x_ffn = low(after_cross * inverse_rms(after_cross) * row(gain_ffn))
    grad_low = cotangent[...]
    slope = (2.0 / 3.141592653589793) ** 0.5
    span = units // chips
    piece = units // (count * chips)

    def step(chunk, carry):
        part = pl.ds(pl.multiple_of(chunk * wide, LANES), wide)
        pre = nn(x_ffn, w_in[:, part])
        square = pre * pre
        bent = jnp.tanh(pre * (slope + (0.044715 * slope) * square))
        act_held[:, part] = low(0.5 * pre * (1.0 + bent))
        grad_act = nt(grad_low, w_out[part, :])
        bend = 0.5 * (1.0 + bent) + 0.5 * pre * (1.0 - bent * bent) * (slope + (3 * 0.044715 * slope) * square)
        grad_held[:, part] = low(grad_act * bend)
        return carry

    lax.fori_loop(0, chunks, step, 0)
    result = after_cross + nn(act_held[...], w_out[...])
    grad_x = nt(grad_held[...], w_in[...])
    for which in range(units // piece):
        slot = which // chips * piece
        acts[which % chips, :, slot : slot + piece] = act_held[:, which * piece : (which + 1) * piece]
    for which in range(chips):
        grad_pres[which] = grad_held[:, which * span : (which + 1) * span]
    result_out[...] = low(result)
    grad_values, grad_gain = norm_back(grad_x, after_cross, row(gain_ffn))
    grad_gain_out[...] = grad_gain
    grad_after = grad_low.astype(F32) + grad_values
    grad_after_out[...] = grad_after
    g_cross = low(grad_after)
    g_cross_out[...] = g_cross
    grad_mix = low(nt(g_cross, w_co[...]))
    delta = head_sums(grad_mix.astype(F32) * mixture, gather_matrix(width))
    send_out[:, :width] = grad_mix
    send_out[:, width:] = low(in_slots(log_total) + in_slots(delta, 3))
    chip = ids[1]
    for by, out in enumerate(middle):
        index = chip ^ by
        out[:, :width] = x_ffn
        out[:, 2 * width : 2 * width + span] = acts[index]
        out[:, 2 * width + span :] = grad_pres[index]
        early = lax.div(index * 2, chips) == 0

        @pl.when(early)
        def _():
            out[:, width : 2 * width] = mix

        @pl.when(jnp.logical_not(early))
        def _():
            out[:, width : 2 * width] = x_cross[...]


def feed_forward(call, after_self, cotangent, x_cross, gain_ffn, w_co, w_in, w_out, packed, chips):
    tokens, width = after_self.shape
    units = w_in.shape[1]
    span, chunks = units // chips, 4
    return call(
        functools.partial(feed_forward_kernel, count=len(packed), chips=chips, chunks=chunks),
        "feed_forward",
        (shape(tokens, width), shape32(tokens, width), shape(tokens, width), shape(tokens, width + LANES),
         shape32(1, width)) + (shape(tokens, 2 * width + 2 * span),) * chips,
        (after_self, cotangent, x_cross, gain_ffn, w_co, w_in, w_out) + tuple(packed),
        28,
        [pltpu.VMEM((chips, tokens, span), BF)] * 2 + [pltpu.VMEM((tokens, units), BF)] * 2,
        "ivvvvvvv" + "v" * len(packed),
    )


def cross_backward_kernel(ids, lengths, keys, values, queries, grads, grad_queries, grad_keys, grad_values, *, step):
    tokens, width = queries.shape
    key_count = grad_keys.shape[0]
    factor = (width // HEADS) ** -0.5
    rows = key_rows(ids, key_count, step)
    size = (key_count, LANES)
    hidden_key = jnp.where(rows_of(size) < lengths[ids[0] ^ step], 0.0, NEG)
    key_more = jnp.where(lanes_of(size) == LANES - 1, hidden_key, minus_slots(key_count, 0)).astype(BF)
    value_more = minus_slots(key_count, 3).astype(BF)
    extra = grads[:, width:]
    one = last_lane(2 * tokens, 1.0)
    pair_width = 2 * width // HEADS
    for pair in range(HEADS // 2):
        part = slice(pair * pair_width, (pair + 1) * pair_width)
        grad_q, grad_k, grad_v = attend_pair_back(
            queries[:, part] * factor, keys[rows, part], values[rows, part], grads[:, part],
            pair_of_slots(extra, pair, 0, one), key_more, pair_of_slots(extra, pair, 3), value_more,
        )
        grad_queries[:, part] = low(grad_q * factor)
        grad_keys[:, part] = low(grad_k)
        grad_values[:, part] = low(grad_v)


def cross_backward(call, lengths, queries, grads, keys, values, step):
    tokens, width = queries.shape
    key_count = keys.shape[0] // lengths.shape[0]
    return call(
        functools.partial(cross_backward_kernel, step=step),
        "cross_backward",
        (shape(tokens, width), shape(key_count, width), shape(key_count, width)),
        (lengths, keys, values, queries, grads), 20, (), "isvvvv",
    )


def extra_rows(four, width):
    return -(-6 * width // four // 8) * 8


def gain_block(gains, four, width_out):
    count = gains.shape[1] // four
    few = extra_rows(four, gains.shape[1])
    high = low(gains).astype(F32)
    rows = [part[i : i + 1, v * four : (v + 1) * four] for part in (high, gains - high) for i in range(3) for v in range(count)]
    block = jnp.concatenate(rows + [jnp.zeros((few - len(rows), four), F32)], 0)
    return low(jnp.concatenate([block, jnp.zeros((few, width_out - four), F32)], 1))


def gain_values(block, four, width):
    count = width // four
    rows = []
    for i in range(3):
        pieces = [
            block[i * count + v : i * count + v + 1, :four] + block[(3 + i) * count + v : (3 + i) * count + v + 1, :four]
            for v in range(count)
        ]
        rows.append(jnp.concatenate(pieces, 1))
    return jnp.concatenate(rows, 0)


def self_backward_kernel(
    ids, grad_after_cross, after_self, hidden, gain_self, gain_cross, grad_gain_ffn, g_cross,
    self_q, self_k, self_v, mixture, logs, *refs, count, chips
):
    weights, partial, refs = refs[:5], refs[5 : 5 + count], refs[5 + count :]
    hidden_out, late = refs[0], refs[1 : 1 + chips]
    fours, twos = refs[1 + chips :]
    tokens, width = after_self.shape
    factor = (width // HEADS) ** -0.5
    four, two = 4 * width // chips, 2 * width // chips
    grad_cq = low(sum(item[...].astype(F32) for item in partial))
    grad_values, grad_gain_cross = norm_back(nt(grad_cq, weights[0][...]), after_self[...], row(gain_cross))
    grad_after = grad_after_cross[...] + grad_values
    g_self = low(grad_after)
    grad_mix = low(nt(g_self, weights[1][...]))
    delta = head_sums(grad_mix.astype(F32) * mixture[...], gather_matrix(width))
    extra = low(in_slots(logs[...]) + in_slots(delta, 3))
    valid = causal_mask(tokens)
    key_more = minus_slots(tokens, 0).astype(BF)
    value_more = minus_slots(tokens, 3).astype(BF)
    pair_width = 2 * width // HEADS
    found = []
    for pair in range(HEADS // 2):
        part = slice(pair * pair_width, (pair + 1) * pair_width)
        grad_q, grad_k, grad_v = attend_pair_back(
            self_q[:, part] * factor, self_k[:, part], self_v[:, part], grad_mix[:, part],
            pair_of_slots(extra, pair, 0), key_more, pair_of_slots(extra, pair, 3), value_more, valid,
        )
        found.append((low(grad_q * factor), low(grad_k), low(grad_v)))
    grads = [jnp.concatenate([item[i] for item in found], 1) for i in range(3)]
    grad_x = jnp.zeros((tokens, width), F32)
    for i in range(3):
        grad_x = grad_x + nt(grads[i], weights[2 + i][...])
    grad_values, grad_gain_self = norm_back(grad_x, hidden[...].astype(F32), row(gain_self))
    hidden_out[...] = low(grad_after + grad_values)
    gains = jnp.concatenate([grad_gain_self, grad_gain_cross, grad_gain_ffn[...]], 0)
    block = gain_block(gains, four, four + two)
    for i, item in enumerate(grads + [g_self]):
        for v in range(width // four):
            fours[i * (width // four) + v] = item[:, v * four : (v + 1) * four]
    for i, item in enumerate((g_cross[...], grad_cq)):
        for v in range(width // two):
            twos[i * (width // two) + v] = item[:, v * two : (v + 1) * two]
    chip = ids[1]
    for by, out in enumerate(late):
        out[:tokens, :four] = fours[chip ^ by]
        out[:tokens, four:] = twos[chip ^ by]
        out[tokens:] = block


def self_backward(call, first, weights, partial, chips):
    tokens, width = first[1].shape
    four, two = 4 * width // chips, 2 * width // chips
    return call(
        functools.partial(self_backward_kernel, count=len(partial), chips=chips),
        "self_backward",
        (shape(tokens, width),) + (shape(tokens + extra_rows(four, width), four + two),) * chips,
        tuple(first) + tuple(weights) + tuple(partial),
        20,
        [pltpu.VMEM((chips, tokens, four), BF), pltpu.VMEM((chips, tokens, two), BF)],
        "i" + "v" * (len(first) + 5 + len(partial)),
    )


def stacked(refs, rows, lanes):
    return jnp.concatenate([item[rows, lanes] for item in refs], 0)


def hand_out(ids, held, keep, give):
    core = ids[2]
    keep[...] = held[core]
    give[...] = held[1 - core]


def ffn_grads_kernel(ids, *refs, chips):
    early, middle, (keep, give, held) = refs[:chips], refs[chips : 2 * chips], refs[2 * chips :]
    _, ring, half, both = held.shape
    span = both // 2
    width = early[0].shape[1] // 2
    every = slice(None)
    grad_in = low(
        tn(stacked(middle, every, slice(0, width)), stacked(middle, every, slice(2 * width + span, 2 * width + 2 * span)))
    )
    for z in range(ring):
        for c in range(2):
            at = (2 * z + c) * half
            held[c, z, :, :span] = grad_in[at : at + half]
    grad_out = low(
        tn(stacked(middle, every, slice(2 * width, 2 * width + span)), stacked(early, every, slice(width, 2 * width)))
    )
    few = span // (2 * ring)
    for z in range(ring):
        for c in range(2):
            at = (2 * z + c) * few
            block = grad_out[at : at + few]
            held[c, z, :, span:] = jnp.concatenate([block[:, v : v + span] for v in range(0, width, span)], 0)
    hand_out(ids, held, keep, give)


def ffn_grads(call, early, middle, ring, units):
    chips = len(early)
    width = early[0].shape[1] // 2
    part = (ring, width // (2 * ring), 2 * units // chips)
    return call(
        functools.partial(ffn_grads_kernel, chips=chips), "ffn_grads", (shape(*part),) * 2,
        tuple(early) + tuple(middle), 28, [pltpu.VMEM((2,) + part, BF)], "i" + "v" * (2 * chips),
    )


def key_grads_kernel(ids, encoder, *refs):
    grads, (keep, give, held) = refs[:-3], refs[-3:]
    count = len(grads) // 2
    _, ring, half, both = held.shape
    width = both // 2
    key_count = grads[0].shape[0]
    rows = jnp.concatenate([encoder[key_rows(ids, key_count, step), :] for step in range(count)], 0)
    for i in range(2):
        grad = low(tn(rows, stacked(grads[i * count : (i + 1) * count], slice(None), slice(None))))
        for z in range(ring):
            for c in range(2):
                at = (2 * z + c) * half
                held[c, z, :, i * width : (i + 1) * width] = grad[at : at + half]
    hand_out(ids, held, keep, give)


def key_grads(call, encoder, grad_keys, grad_values, ring):
    width = encoder.shape[1]
    part = (ring, width // (2 * ring), 2 * width)
    return call(
        key_grads_kernel, "key_grads", (shape(*part),) * 2, (encoder,) + tuple(grad_keys) + tuple(grad_values), 32,
        [pltpu.VMEM((2,) + part, BF)], "iv" + "v" * (2 * len(grad_keys)),
    )


def encoder_grad_kernel(ids, w_ck, w_cv, *refs):
    grads, out, held = refs[:-2], refs[-2], refs[-1]
    count = len(grads) // 2
    key_count = grads[0].shape[0]
    for index, item in enumerate(grads):
        held[index] = item[...]

    def step(index, carry):
        rows = pl.ds(pl.multiple_of((ids[0] ^ index) * key_count, LANES), key_count)
        out[rows, :] = low(nt(held[index], w_ck[...]) + nt(held[count + index], w_cv[...]))
        return carry

    lax.fori_loop(0, count, step, 0)


def encoder_grad(call, w_ck, w_cv, grad_keys, grad_values):
    key_count, width = grad_keys[0].shape
    return call(
        encoder_grad_kernel, "encoder_grad", shape(key_count * len(grad_keys), width),
        (w_ck, w_cv) + tuple(grad_keys) + tuple(grad_values), 12 + 3 * len(grad_keys),
        [pltpu.VMEM((2 * len(grad_keys), key_count, width), BF)], "ivv" + "v" * (2 * len(grad_keys)),
    )


def key_sum_kernel(ids, keep, came, even, odd, held):
    chips, two = held.shape[0], held.shape[3]
    summed = low(keep[...].astype(F32) + came[...].astype(F32))
    for j in range(chips):
        held[j] = summed[:, :, j * two : (j + 1) * two]
    for by in range(chips):
        (even, odd)[by % 2][by // 2] = held[ids[1] ^ by]


def key_sum(call, keep, came, chips):
    ring, half, both = keep.shape
    part = (ring, half, both // chips)
    return call(
        key_sum_kernel, "key_sum", (shape(chips // 2, *part),) * 2, (keep, came), 20, [pltpu.VMEM((chips,) + part, BF)],
        "ivv",
    )


def first_sum_kernel(ids, keep, came, *outs):
    for by in range(keep.shape[0]):
        z = ids[0] ^ by
        outs[by % 2][by // 2] = low(keep[z].astype(F32) + came[z].astype(F32))


def first_sum(call, keep, came):
    part = (keep.shape[0] // 2,) + keep.shape[1:]
    return call(first_sum_kernel, "first_sum", (shape(*part),) * 2, (keep, came), 16, (), "ivv")


def hold_kernel(item, out):
    out[...] = item[...]


def hold(call, item):
    return call(hold_kernel, "hold", shape(*item.shape), (item,), 8, (), "v")


def pack_kernel(*refs):
    for at, item in enumerate(refs[:-1]):
        refs[-1][at] = item[...]


def pack(call, parts):
    return call(pack_kernel, "pack", shape(len(parts), *parts[0].shape), tuple(parts), 16, (), "v" * len(parts))


def add_halves_kernel(*refs, count, inner):
    keep, came, outs = refs[: 1 if inner else count], refs[1 if inner else count], refs[2 if inner else count + 1 :]
    for at in range(count):
        mine = keep[0][at] if inner else keep[at][...]
        outs[at % 2][at // 2] = low(mine.astype(F32) + came[at].astype(F32))


def add_halves(call, name, keep, came):
    inner = not isinstance(keep, (tuple, list))
    count = came.shape[0]
    part = (count // 2,) + came.shape[1:]
    args = (keep,) if inner else tuple(keep)
    return call(
        functools.partial(add_halves_kernel, count=count, inner=inner), name, (shape(*part),) * 2, args + (came,), 16, (),
        "v" * (len(args) + 1),
    )


def halve(call, name, axis, keep, give, by):
    came = swap(give, axis, by)
    if came.shape[0] == 1:
        return keep, came
    keep, give = add_halves(call, name, keep, came)
    return halve(call, name, axis, keep, give, 2 * by)


def tail_grads_kernel(ids, *refs, chips):
    early, middle, late = refs[:chips], refs[chips : 2 * chips], refs[2 * chips : 3 * chips]
    keep, give, held = refs[3 * chips :]
    _, ring, more, both = held.shape
    four = both // 3 * 2
    width = early[0].shape[1] // 2
    half = more - extra_rows(four, width)
    tokens = early[0].shape[0]
    every, rows = slice(None), slice(0, tokens)
    grads = (
        (low(tn(stacked(early, every, slice(0, width)), stacked(late, rows, slice(0, four)))), slice(0, four)),
        (low(tn(stacked(middle, every, slice(width, 2 * width)), stacked(late, rows, slice(four, both)))), slice(four, both)),
    )
    gains = sum(gain_values(item[tokens:].astype(F32), four, width) for item in late)
    block = gain_block(gains, four, both)
    for z in range(ring):
        for c in range(2):
            at = (2 * z + c) * half
            for grad, lanes in grads:
                held[c, z, :half, lanes] = grad[at : at + half]
            held[c, z, half:, :] = block
    hand_out(ids, held, keep, give)


def tail_grads(call, early, middle, late, ring):
    chips = len(early)
    width = early[0].shape[1] // 2
    both = late[0].shape[1]
    part = (ring, width // (2 * ring) + extra_rows(both // 3 * 2, width), both)
    return call(
        functools.partial(tail_grads_kernel, chips=chips), "tail_grads", (shape(*part),) * 2,
        tuple(early) + tuple(middle) + tuple(late), 28, [pltpu.VMEM((2,) + part, BF)], "i" + "v" * (3 * chips),
    )


def tail_sum_kernel(ids, keep, came, part, more, *outs, chips):
    both = keep.shape[2]
    four = both // 3 * 2
    width = four * chips // 4
    half = keep.shape[1] - extra_rows(four, width)
    gains = gain_values(keep[0, half:].astype(F32), four, width) + gain_values(came[0, half:].astype(F32), four, width)
    block = gain_block(gains, four, outs[0].shape[1])
    for by, out in enumerate(outs):
        z = ids[0] ^ by
        out[:half, :both] = low(keep[z, :half].astype(F32) + came[z, :half].astype(F32))
        out[:half, both:] = low(part[0, z].astype(F32) + more[0, z].astype(F32))
        out[half:] = block


def tail_sum(call, keep, came, parts, chips):
    ring, more, both = keep.shape
    return call(
        functools.partial(tail_sum_kernel, chips=chips), "tail_sum",
        (shape(more, both + parts[0].shape[3]),) * ring, (keep, came) + tuple(parts), 16, (), "ivvvv",
    )


def ring_sum_kernel(keep, came, out):
    out[...] = low(keep[0].astype(F32) + came[0].astype(F32))


def ring_sum(call, parts):
    return call(ring_sum_kernel, "ring_sum", shape(*parts[0].shape[1:]), tuple(parts), 16, (), "vv")


def last_sum_kernel(ids, *refs):
    parts, (out, gains_out, held) = refs[:-3], refs[-3:]
    half, both = out.shape
    ring, _, rows = held.shape
    four = both // 2
    out[...] = low(sum(item[:half].astype(F32) for item in parts))
    gains = sum(gain_values(item[half:].astype(F32), four, ring * rows) for item in parts)
    for z in range(ring):
        held[z] = gains[:, z * rows : (z + 1) * rows]
    gains_out[...] = held[ids[0]]


def last_sum(call, parts, rows):
    more, both = parts[0].shape
    half = rows // 2
    return call(
        last_sum_kernel, "last_sum", (shape(half, both), shape32(3, rows)), tuple(parts), 16,
        [pltpu.VMEM((len(parts), 3, rows), F32)], "i" + "v" * len(parts),
    )


def place_pieces(ids, own, other, held):
    for by in range(own.shape[0]):
        held[ids[1] ^ by, ids[2]] = own[by]
        held[ids[1] ^ by, 1 - ids[2]] = other[by]


def first_out_kernel(ids, *refs, chips):
    own, other, in_out, out_out, held = refs
    place_pieces(ids, own, other, held)
    half, wide = held.shape[2:]
    span = wide // 2
    width = out_out.shape[1]
    few = half * span // width
    for j in range(chips):
        for c in range(2):
            rows = slice(c * half, (c + 1) * half)
            in_out[rows, j * span : (j + 1) * span] = held[j, c, :, :span].astype(F32)
            for v in range(width // span):
                at = (2 * j + c) * few
                out_out[at : at + few, v * span : (v + 1) * span] = held[
                    j, c, v * few : (v + 1) * few, span : 2 * span
                ].astype(F32)


def first_out(call, own, other, units, width):
    chips, half, wide = own.shape
    rows = 2 * half
    return call(
        functools.partial(first_out_kernel, chips=chips), "first_out",
        (shape32(rows, units), shape32(rows * units // width, width)),
        (own, other), 24, [pltpu.VMEM((chips, 2, half, wide), BF)], "ivv",
    )


def last_out_kernel(ids, *refs, chips):
    own, other, outs, held = refs[0], refs[1], refs[2:-1], refs[-1]
    place_pieces(ids, own, other, held)
    half, both = held.shape[2:]
    four, two = both // 2, both // 4
    for j in range(chips):
        for c in range(2):
            rows = slice(c * half, (c + 1) * half)
            at = j % (chips // 4) * four
            outs[j * 4 // chips][rows, at : at + four] = held[j, c, :, :four].astype(F32)
            at = j % (chips // 2) * two
            outs[4 + j * 2 // chips][rows, at : at + two] = held[j, c, :, four : four + two].astype(F32)
            outs[6 + j * 2 // chips][rows, at : at + two] = held[j, c, :, four + two :].astype(F32)


def last_out(call, own, other, width):
    chips, half, both = own.shape
    return call(
        functools.partial(last_out_kernel, chips=chips), "last_out", (shape32(2 * half, width),) * 8,
        (own, other), 24, [pltpu.VMEM((chips, 2, half, both), BF)], "ivv",
    )


def swap(values, axis, by):
    peers = lax.axis_size(axis)
    return lax.ppermute(values, axis, [(i, i ^ by) for i in range(peers)])


def over_chips(blocks):
    return [blocks[0]] + [swap(item, "pb", 2 * by) for by, item in enumerate(blocks) if by]


def over_ring(blocks):
    return [blocks[0]] + [swap(item, "pa", by) for by, item in enumerate(blocks) if by]


def over_core(blocks):
    return [swap(item, "pb", 1) for item in blocks]


def body(
    hidden, encoder, lengths, w_sq, w_sk, w_sv, w_so, w_cq, w_ck, w_cv, w_co, w_in, w_out,
    gain_self, gain_cross, gain_ffn, cotangent,
):
    _, tokens, width = hidden.shape
    questions, _, passage_len, _ = encoder.shape
    units = w_in.shape[1]
    ring = lax.axis_size("pa")
    chips = lax.axis_size("pb") // 2
    true_len = lengths.reshape(questions)
    hidden2 = hidden.reshape(tokens, width)
    cot = cotangent.reshape(tokens, width)
    enc = encoder.reshape(questions * passage_len, width)

    call = Line()
    found = self_forward(call, hidden2, cot, gain_self, gain_cross, (w_sq, w_sk, w_sv, w_so, w_cq), chips)
    self_q, self_k, self_v, mixture, logs, after_self, x_cross, cross_q = found[:8]
    asked = over_ring([cross_q] * ring)
    early = over_chips(found[8:])
    keys, values = key_values(call, enc, w_ck, w_cv, passage_len)
    near = chips - 1
    partial = []
    for step in range(ring):
        last = step == ring - 1
        partial.append(
            cross_forward(call, true_len, asked[step], keys, values, step, early[1:near] if last else (), 10 if last else None)
        )
    packed = over_ring(partial)
    call.meet(0, packed[1 : ring - 1] + early[near:])
    call.meet(3)
    found = feed_forward(call, after_self, cot, x_cross, gain_ffn, w_co, w_in, w_out, packed, chips)
    result, grad_after_cross, g_cross, sent, grad_gain_ffn = found[:5]
    given = over_ring([sent] * ring)
    middle = list(found[5:])
    back = {}
    for step in range(ring):
        back[step] = cross_backward(call, true_len, asked[step], given[step], keys, values, step)
        if step == 0:
            middle[near] = hold(call, middle[near])
    middle = over_chips(middle)
    partial = over_ring([back[step][0] for step in range(ring)])
    grad_keys, grad_values = [back[step][1] for step in range(ring)], [back[step][2] for step in range(ring)]
    key_keep, key_give = key_grads(call, enc, grad_keys, grad_values, ring)
    grad_encoder = encoder_grad(call, w_ck, w_cv, grad_keys, grad_values)
    ffn_keep, ffn_give = ffn_grads(call, early, middle, ring, units)
    call.meet(0, partial[2:])
    call.meet(20, ())
    key_parts = key_sum(call, key_keep, swap(key_give, "pb", 1), chips)
    first = first_sum(call, ffn_keep, swap(ffn_give, "pb", 1))
    found = self_backward(
        call,
        (grad_after_cross, after_self, hidden2, gain_self, gain_cross, grad_gain_ffn, g_cross,
         self_q, self_k, self_v, mixture, logs),
        (w_cq, w_so, w_sq, w_sk, w_sv),
        partial,
        chips,
    )
    grad_hidden = found[0]
    late = over_chips(found[1:])
    key_parts = halve(call, "key_add", "pb", *key_parts, 2)
    first = halve(call, "first_add", "pa", *first, 1)
    keep, give = tail_grads(call, early, middle, late, ring)
    call.meet(0, [key_parts[1], first[1]])
    call.meet(12)
    last = over_ring(tail_sum(call, keep, swap(give, "pb", 1), key_parts, chips))
    first = over_chips([ring_sum(call, first)] * chips)
    last, gains = last_sum(call, last, width // ring)
    last = over_chips([last] * chips)
    first = pack(call, first)
    last = pack(call, last)
    grad_in, grad_out = first_out(call, first, swap(first, "pb", 1), units, width)
    grad_sq, grad_sk, grad_sv, grad_so, grad_co, grad_cq, grad_ck, grad_cv = last_out(
        call, last, swap(last, "pb", 1), width
    )
    return (
        result.reshape(hidden.shape),
        grad_hidden.reshape(hidden.shape),
        grad_encoder.reshape(encoder.shape),
        grad_sq,
        grad_sk,
        grad_sv,
        grad_so,
        grad_cq,
        grad_ck,
        grad_cv,
        grad_co,
        grad_in,
        grad_out,
        gains[0],
        gains[1],
        gains[2],
    )


def solution(mesh):
    split = P(("pb", "pa"), None, None)
    passages = P("pb", "pa", None, None)
    return jax.shard_map(
        body,
        mesh=mesh,
        in_specs=(split, passages, P("pb", "pa")) + (P(),) * 13 + (split,),
        out_specs=(split, split, passages) + (P("pa", None),) * 10 + (P("pa"),) * 3,
        check_vma=False,
    )
```

```python
import functools

import jax
import jax.numpy as jnp
from jax import lax
from jax.experimental import pallas as pl
from jax.experimental.pallas import tpu as pltpu
from jax.sharding import PartitionSpec as P

HEADS = 12
EPS = 1e-06
NEG = -1000000000.0
F32 = jnp.float32
BF = jnp.bfloat16
SLOTS = 4
LANES = 128
MIB = 1 << 20


def dot(left, right, left_dim, right_dim, precision=None):
    return lax.dot_general(
        left,
        right,
        (((left_dim,), (right_dim,)), ((), ())),
        precision=precision,
        preferred_element_type=F32,
    )


def nn(left, right):
    return dot(left, right, 1, 0)


def nt(left, right):
    return dot(left, right, 1, 1)


def tn(left, right):
    return dot(left, right, 0, 0)


def low(values):
    return values.astype(BF)


def inverse_rms(values):
    return lax.rsqrt(jnp.mean(values * values, axis=-1, keepdims=True) + EPS)


def norm_back(grad, values, gain):
    inv = inverse_rms(values)
    scaled = gain * grad
    inner = jnp.mean(values * scaled, axis=-1, keepdims=True)
    grad_values = inv * scaled - values * (inv * inv * inv * inner)
    grad_gain = jnp.sum(grad * values * inv, axis=0, keepdims=True)
    return grad_values, grad_gain


def lanes_of(shape):
    return lax.broadcasted_iota(jnp.int32, shape, len(shape) - 1)


def rows_of(shape):
    return lax.broadcasted_iota(jnp.int32, shape, len(shape) - 2)


def ones_where(condition):
    return jnp.where(condition, 1.0, 0.0).astype(BF)


def spread_matrix(width):
    slot, lane = rows_of((LANES, width)), lanes_of((LANES, width))
    return ones_where((slot // SLOTS == lane // (width // HEADS)) & (slot % SLOTS < 2))


def compact_matrix():
    slot, lane = rows_of((LANES, LANES)), lanes_of((LANES, LANES))
    return ones_where((slot // SLOTS == lane // SLOTS) & (slot % SLOTS < 2))


def gather_matrix(width):
    feature, lane = rows_of((width, LANES)), lanes_of((width, LANES))
    return ones_where(feature // (width // HEADS) == lane // SLOTS)


def split_three(values):
    first = low(values).astype(F32)
    rest = values - first
    second = low(rest).astype(F32)
    third = low(rest - second).astype(F32)
    return first, second, third


def in_slots(values, start=0):
    first, second, _ = split_three(values)
    slot = lanes_of(values.shape) % SLOTS - start
    return jnp.where(slot == 0, first, jnp.where(slot == 1, second, 0.0))


def to_rows(extra, width):
    turned = jnp.transpose(extra)
    few = HEADS * SLOTS * extra.shape[0] // width
    return jnp.concatenate([turned[at : at + few] for at in range(0, HEADS * SLOTS, few)], 1)


def from_rows(rows, tokens):
    few = rows.shape[0]
    parts = [rows[:, at : at + tokens].astype(F32) for at in range(0, rows.shape[1], tokens)]
    parts.append(jnp.zeros((LANES - few * len(parts), tokens), F32))
    return low(jnp.transpose(jnp.concatenate(parts, 0)))


def few_rows(tokens, width):
    return HEADS * SLOTS * tokens // width


def head_sums(values, matrix):
    first, second, third = split_three(values)
    return nn(low(first), matrix) + nn(low(second), matrix) + nn(low(third), matrix)


def two_heads(block):
    first = lanes_of(block.shape) < block.shape[1] // 2
    zero = jnp.zeros_like(block)
    return jnp.concatenate([jnp.where(first, block, zero), jnp.where(first, zero, block)], 0)


def fold_heads(block):
    half = block.shape[0] // 2
    lane = lanes_of((half, block.shape[1]))
    return jnp.where(lane < block.shape[1] // 2, block[:half], block[half:])


def pair_of_slots(extra, pair, start, more=None):
    lane = lanes_of(extra.shape)
    slot = lane % SLOTS
    wanted = (slot >= start) & (slot < start + 2)
    halves = [
        jnp.where(wanted & (lane // SLOTS == 2 * pair + i), extra, jnp.zeros_like(extra)) for i in range(2)
    ]
    block = jnp.concatenate(halves, 0)
    return block if more is None else block + more


def last_lane(rows, value):
    return jnp.where(lanes_of((rows, LANES)) == LANES - 1, value, 0.0).astype(BF)


def attend_pair(queries, keys, values, valid=None):
    scores = nt(keys, queries)
    if valid is not None:
        scores = jnp.where(valid, scores, NEG)
    top = jnp.max(scores, axis=0, keepdims=True)
    weights = low(jnp.exp(scores - top))
    both = tn(weights, values)
    split = both.shape[1] - LANES
    mixture = fold_heads(both[:, :split]) * (1.0 / fold_heads(both[:, split:]))
    return mixture, both[:, split:], top


def log_totals(sums, tops):
    tokens = tops[0].shape[1] // 2
    lane = lanes_of((tokens, LANES)) // SLOTS
    found = jnp.ones((tokens, LANES), F32)
    rows = []
    for pair, (both, top) in enumerate(zip(sums, tops)):
        found = jnp.where(lane == 2 * pair, both[:tokens], jnp.where(lane == 2 * pair + 1, both[tokens:], found))
        rows += [jnp.broadcast_to(top[:, :tokens], (SLOTS, tokens)), jnp.broadcast_to(top[:, tokens:], (SLOTS, tokens))]
    rows.append(jnp.zeros((LANES - HEADS * SLOTS, tokens), F32))
    return jnp.transpose(jnp.concatenate(rows, 0)) + jnp.log(found)


def attend_pair_back(queries, keys, values, grad_mix, query_more, key_more, grad_more, value_more, valid=None):
    scaled = two_heads(queries)
    grad_two = two_heads(grad_mix)
    scores = nt(jnp.concatenate([keys, key_more], 1), jnp.concatenate([scaled, query_more], 1))
    probs = jnp.exp(scores)
    if valid is not None:
        probs = jnp.where(valid, probs, 0.0)
    grad_probs = nt(jnp.concatenate([values, value_more], 1), jnp.concatenate([grad_two, grad_more], 1))
    grad_scores = low(probs * grad_probs)
    grad_values = nn(low(probs), grad_two)
    grad_keys = nn(grad_scores, scaled)
    grad_queries = fold_heads(tn(grad_scores, keys))
    return grad_queries, grad_keys, grad_values


def minus_slots(rows, start):
    slot = lanes_of((rows, LANES)) % SLOTS
    return jnp.where((slot >= start) & (slot < start + 2), -1.0, 0.0)


def causal_mask(tokens):
    key = rows_of((tokens, 2 * tokens))
    token = lanes_of((tokens, 2 * tokens))
    return key <= jnp.where(token >= tokens, token - tokens, token)


WEIGHTS = {
    "self_forward": 0,
    "key_values": 5,
    "cross_forward": 1,
    "feed_forward": 5,
    "cross_backward": 4,
    "key_grads": 2,
    "ffn_grads": 0,
    "first_sum": 0,
    "self_backward": 20,
    "early_pack": 0,
    "encoder_grad": 0,
    "ring_sum": 0,
    "tail_grads": 0,
    "tail_sum": 0,
    "first_out": 0,
    "last_sum": 0,
    "last_out": 0,
    "meet": 0,
    "pack": 0,
    "hold": 0,
    "key_sum": 0,
    "key_add": 0,
    "first_add": 0,
}


class Line:
    def __init__(self):
        self.token = None

    def __call__(self, kernel, name, outs, args, mib, scratch=(), places="", after=(), weight=None):
        kinds = {"s": pltpu.SMEM, "h": pltpu.HBM, "v": pltpu.VMEM}
        placed = places[:1] == "i"
        specs = [pl.BlockSpec(memory_space=kinds[letter]) for letter in places[placed:]]
        count = len(args)
        single = not isinstance(outs, (tuple, list))
        outs = ((outs,) if single else tuple(outs)) + (shape32(8, LANES),)
        given = (() if self.token is None else (self.token,)) + tuple(after)
        homes = [pltpu.HBM if name == "self_forward" else pltpu.VMEM] * (len(outs) - 1) + [pltpu.VMEM]

        def run(*refs):
            at = count + len(given)
            made = refs[at : at + len(outs)]
            made[-1][...] = jnp.zeros((8, LANES), F32)
            here = ()
            if placed:
                lane = lax.axis_index("pb").astype(jnp.int32)
                here = ((lax.axis_index("pa").astype(jnp.int32), lane >> 1, lane & 1),)
            kernel(*here, *refs[:count], *made[:-1], *refs[at + len(outs) :])

        found = pl.pallas_call(
            run,
            out_shape=outs,
            in_specs=specs + [pl.BlockSpec(memory_space=pl.ANY)] * len(given),
            out_specs=[pl.BlockSpec(memory_space=home) for home in homes],
            scratch_shapes=scratch,
            compiler_params=pltpu.CompilerParams(vmem_limit_bytes=mib * MIB),
            cost_estimate=pl.CostEstimate(flops=int(1153000000 * (WEIGHTS[name] if weight is None else weight)), bytes_accessed=0, transcendentals=0),
            name=name,
        )(*args, *given)
        self.token = found[-1]
        return found[0] if single else found[:-1]

    def meet(self, weight, after=()):
        self(lambda *refs: None, "meet", (), (), 4, (), "", after, weight)


def shape(*dims):
    return jax.ShapeDtypeStruct(dims, BF)


def shape32(*dims):
    return jax.ShapeDtypeStruct(dims, F32)


def row(gain):
    return gain[...].reshape(1, gain.shape[0])


def self_forward_kernel(*refs):
    far, outs, refs = refs[:8], refs[8:18], refs[18:]
    held, made, (sems, out_sems) = refs[:8], refs[8:18], refs[18:]
    copies = [pltpu.make_async_copy(item, near, sems.at[i]) for i, (item, near) in enumerate(zip(far, held))]
    for item in copies:
        item.start()
    hidden, gain_self, gain_cross = held[:3]
    weights = held[3:]
    (x_self_out, q_out, k_out, v_out, mix_out, mixture_out, logs_out, after_out, x_cross_out, cross_q_out) = made
    pending = []

    def send(index):
        pending.append(pltpu.make_async_copy(made[index], outs[index], out_sems.at[index]))
        pending[-1].start()

    tokens, width = hidden.shape
    factor = (width // HEADS) ** -0.5
    copies[0].wait()
    copies[1].wait()
    stream = hidden[...].astype(F32)
    x_self = low(stream * inverse_rms(stream) * row(gain_self))
    x_self_out[...] = x_self
    send(0)
    for i in range(3):
        copies[3 + i].wait()
        made[1 + i][...] = low(nn(x_self, weights[i][...]))
        send(1 + i)
    queries, keys, values = (made[1 + i][...] for i in range(3))
    valid = causal_mask(tokens)
    pair_width = 2 * width // HEADS
    ones = jnp.ones((tokens, LANES), BF)
    mixtures, sums, tops = [], [], []
    for pair in range(HEADS // 2):
        part = slice(pair * pair_width, (pair + 1) * pair_width)
        mixture, both, top = attend_pair(
            two_heads(queries[:, part] * factor), keys[:, part], jnp.concatenate([values[:, part], ones], 1), valid
        )
        mixtures.append(mixture)
        sums.append(both)
        tops.append(top)
    mixture = jnp.concatenate(mixtures, 1)
    mixture_out[...] = mixture
    send(5)
    mix = low(mixture)
    mix_out[...] = mix
    send(4)
    logs_out[...] = log_totals(sums, tops)
    send(6)
    copies[2].wait()
    copies[6].wait()
    after_self = stream + nn(mix, weights[3][...])
    after_out[...] = after_self
    send(7)
    x_cross = low(after_self * inverse_rms(after_self) * row(gain_cross))
    x_cross_out[...] = x_cross
    send(8)
    copies[7].wait()
    cross_q_out[...] = low(nn(x_cross, weights[4][...]))
    send(9)
    for item in pending:
        item.wait()


def self_forward(call, hidden, gain_self, gain_cross, weights):
    tokens, width = hidden.shape
    low_one = shape(tokens, width)
    args = (hidden, gain_self, gain_cross) + tuple(weights)
    outs = (low_one,) * 5 + (
        shape32(tokens, width), shape32(tokens, LANES), shape32(tokens, width), low_one, low_one,
    )
    return call(
        self_forward_kernel, "self_forward", outs, args, 56,
        [pltpu.VMEM(item.shape, item.dtype) for item in args + outs]
        + [pltpu.SemaphoreType.DMA((size,)) for size in (len(args), len(outs))],
        "h" * len(args),
    )


def early_pack_kernel(ids, x_self, mix, cot, after_self, *early):
    chips = len(early)
    width = cot.shape[1]
    for by, out in enumerate(early):
        out[:, width : 2 * width] = cot[...]
        out[:, 2 * width :] = low(after_self[...])
        last = lax.div((ids[1] ^ by) * 4, chips) == 3

        @pl.when(last)
        def _():
            out[:, :width] = mix[...]

        @pl.when(jnp.logical_not(last))
        def _():
            out[:, :width] = x_self[...]


def early_pack(call, x_self, mix, cot, after_self, chips):
    tokens, width = cot.shape
    return call(
        early_pack_kernel, "early_pack", (shape(tokens, 3 * width),) * chips, (x_self, mix, cot, after_self), 12, (), "ivvvv"
    )


def key_values_kernel(encoder, w_ck, w_cv, keys, values, *, block):
    def step(index, carry):
        rows = pl.ds(pl.multiple_of(index * block, block), block)
        here = encoder[rows, :]
        keys[rows, :] = low(nn(here, w_ck[...]))
        values[rows, :] = low(nn(here, w_cv[...]))
        return carry

    lax.fori_loop(0, encoder.shape[0] // block, step, 0)


def key_values(call, encoder, w_ck, w_cv, block):
    return call(
        functools.partial(key_values_kernel, block=block), "key_values", (shape(*encoder.shape), shape(*encoder.shape)), (encoder, w_ck, w_cv), 24, (), "vvv"
    )


def key_rows(ids, count, step):
    key_count = count
    return pl.ds(pl.multiple_of((ids[0] ^ step) * key_count, LANES), key_count)


def cross_forward_kernel(ids, lengths, keys, values, queries, out, *, step, key_count):
    tokens, width = queries.shape
    factor = (width // HEADS) ** -0.5
    rows = key_rows(ids, key_count, step)
    size = (key_count, LANES)
    hidden_key = jnp.where(rows_of(size) < lengths[ids[0] ^ step], 0.0, NEG)
    key_more = jnp.where(lanes_of(size) == LANES - 1, hidden_key, 0.0).astype(BF)
    query_more = last_lane(2 * tokens, 1.0)
    ones = jnp.ones(size, BF)
    pair_width = 2 * width // HEADS
    sums, tops = [], []
    for pair in range(HEADS // 2):
        part = slice(pair * pair_width, (pair + 1) * pair_width)
        mixture, both, top = attend_pair(
            jnp.concatenate([two_heads(queries[:, part] * factor), query_more], 1),
            jnp.concatenate([keys[rows, part], key_more], 1),
            jnp.concatenate([values[rows, part], ones], 1),
        )
        out[:tokens, part] = low(mixture)
        sums.append(both)
        tops.append(top)
    out[tokens:] = low(to_rows(in_slots(log_totals(sums, tops)), width))


def cross_forward(call, lengths, queries, keys, values, step, after=(), weight=None):
    tokens, width = queries.shape
    key_count = keys.shape[0] // lengths.shape[0]
    return call(
        functools.partial(cross_forward_kernel, step=step, key_count=key_count),
        "cross_forward", shape(tokens + few_rows(tokens, width), width), (lengths, keys, values, queries), 16, (), "isvvv",
        after, weight,
    )


def feed_forward_kernel(
    ids, after_self, cotangent, gain_ffn, w_co, w_in, w_out, *refs, count, chips, chunks
):
    packed, refs = refs[:count], refs[count:]
    result_out, grad_after_out, g_cross_out, send_out, grad_gain_out = refs[:5]
    middle = refs[5 : 5 + chips]
    acts, grad_pres, act_held, grad_held = refs[5 + chips :]
    tokens, width = after_self.shape
    units = w_in.shape[1]
    wide = units // chunks
    compact, spread = compact_matrix(), spread_matrix(width)
    logs = [nn(from_rows(part[tokens:], tokens), compact) for part in packed]
    top = functools.reduce(jnp.maximum, logs)
    log_total = top + jnp.log(sum(jnp.exp(item - top) for item in logs))
    mixture = sum(
        nn(low(in_slots(jnp.exp(item - log_total))), spread) * part[:tokens].astype(F32)
        for item, part in zip(logs, packed)
    )
    mix = low(mixture)
    after_cross = after_self[...] + nn(mix, w_co[...])
    x_ffn = low(after_cross * inverse_rms(after_cross) * row(gain_ffn))
    grad_low = cotangent[...]
    slope = (2.0 / 3.141592653589793) ** 0.5
    span = units // chips
    piece = units // (count * chips)

    def step(chunk, carry):
        part = pl.ds(pl.multiple_of(chunk * wide, LANES), wide)
        pre = nn(x_ffn, w_in[:, part])
        square = pre * pre
        bent = jnp.tanh(pre * (slope + (0.044715 * slope) * square))
        act_held[:, part] = low(0.5 * pre * (1.0 + bent))
        grad_act = nt(grad_low, w_out[part, :])
        bend = 0.5 * (1.0 + bent) + 0.5 * pre * (1.0 - bent * bent) * (slope + (3 * 0.044715 * slope) * square)
        grad_held[:, part] = low(grad_act * bend)
        return carry

    lax.fori_loop(0, chunks, step, 0, unroll=True)
    result = after_cross + nn(act_held[...], w_out[...])
    grad_x = nt(grad_held[...], w_in[...])
    for which in range(units // piece):
        slot = which // chips * piece
        acts[which % chips, :, slot : slot + piece] = act_held[:, which * piece : (which + 1) * piece]
    for which in range(chips):
        grad_pres[which] = grad_held[:, which * span : (which + 1) * span]
    result_out[...] = low(result)
    grad_values, grad_gain = norm_back(grad_x, after_cross, row(gain_ffn))
    grad_gain_out[...] = grad_gain
    grad_after = grad_low.astype(F32) + grad_values
    grad_after_out[...] = grad_after
    g_cross = low(grad_after)
    g_cross_out[...] = g_cross
    grad_mix = low(nt(g_cross, w_co[...]))
    delta = head_sums(grad_mix.astype(F32) * mixture, gather_matrix(width))
    send_out[:tokens] = grad_mix
    send_out[tokens:] = low(to_rows(in_slots(log_total) + in_slots(delta, 2), width))
    chip = ids[1]
    for by, out in enumerate(middle):
        index = chip ^ by
        out[:, :width] = mix
        out[:, width : width + span] = acts[index]
        out[:, width + span :] = grad_pres[index]


def feed_forward(call, after_self, cotangent, gain_ffn, w_co, w_in, w_out, packed, chips):
    tokens, width = after_self.shape
    units = w_in.shape[1]
    span, chunks = units // chips, 4
    return call(
        functools.partial(feed_forward_kernel, count=len(packed), chips=chips, chunks=chunks),
        "feed_forward",
        (shape(tokens, width), shape32(tokens, width), shape(tokens, width), shape(tokens + few_rows(tokens, width), width),
         shape32(1, width)) + (shape(tokens, width + 2 * span),) * chips,
        (after_self, cotangent, gain_ffn, w_co, w_in, w_out) + tuple(packed),
        28,
        [pltpu.VMEM((chips, tokens, span), BF)] * 2 + [pltpu.VMEM((tokens, units), BF)] * 2,
        "ivvvvvv" + "v" * len(packed),
    )


def cross_backward_kernel(ids, lengths, keys, values, queries, grads, grad_queries, grad_keys, grad_values, *, step):
    tokens, width = queries.shape
    key_count = grad_keys.shape[0]
    factor = (width // HEADS) ** -0.5
    rows = key_rows(ids, key_count, step)
    size = (key_count, LANES)
    hidden_key = jnp.where(rows_of(size) < lengths[ids[0] ^ step], 0.0, NEG)
    key_more = jnp.where(lanes_of(size) == LANES - 1, hidden_key, minus_slots(key_count, 0)).astype(BF)
    value_more = minus_slots(key_count, 2).astype(BF)
    extra = from_rows(grads[tokens:], tokens)
    one = last_lane(2 * tokens, 1.0)
    pair_width = 2 * width // HEADS
    for pair in range(HEADS // 2):
        part = slice(pair * pair_width, (pair + 1) * pair_width)
        grad_q, grad_k, grad_v = attend_pair_back(
            queries[:, part] * factor, keys[rows, part], values[rows, part], grads[:tokens, part],
            pair_of_slots(extra, pair, 0, one), key_more, pair_of_slots(extra, pair, 2), value_more,
        )
        grad_queries[:, part] = low(grad_q * factor)
        grad_keys[:, part] = low(grad_k)
        grad_values[:, part] = low(grad_v)


def cross_backward(call, lengths, queries, grads, keys, values, step):
    tokens, width = queries.shape
    key_count = keys.shape[0] // lengths.shape[0]
    return call(
        functools.partial(cross_backward_kernel, step=step),
        "cross_backward",
        (shape(tokens, width), shape(key_count, width), shape(key_count, width)),
        (lengths, keys, values, queries, grads), 20, (), "isvvvv",
    )


def extra_rows(four, width):
    return -(-6 * width // four // 8) * 8


def gain_block(gains, four, width_out):
    count = gains.shape[1] // four
    few = extra_rows(four, gains.shape[1])
    high = low(gains).astype(F32)
    rows = [part[i : i + 1, v * four : (v + 1) * four] for part in (high, gains - high) for i in range(3) for v in range(count)]
    block = jnp.concatenate(rows + [jnp.zeros((few - len(rows), four), F32)], 0)
    return low(jnp.concatenate([block, jnp.zeros((few, width_out - four), F32)], 1))


def gain_values(block, four, width):
    count = width // four
    rows = []
    for i in range(3):
        pieces = [
            block[i * count + v : i * count + v + 1, :four] + block[(3 + i) * count + v : (3 + i) * count + v + 1, :four]
            for v in range(count)
        ]
        rows.append(jnp.concatenate(pieces, 1))
    return jnp.concatenate(rows, 0)


def self_backward_kernel(
    ids, grad_after_cross, after_self, hidden, gain_self, gain_cross, grad_gain_ffn, g_cross,
    self_q, self_k, self_v, mixture, logs, *refs, count, chips
):
    weights, partial, refs = refs[:5], refs[5 : 5 + count], refs[5 + count :]
    hidden_out, late = refs[0], refs[1 : 1 + chips]
    fours, twos = refs[1 + chips :]
    tokens, width = after_self.shape
    factor = (width // HEADS) ** -0.5
    four, two = 4 * width // chips, 2 * width // chips
    grad_cq = low(sum(item[...].astype(F32) for item in partial))
    grad_values, grad_gain_cross = norm_back(nt(grad_cq, weights[0][...]), after_self[...], row(gain_cross))
    grad_after = grad_after_cross[...] + grad_values
    g_self = low(grad_after)
    grad_mix = low(nt(g_self, weights[1][...]))
    delta = head_sums(grad_mix.astype(F32) * mixture[...], gather_matrix(width))
    extra = low(in_slots(logs[...]) + in_slots(delta, 2))
    valid = causal_mask(tokens)
    key_more = minus_slots(tokens, 0).astype(BF)
    value_more = minus_slots(tokens, 2).astype(BF)
    pair_width = 2 * width // HEADS
    found = []
    for pair in range(HEADS // 2):
        part = slice(pair * pair_width, (pair + 1) * pair_width)
        grad_q, grad_k, grad_v = attend_pair_back(
            self_q[:, part] * factor, self_k[:, part], self_v[:, part], grad_mix[:, part],
            pair_of_slots(extra, pair, 0), key_more, pair_of_slots(extra, pair, 2), value_more, valid,
        )
        found.append((low(grad_q * factor), low(grad_k), low(grad_v)))
    grads = [jnp.concatenate([item[i] for item in found], 1) for i in range(3)]
    grad_x = jnp.zeros((tokens, width), F32)
    for i in range(3):
        grad_x = grad_x + nt(grads[i], weights[2 + i][...])
    grad_values, grad_gain_self = norm_back(grad_x, hidden[...].astype(F32), row(gain_self))
    hidden_out[...] = low(grad_after + grad_values)
    gains = jnp.concatenate([grad_gain_self, grad_gain_cross, grad_gain_ffn[...]], 0)
    block = gain_block(gains, four, four + two)
    for i, item in enumerate(grads + [g_self]):
        for v in range(width // four):
            fours[i * (width // four) + v] = item[:, v * four : (v + 1) * four]
    for i, item in enumerate((g_cross[...], grad_cq)):
        for v in range(width // two):
            twos[i * (width // two) + v] = item[:, v * two : (v + 1) * two]
    chip = ids[1]
    for by, out in enumerate(late):
        out[:tokens, :four] = fours[chip ^ by]
        out[:tokens, four:] = twos[chip ^ by]
        out[tokens:] = block


def self_backward(call, first, weights, partial, chips):
    tokens, width = first[1].shape
    four, two = 4 * width // chips, 2 * width // chips
    return call(
        functools.partial(self_backward_kernel, count=len(partial), chips=chips),
        "self_backward",
        (shape(tokens, width),) + (shape(tokens + extra_rows(four, width), four + two),) * chips,
        tuple(first) + tuple(weights) + tuple(partial),
        20,
        [pltpu.VMEM((chips, tokens, four), BF), pltpu.VMEM((chips, tokens, two), BF)],
        "i" + "v" * (len(first) + 5 + len(partial)),
    )


def stacked(refs, rows, lanes):
    return jnp.concatenate([item[rows, lanes] for item in refs], 0)


def hand_out(ids, held, keep, give):
    core = ids[2]
    keep[...] = held[core]
    give[...] = held[1 - core]


def ffn_grads_kernel(ids, w_co, gain_ffn, *refs, chips):
    early, middle, (keep, give, held) = refs[:chips], refs[chips : 2 * chips], refs[2 * chips :]
    _, ring, half, both = held.shape
    span = both // 2
    width = early[0].shape[1] // 3
    every = slice(None)
    mix = stacked(middle, every, slice(0, width))
    after_cross = stacked(early, every, slice(2 * width, 3 * width)).astype(F32) + nn(mix, w_co[...])
    x_ffn = low(after_cross * inverse_rms(after_cross) * row(gain_ffn))
    grad_in = low(tn(x_ffn, stacked(middle, every, slice(width + span, width + 2 * span))))
    for z in range(ring):
        for c in range(2):
            at = (2 * z + c) * half
            held[c, z, :, :span] = grad_in[at : at + half]
    grad_out = low(
        tn(stacked(middle, every, slice(width, width + span)), stacked(early, every, slice(width, 2 * width)))
    )
    few = span // (2 * ring)
    for z in range(ring):
        for c in range(2):
            at = (2 * z + c) * few
            block = grad_out[at : at + few]
            held[c, z, :, span:] = jnp.concatenate([block[:, v : v + span] for v in range(0, width, span)], 0)
    hand_out(ids, held, keep, give)


def ffn_grads(call, w_co, gain_ffn, early, middle, ring, units):
    chips = len(early)
    width = early[0].shape[1] // 3
    part = (ring, width // (2 * ring), 2 * units // chips)
    return call(
        functools.partial(ffn_grads_kernel, chips=chips), "ffn_grads", (shape(*part),) * 2,
        (w_co, gain_ffn) + tuple(early) + tuple(middle), 28, [pltpu.VMEM((2,) + part, BF)], "ivv" + "v" * (2 * chips),
    )


def key_grads_kernel(ids, encoder, *refs):
    grads, (keep, give, held) = refs[:-3], refs[-3:]
    count = len(grads) // 2
    _, ring, half, both = held.shape
    width = both // 2
    key_count = grads[0].shape[0]
    rows = jnp.concatenate([encoder[key_rows(ids, key_count, step), :] for step in range(count)], 0)
    for i in range(2):
        grad = low(tn(rows, stacked(grads[i * count : (i + 1) * count], slice(None), slice(None))))
        for z in range(ring):
            for c in range(2):
                at = (2 * z + c) * half
                held[c, z, :, i * width : (i + 1) * width] = grad[at : at + half]
    hand_out(ids, held, keep, give)


def key_grads(call, encoder, grad_keys, grad_values, ring):
    width = encoder.shape[1]
    part = (ring, width // (2 * ring), 2 * width)
    return call(
        key_grads_kernel, "key_grads", (shape(*part),) * 2, (encoder,) + tuple(grad_keys) + tuple(grad_values), 32,
        [pltpu.VMEM((2,) + part, BF)], "iv" + "v" * (2 * len(grad_keys)),
    )


def encoder_grad_kernel(ids, w_ck, w_cv, *refs):
    grads, out, held = refs[:-2], refs[-2], refs[-1]
    count = len(grads) // 2
    key_count = grads[0].shape[0]
    for index, item in enumerate(grads):
        held[index] = item[...]

    def step(index, carry):
        rows = pl.ds(pl.multiple_of((ids[0] ^ index) * key_count, LANES), key_count)
        out[rows, :] = low(nt(held[index], w_ck[...]) + nt(held[count + index], w_cv[...]))
        return carry

    lax.fori_loop(0, count, step, 0)


def encoder_grad(call, w_ck, w_cv, grad_keys, grad_values):
    key_count, width = grad_keys[0].shape
    return call(
        encoder_grad_kernel, "encoder_grad", shape(key_count * len(grad_keys), width),
        (w_ck, w_cv) + tuple(grad_keys) + tuple(grad_values), 12 + 3 * len(grad_keys),
        [pltpu.VMEM((2 * len(grad_keys), key_count, width), BF)], "ivv" + "v" * (2 * len(grad_keys)),
    )


def key_sum_kernel(ids, keep, came, even, odd, held):
    chips, two = held.shape[0], held.shape[3]
    summed = low(keep[...].astype(F32) + came[...].astype(F32))
    for j in range(chips):
        held[j] = summed[:, :, j * two : (j + 1) * two]
    for by in range(chips):
        (even, odd)[by % 2][by // 2] = held[ids[1] ^ by]


def key_sum(call, keep, came, chips):
    ring, half, both = keep.shape
    part = (ring, half, both // chips)
    return call(
        key_sum_kernel, "key_sum", (shape(chips // 2, *part),) * 2, (keep, came), 20, [pltpu.VMEM((chips,) + part, BF)],
        "ivv",
    )


def first_sum_kernel(ids, keep, came, *outs):
    for by in range(keep.shape[0]):
        z = ids[0] ^ by
        outs[by % 2][by // 2] = low(keep[z].astype(F32) + came[z].astype(F32))


def first_sum(call, keep, came):
    part = (keep.shape[0] // 2,) + keep.shape[1:]
    return call(first_sum_kernel, "first_sum", (shape(*part),) * 2, (keep, came), 16, (), "ivv")


def hold_kernel(item, out):
    out[...] = item[...]


def hold(call, item):
    return call(hold_kernel, "hold", shape(*item.shape), (item,), 8, (), "v")


def pack_kernel(*refs):
    for at, item in enumerate(refs[:-1]):
        refs[-1][at] = item[...]


def pack(call, parts):
    return call(pack_kernel, "pack", shape(len(parts), *parts[0].shape), tuple(parts), 16, (), "v" * len(parts))


def add_halves_kernel(*refs, count, inner):
    keep, came, outs = refs[: 1 if inner else count], refs[1 if inner else count], refs[2 if inner else count + 1 :]
    for at in range(count):
        mine = keep[0][at] if inner else keep[at][...]
        outs[at % 2][at // 2] = low(mine.astype(F32) + came[at].astype(F32))


def add_halves(call, name, keep, came):
    inner = not isinstance(keep, (tuple, list))
    count = came.shape[0]
    part = (count // 2,) + came.shape[1:]
    args = (keep,) if inner else tuple(keep)
    return call(
        functools.partial(add_halves_kernel, count=count, inner=inner), name, (shape(*part),) * 2, args + (came,), 16, (),
        "v" * (len(args) + 1),
    )


def halve(call, name, axis, keep, give, by):
    came = swap(give, axis, by)
    if came.shape[0] == 1:
        return keep, came
    keep, give = add_halves(call, name, keep, came)
    return halve(call, name, axis, keep, give, 2 * by)


def tail_grads_kernel(ids, gain_cross, *refs, chips):
    early, middle, late = refs[:chips], refs[chips : 2 * chips], refs[2 * chips : 3 * chips]
    keep, give, held, chosen = refs[3 * chips :]
    _, ring, more, both = held.shape
    four = both // 3 * 2
    width = early[0].shape[1] // 3
    half = more - extra_rows(four, width)
    tokens = early[0].shape[0]
    every, rows = slice(None), slice(0, tokens)
    first = lax.div(ids[1] * 2, chips) == 0

    @pl.when(first)
    def _():
        chosen[...] = stacked(middle, every, slice(0, width))

    @pl.when(jnp.logical_not(first))
    def _():
        after_self = stacked(early, every, slice(2 * width, 3 * width)).astype(F32)
        chosen[...] = low(after_self * inverse_rms(after_self) * row(gain_cross))

    grads = (
        (low(tn(stacked(early, every, slice(0, width)), stacked(late, rows, slice(0, four)))), slice(0, four)),
        (low(tn(chosen[...], stacked(late, rows, slice(four, both)))), slice(four, both)),
    )
    gains = sum(gain_values(item[tokens:].astype(F32), four, width) for item in late)
    block = gain_block(gains, four, both)
    for z in range(ring):
        for c in range(2):
            at = (2 * z + c) * half
            for grad, lanes in grads:
                held[c, z, :half, lanes] = grad[at : at + half]
            held[c, z, half:, :] = block
    hand_out(ids, held, keep, give)


def tail_grads(call, gain_cross, early, middle, late, ring):
    chips = len(early)
    width = early[0].shape[1] // 3
    both = late[0].shape[1]
    part = (ring, width // (2 * ring) + extra_rows(both // 3 * 2, width), both)
    return call(
        functools.partial(tail_grads_kernel, chips=chips), "tail_grads", (shape(*part),) * 2,
        (gain_cross,) + tuple(early) + tuple(middle) + tuple(late), 28,
        [pltpu.VMEM((2,) + part, BF), pltpu.VMEM((chips * early[0].shape[0], width), BF)], "iv" + "v" * (3 * chips),
    )


def tail_sum_kernel(ids, keep, came, part, more, *outs, chips):
    both = keep.shape[2]
    four = both // 3 * 2
    width = four * chips // 4
    half = keep.shape[1] - extra_rows(four, width)
    gains = gain_values(keep[0, half:].astype(F32), four, width) + gain_values(came[0, half:].astype(F32), four, width)
    block = gain_block(gains, four, outs[0].shape[1])
    for by, out in enumerate(outs):
        z = ids[0] ^ by
        out[:half, :both] = low(keep[z, :half].astype(F32) + came[z, :half].astype(F32))
        out[:half, both:] = low(part[0, z].astype(F32) + more[0, z].astype(F32))
        out[half:] = block


def tail_sum(call, keep, came, parts, chips):
    ring, more, both = keep.shape
    return call(
        functools.partial(tail_sum_kernel, chips=chips), "tail_sum",
        (shape(more, both + parts[0].shape[3]),) * ring, (keep, came) + tuple(parts), 16, (), "ivvvv",
    )


def ring_sum_kernel(keep, came, out):
    out[...] = low(keep[0].astype(F32) + came[0].astype(F32))


def ring_sum(call, parts):
    return call(ring_sum_kernel, "ring_sum", shape(*parts[0].shape[1:]), tuple(parts), 16, (), "vv")


def last_sum_kernel(ids, *refs):
    parts, (out, *gain_outs, held) = refs[:-5], refs[-5:]
    half, both = out.shape
    ring, _, rows = held.shape
    four = both // 2
    out[...] = low(sum(item[:half].astype(F32) for item in parts))
    gains = sum(gain_values(item[half:].astype(F32), four, ring * rows) for item in parts)
    for z in range(ring):
        held[z] = gains[:, z * rows : (z + 1) * rows]
    for i, gain_out in enumerate(gain_outs):
        gain_out[...] = held[ids[0], i]


def last_sum(call, parts, rows):
    more, both = parts[0].shape
    half = rows // 2
    return call(
        last_sum_kernel, "last_sum", (shape(half, both),) + (shape32(rows),) * 3, tuple(parts), 16,
        [pltpu.VMEM((len(parts), 3, rows), F32)], "i" + "v" * len(parts),
    )


def place_pieces(ids, own, other, held):
    for by in range(own.shape[0]):
        held[ids[1] ^ by, ids[2]] = own[by]
        held[ids[1] ^ by, 1 - ids[2]] = other[by]


def first_out_kernel(ids, *refs, chips):
    own, other, in_out, out_out, held = refs
    place_pieces(ids, own, other, held)
    half, wide = held.shape[2:]
    span = wide // 2
    width = out_out.shape[1]
    few = half * span // width
    for j in range(chips):
        for c in range(2):
            rows = slice(c * half, (c + 1) * half)
            in_out[rows, j * span : (j + 1) * span] = held[j, c, :, :span].astype(F32)
            for v in range(width // span):
                at = (2 * j + c) * few
                out_out[at : at + few, v * span : (v + 1) * span] = held[
                    j, c, v * few : (v + 1) * few, span : 2 * span
                ].astype(F32)


def first_out(call, own, other, units, width):
    chips, half, wide = own.shape
    rows = 2 * half
    return call(
        functools.partial(first_out_kernel, chips=chips), "first_out",
        (shape32(rows, units), shape32(rows * units // width, width)),
        (own, other), 24, [pltpu.VMEM((chips, 2, half, wide), BF)], "ivv",
    )


def last_out_kernel(ids, *refs, chips):
    own, other, outs, held = refs[0], refs[1], refs[2:-1], refs[-1]
    place_pieces(ids, own, other, held)
    half, both = held.shape[2:]
    four, two = both // 2, both // 4
    for j in range(chips):
        for c in range(2):
            rows = slice(c * half, (c + 1) * half)
            at = j % (chips // 4) * four
            outs[j * 4 // chips][rows, at : at + four] = held[j, c, :, :four].astype(F32)
            at = j % (chips // 2) * two
            outs[4 + j * 2 // chips][rows, at : at + two] = held[j, c, :, four : four + two].astype(F32)
            outs[6 + j * 2 // chips][rows, at : at + two] = held[j, c, :, four + two :].astype(F32)


def last_out(call, own, other, width):
    chips, half, both = own.shape
    return call(
        functools.partial(last_out_kernel, chips=chips), "last_out", (shape32(2 * half, width),) * 8,
        (own, other), 24, [pltpu.VMEM((chips, 2, half, both), BF)], "ivv",
    )


def swap(values, axis, by):
    peers = lax.axis_size(axis)
    return lax.ppermute(values, axis, [(i, i ^ by) for i in range(peers)])


def over_chips(blocks):
    return [blocks[0]] + [swap(item, "pb", 2 * by) for by, item in enumerate(blocks) if by]


def over_ring(blocks):
    return [blocks[0]] + [swap(item, "pa", by) for by, item in enumerate(blocks) if by]


def over_core(blocks):
    return [swap(item, "pb", 1) for item in blocks]


def body(
    hidden, encoder, lengths, w_sq, w_sk, w_sv, w_so, w_cq, w_ck, w_cv, w_co, w_in, w_out,
    gain_self, gain_cross, gain_ffn, cotangent,
):
    _, tokens, width = hidden.shape
    questions, _, passage_len, _ = encoder.shape
    units = w_in.shape[1]
    ring = lax.axis_size("pa")
    chips = lax.axis_size("pb") // 2
    true_len = lengths.reshape(questions)
    hidden2 = hidden.reshape(tokens, width)
    cot = cotangent.reshape(tokens, width)
    enc = encoder.reshape(questions * passage_len, width)

    call = Line()
    x_self, self_q, self_k, self_v, self_mix, mixture, logs, after_self, x_cross, cross_q = self_forward(
        call, hidden2, gain_self, gain_cross, (w_sq, w_sk, w_sv, w_so, w_cq)
    )
    asked = over_ring([cross_q] * ring)
    keys, values = key_values(call, enc, w_ck, w_cv, passage_len)
    near = chips - 1
    partial = []
    for step in range(ring):
        last = step == ring - 1
        if step == 1:
            early = list(early_pack(call, x_self, self_mix, cot, after_self, chips))
        partial.append(
            cross_forward(call, true_len, asked[step], keys, values, step, (), 10 if last else None)
        )
    early[near] = hold(call, early[near])
    early = over_chips(early)
    packed = over_ring(partial)
    call.meet(0, packed[1 : ring - 1])
    call.meet(3)
    found = feed_forward(call, after_self, cot, gain_ffn, w_co, w_in, w_out, packed, chips)
    result, grad_after_cross, g_cross, sent, grad_gain_ffn = found[:5]
    given = over_ring([sent] * ring)
    middle = list(found[5:])
    call.meet(0, early[1:])
    back = {}
    for step in range(ring):
        back[step] = cross_backward(call, true_len, asked[step], given[step], keys, values, step)
        if step == min(0, ring - 1):
            middle[near] = hold(call, middle[near])
    middle = over_chips(middle)
    partial = over_ring([back[step][0] for step in range(ring)])
    grad_keys, grad_values = [back[step][1] for step in range(ring)], [back[step][2] for step in range(ring)]
    key_keep, key_give = key_grads(call, enc, grad_keys, grad_values, ring)
    grad_encoder = encoder_grad(call, w_ck, w_cv, grad_keys, grad_values)
    ffn_keep, ffn_give = ffn_grads(call, w_co, gain_ffn, early, middle, ring, units)
    call.meet(0, partial[2:])
    call.meet(20, ())
    key_parts = key_sum(call, key_keep, swap(key_give, "pb", 1), chips)
    first = first_sum(call, ffn_keep, swap(ffn_give, "pb", 1))
    found = self_backward(
        call,
        (grad_after_cross, after_self, hidden2, gain_self, gain_cross, grad_gain_ffn, g_cross,
         self_q, self_k, self_v, mixture, logs),
        (w_cq, w_so, w_sq, w_sk, w_sv),
        partial,
        chips,
    )
    grad_hidden = found[0]
    late = over_chips(found[1:])
    key_parts = halve(call, "key_add", "pb", *key_parts, 2)
    first = halve(call, "first_add", "pa", *first, 1)
    keep, give = tail_grads(call, gain_cross, early, middle, late, ring)
    call.meet(0, [key_parts[1], first[1]])
    call.meet(12)
    last = over_ring(tail_sum(call, keep, swap(give, "pb", 1), key_parts, chips))
    first = over_chips([ring_sum(call, first)] * chips)
    last, *gains = last_sum(call, last, width // ring)
    last = over_chips([last] * chips)
    first = pack(call, first)
    last = pack(call, last)
    grad_in, grad_out = first_out(call, first, swap(first, "pb", 1), units, width)
    grad_sq, grad_sk, grad_sv, grad_so, grad_co, grad_cq, grad_ck, grad_cv = last_out(
        call, last, swap(last, "pb", 1), width
    )
    return (
        result.reshape(hidden.shape),
        grad_hidden.reshape(hidden.shape),
        grad_encoder.reshape(encoder.shape),
        grad_sq,
        grad_sk,
        grad_sv,
        grad_so,
        grad_cq,
        grad_ck,
        grad_cv,
        grad_co,
        grad_in,
        grad_out,
        gains[0],
        gains[1],
        gains[2],
    )


def solution(mesh):
    split = P(("pb", "pa"), None, None)
    passages = P("pb", "pa", None, None)
    return jax.shard_map(
        body,
        mesh=mesh,
        in_specs=(split, passages, P("pb", "pa")) + (P(),) * 13 + (split,),
        out_specs=(split, split, passages) + (P("pa", None),) * 10 + (P("pa"),) * 3,
        check_vma=False,
    )
```

```python
import functools

import jax
import jax.numpy as jnp
from jax import lax
from jax.experimental import pallas as pl
from jax.experimental.pallas import tpu as pltpu
from jax.sharding import PartitionSpec as P

HEADS = 12
EPS = 1e-06
NEG = -1000000000.0
F32 = jnp.float32
BF = jnp.bfloat16
SLOTS = 4
LANES = 128
MIB = 1 << 20


def dot(left, right, left_dim, right_dim, precision=None):
    return lax.dot_general(
        left,
        right,
        (((left_dim,), (right_dim,)), ((), ())),
        precision=precision,
        preferred_element_type=F32,
    )


def nn(left, right):
    return dot(left, right, 1, 0)


def nt(left, right):
    return dot(left, right, 1, 1)


def tn(left, right):
    return dot(left, right, 0, 0)


def low(values):
    return values.astype(BF)


def inverse_rms(values):
    return lax.rsqrt(jnp.mean(values * values, axis=-1, keepdims=True) + EPS)


def norm_back(grad, values, gain):
    inv = inverse_rms(values)
    scaled = gain * grad
    inner = jnp.mean(values * scaled, axis=-1, keepdims=True)
    grad_values = inv * scaled - values * (inv * inv * inv * inner)
    grad_gain = jnp.sum(grad * values * inv, axis=0, keepdims=True)
    return grad_values, grad_gain


def lanes_of(shape):
    return lax.broadcasted_iota(jnp.int32, shape, len(shape) - 1)


def rows_of(shape):
    return lax.broadcasted_iota(jnp.int32, shape, len(shape) - 2)


def ones_where(condition):
    return jnp.where(condition, 1.0, 0.0).astype(BF)


def spread_matrix(width):
    slot, lane = rows_of((LANES, width)), lanes_of((LANES, width))
    return ones_where((slot // SLOTS == lane // (width // HEADS)) & (slot % SLOTS < 2))


def compact_matrix():
    slot, lane = rows_of((LANES, LANES)), lanes_of((LANES, LANES))
    return ones_where((slot // SLOTS == lane // SLOTS) & (slot % SLOTS < 2))


def gather_matrix(width):
    feature, lane = rows_of((width, LANES)), lanes_of((width, LANES))
    return ones_where(feature // (width // HEADS) == lane // SLOTS)


def split_three(values):
    first = low(values).astype(F32)
    rest = values - first
    second = low(rest).astype(F32)
    third = low(rest - second).astype(F32)
    return first, second, third


def in_slots(values, start=0):
    first, second, _ = split_three(values)
    slot = lanes_of(values.shape) % SLOTS - start
    return jnp.where(slot == 0, first, jnp.where(slot == 1, second, 0.0))


def to_rows(extra, width):
    turned = jnp.transpose(extra)
    few = HEADS * SLOTS * extra.shape[0] // width
    return jnp.concatenate([turned[at : at + few] for at in range(0, HEADS * SLOTS, few)], 1)


def from_rows(rows, tokens):
    few = rows.shape[0]
    parts = [rows[:, at : at + tokens].astype(F32) for at in range(0, rows.shape[1], tokens)]
    parts.append(jnp.zeros((LANES - few * len(parts), tokens), F32))
    return low(jnp.transpose(jnp.concatenate(parts, 0)))


def few_rows(tokens, width):
    return HEADS * SLOTS * tokens // width


def head_sums(values, matrix):
    first, second, third = split_three(values)
    return nn(low(first), matrix) + nn(low(second), matrix) + nn(low(third), matrix)


def two_heads(block):
    first = lanes_of(block.shape) < block.shape[1] // 2
    zero = jnp.zeros_like(block)
    return jnp.concatenate([jnp.where(first, block, zero), jnp.where(first, zero, block)], 0)


def fold_heads(block):
    half = block.shape[0] // 2
    lane = lanes_of((half, block.shape[1]))
    return jnp.where(lane < block.shape[1] // 2, block[:half], block[half:])


def pair_of_slots(extra, pair, start, more=None):
    lane = lanes_of(extra.shape)
    slot = lane % SLOTS
    wanted = (slot >= start) & (slot < start + 2)
    halves = [
        jnp.where(wanted & (lane // SLOTS == 2 * pair + i), extra, jnp.zeros_like(extra)) for i in range(2)
    ]
    block = jnp.concatenate(halves, 0)
    return block if more is None else block + more


def last_lane(rows, value):
    return jnp.where(lanes_of((rows, LANES)) == LANES - 1, value, 0.0).astype(BF)


def attend_pair(queries, keys, values, valid=None):
    scores = nt(keys, queries)
    if valid is not None:
        scores = jnp.where(valid, scores, NEG)
    top = jnp.max(scores, axis=0, keepdims=True)
    weights = low(jnp.exp(scores - top))
    both = tn(weights, values)
    split = both.shape[1] - LANES
    mixture = fold_heads(both[:, :split]) * (1.0 / fold_heads(both[:, split:]))
    return mixture, both[:, split:], top


def log_totals(sums, tops):
    tokens = tops[0].shape[1] // 2
    lane = lanes_of((tokens, LANES)) // SLOTS
    found = jnp.ones((tokens, LANES), F32)
    rows = []
    for pair, (both, top) in enumerate(zip(sums, tops)):
        found = jnp.where(lane == 2 * pair, both[:tokens], jnp.where(lane == 2 * pair + 1, both[tokens:], found))
        rows += [jnp.broadcast_to(top[:, :tokens], (SLOTS, tokens)), jnp.broadcast_to(top[:, tokens:], (SLOTS, tokens))]
    rows.append(jnp.zeros((LANES - HEADS * SLOTS, tokens), F32))
    return jnp.transpose(jnp.concatenate(rows, 0)) + jnp.log(found)


def attend_pair_back(queries, keys, values, grad_mix, query_more, key_more, grad_more, value_more, valid=None):
    scaled = two_heads(queries)
    grad_two = two_heads(grad_mix)
    scores = nt(jnp.concatenate([keys, key_more], 1), jnp.concatenate([scaled, query_more], 1))
    probs = jnp.exp(scores)
    if valid is not None:
        probs = jnp.where(valid, probs, 0.0)
    grad_probs = nt(jnp.concatenate([values, value_more], 1), jnp.concatenate([grad_two, grad_more], 1))
    grad_scores = low(probs * grad_probs)
    grad_values = nn(low(probs), grad_two)
    grad_keys = nn(grad_scores, scaled)
    grad_queries = fold_heads(tn(grad_scores, keys))
    return grad_queries, grad_keys, grad_values


def minus_slots(rows, start):
    slot = lanes_of((rows, LANES)) % SLOTS
    return jnp.where((slot >= start) & (slot < start + 2), -1.0, 0.0)


def causal_mask(tokens):
    key = rows_of((tokens, 2 * tokens))
    token = lanes_of((tokens, 2 * tokens))
    return key <= jnp.where(token >= tokens, token - tokens, token)


WEIGHTS = {
    "self_forward": 0,
    "key_values": 5,
    "cross_forward": 1,
    "feed_forward": 5,
    "cross_backward": 4,
    "key_grads": 2,
    "ffn_grads": 0,
    "first_sum": 0,
    "self_backward": 20,
    "early_pack": 0,
    "middle_pack": 0,
    "encoder_grad": 0,
    "ring_sum": 0,
    "tail_grads": 0,
    "tail_sum": 0,
    "first_out": 0,
    "last_sum": 0,
    "last_out": 0,
    "meet": 0,
    "pack": 0,
    "hold": 0,
    "key_sum": 0,
    "key_add": 0,
    "first_add": 0,
}


class Line:
    def __init__(self):
        self.token = None

    def __call__(self, kernel, name, outs, args, mib, scratch=(), places="", after=(), weight=None):
        kinds = {"s": pltpu.SMEM, "h": pltpu.HBM, "v": pltpu.VMEM}
        placed = places[:1] == "i"
        specs = [pl.BlockSpec(memory_space=kinds[letter]) for letter in places[placed:]]
        count = len(args)
        single = not isinstance(outs, (tuple, list))
        outs = ((outs,) if single else tuple(outs)) + (shape32(8, LANES),)
        given = (() if self.token is None else (self.token,)) + tuple(after)
        homes = [pltpu.HBM if name == "self_forward" else pltpu.VMEM] * (len(outs) - 1) + [pltpu.VMEM]

        def run(*refs):
            at = count + len(given)
            made = refs[at : at + len(outs)]
            made[-1][...] = jnp.zeros((8, LANES), F32)
            here = ()
            if placed:
                lane = lax.axis_index("pb").astype(jnp.int32)
                here = ((lax.axis_index("pa").astype(jnp.int32), lane >> 1, lane & 1),)
            kernel(*here, *refs[:count], *made[:-1], *refs[at + len(outs) :])

        found = pl.pallas_call(
            run,
            out_shape=outs,
            in_specs=specs + [pl.BlockSpec(memory_space=pl.ANY)] * len(given),
            out_specs=[pl.BlockSpec(memory_space=home) for home in homes],
            scratch_shapes=scratch,
            compiler_params=pltpu.CompilerParams(vmem_limit_bytes=mib * MIB),
            cost_estimate=pl.CostEstimate(flops=int(1153000000 * (WEIGHTS[name] if weight is None else weight)), bytes_accessed=0, transcendentals=0),
            name=name,
        )(*args, *given)
        self.token = found[-1]
        return found[0] if single else found[:-1]

    def meet(self, weight, after=()):
        self(lambda *refs: None, "meet", (), (), 4, (), "", after, weight)


def shape(*dims):
    return jax.ShapeDtypeStruct(dims, BF)


def shape32(*dims):
    return jax.ShapeDtypeStruct(dims, F32)


def row(gain):
    return gain[...].reshape(1, gain.shape[0])


def self_forward_kernel(*refs):
    far, outs, refs = refs[:8], refs[8:18], refs[18:]
    held, made, (sems, out_sems) = refs[:8], refs[8:18], refs[18:]
    copies = [pltpu.make_async_copy(item, near, sems.at[i]) for i, (item, near) in enumerate(zip(far, held))]
    for item in copies:
        item.start()
    hidden, gain_self, gain_cross = held[:3]
    weights = held[3:]
    (x_self_out, q_out, k_out, v_out, mix_out, mixture_out, logs_out, after_out, x_cross_out, cross_q_out) = made
    pending = []

    def send(index):
        pending.append(pltpu.make_async_copy(made[index], outs[index], out_sems.at[index]))
        pending[-1].start()

    tokens, width = hidden.shape
    factor = (width // HEADS) ** -0.5
    copies[0].wait()
    copies[1].wait()
    stream = hidden[...].astype(F32)
    x_self = low(stream * inverse_rms(stream) * row(gain_self))
    x_self_out[...] = x_self
    send(0)
    for i in range(3):
        copies[3 + i].wait()
        made[1 + i][...] = low(nn(x_self, weights[i][...]))
        send(1 + i)
    queries, keys, values = (made[1 + i][...] for i in range(3))
    valid = causal_mask(tokens)
    pair_width = 2 * width // HEADS
    ones = jnp.ones((tokens, LANES), BF)
    mixtures, sums, tops = [], [], []
    for pair in range(HEADS // 2):
        part = slice(pair * pair_width, (pair + 1) * pair_width)
        mixture, both, top = attend_pair(
            two_heads(queries[:, part] * factor), keys[:, part], jnp.concatenate([values[:, part], ones], 1), valid
        )
        mixtures.append(mixture)
        sums.append(both)
        tops.append(top)
    mixture = jnp.concatenate(mixtures, 1)
    mixture_out[...] = mixture
    send(5)
    mix = low(mixture)
    mix_out[...] = mix
    send(4)
    logs_out[...] = log_totals(sums, tops)
    send(6)
    copies[2].wait()
    copies[6].wait()
    after_self = stream + nn(mix, weights[3][...])
    after_out[...] = after_self
    send(7)
    x_cross = low(after_self * inverse_rms(after_self) * row(gain_cross))
    x_cross_out[...] = x_cross
    send(8)
    copies[7].wait()
    cross_q_out[...] = low(nn(x_cross, weights[4][...]))
    send(9)
    for item in pending:
        item.wait()


def self_forward(call, hidden, gain_self, gain_cross, weights):
    tokens, width = hidden.shape
    low_one = shape(tokens, width)
    args = (hidden, gain_self, gain_cross) + tuple(weights)
    outs = (low_one,) * 5 + (
        shape32(tokens, width), shape32(tokens, LANES), shape32(tokens, width), low_one, low_one,
    )
    return call(
        self_forward_kernel, "self_forward", outs, args, 56,
        [pltpu.VMEM(item.shape, item.dtype) for item in args + outs]
        + [pltpu.SemaphoreType.DMA((size,)) for size in (len(args), len(outs))],
        "h" * len(args),
    )


def early_pack_kernel(ids, x_self, mix, cot, after_self, *early):
    chips = len(early)
    width = cot.shape[1]
    for by, out in enumerate(early):
        out[:, width : 2 * width] = cot[...]
        out[:, 2 * width :] = low(after_self[...])
        last = lax.div((ids[1] ^ by) * 4, chips) == 3

        @pl.when(last)
        def _():
            out[:, :width] = mix[...]

        @pl.when(jnp.logical_not(last))
        def _():
            out[:, :width] = x_self[...]


def early_pack(call, x_self, mix, cot, after_self, chips):
    tokens, width = cot.shape
    return call(
        early_pack_kernel, "early_pack", (shape(tokens, 3 * width),) * chips, (x_self, mix, cot, after_self), 12, (), "ivvvv"
    )


def key_values_kernel(encoder, w_ck, w_cv, keys, values, *, block):
    def step(index, carry):
        rows = pl.ds(pl.multiple_of(index * block, block), block)
        here = encoder[rows, :]
        keys[rows, :] = low(nn(here, w_ck[...]))
        values[rows, :] = low(nn(here, w_cv[...]))
        return carry

    lax.fori_loop(0, encoder.shape[0] // block, step, 0)


def key_values(call, encoder, w_ck, w_cv, block):
    return call(
        functools.partial(key_values_kernel, block=block), "key_values", (shape(*encoder.shape), shape(*encoder.shape)), (encoder, w_ck, w_cv), 24, (), "vvv"
    )


def key_rows(ids, count, step):
    key_count = count
    return pl.ds(pl.multiple_of((ids[0] ^ step) * key_count, LANES), key_count)


def cross_forward_kernel(ids, lengths, keys, values, queries, out, *, step, key_count):
    tokens, width = queries.shape
    factor = (width // HEADS) ** -0.5
    rows = key_rows(ids, key_count, step)
    size = (key_count, LANES)
    hidden_key = jnp.where(rows_of(size) < lengths[ids[0] ^ step], 0.0, NEG)
    key_more = jnp.where(lanes_of(size) == LANES - 1, hidden_key, 0.0).astype(BF)
    query_more = last_lane(2 * tokens, 1.0)
    ones = jnp.ones(size, BF)
    pair_width = 2 * width // HEADS
    sums, tops = [], []
    for pair in range(HEADS // 2):
        part = slice(pair * pair_width, (pair + 1) * pair_width)
        mixture, both, top = attend_pair(
            jnp.concatenate([two_heads(queries[:, part] * factor), query_more], 1),
            jnp.concatenate([keys[rows, part], key_more], 1),
            jnp.concatenate([values[rows, part], ones], 1),
        )
        out[:tokens, part] = low(mixture)
        sums.append(both)
        tops.append(top)
    out[tokens:] = low(to_rows(in_slots(log_totals(sums, tops)), width))


def cross_forward(call, lengths, queries, keys, values, step, after=(), weight=None):
    tokens, width = queries.shape
    key_count = keys.shape[0] // lengths.shape[0]
    return call(
        functools.partial(cross_forward_kernel, step=step, key_count=key_count),
        "cross_forward", shape(tokens + few_rows(tokens, width), width), (lengths, keys, values, queries), 16, (), "isvvv",
        after, weight,
    )


def feed_forward_kernel(
    after_self, cotangent, gain_ffn, w_co, w_in, w_out, *refs, count, chunks
):
    packed, refs = refs[:count], refs[count:]
    result_out, grad_after_out, g_cross_out, send_out, grad_gain_out, mix_out, act_held, grad_held = refs
    tokens, width = after_self.shape
    units = w_in.shape[1]
    wide = units // chunks
    compact, spread = compact_matrix(), spread_matrix(width)
    logs = [nn(from_rows(part[tokens:], tokens), compact) for part in packed]
    top = functools.reduce(jnp.maximum, logs)
    log_total = top + jnp.log(sum(jnp.exp(item - top) for item in logs))
    mixture = sum(
        nn(low(in_slots(jnp.exp(item - log_total))), spread) * part[:tokens].astype(F32)
        for item, part in zip(logs, packed)
    )
    mix = low(mixture)
    mix_out[...] = mix
    after_cross = after_self[...] + nn(mix, w_co[...])
    x_ffn = low(after_cross * inverse_rms(after_cross) * row(gain_ffn))
    grad_low = cotangent[...]
    slope = (2.0 / 3.141592653589793) ** 0.5

    def step(chunk, carry):
        part = pl.ds(pl.multiple_of(chunk * wide, LANES), wide)
        pre = nn(x_ffn, w_in[:, part])
        square = pre * pre
        bent = jnp.tanh(pre * (slope + (0.044715 * slope) * square))
        act_held[:, part] = low(0.5 * pre * (1.0 + bent))
        grad_act = nt(grad_low, w_out[part, :])
        bend = 0.5 * (1.0 + bent) + 0.5 * pre * (1.0 - bent * bent) * (slope + (3 * 0.044715 * slope) * square)
        grad_held[:, part] = low(grad_act * bend)
        return carry

    lax.fori_loop(0, chunks, step, 0, unroll=True)
    result = after_cross + nn(act_held[...], w_out[...])
    grad_x = nt(grad_held[...], w_in[...])
    result_out[...] = low(result)
    grad_values, grad_gain = norm_back(grad_x, after_cross, row(gain_ffn))
    grad_gain_out[...] = grad_gain
    grad_after = grad_low.astype(F32) + grad_values
    grad_after_out[...] = grad_after
    g_cross = low(grad_after)
    g_cross_out[...] = g_cross
    grad_mix = low(nt(g_cross, w_co[...]))
    delta = head_sums(grad_mix.astype(F32) * mixture, gather_matrix(width))
    send_out[:tokens] = grad_mix
    send_out[tokens:] = low(to_rows(in_slots(log_total) + in_slots(delta, 2), width))


def middle_pack_kernel(ids, mix, act, grad_pre, *refs, count):
    middle, acts, grad_pres = refs[:-2], refs[-2], refs[-1]
    chips, _, span = acts.shape
    width = mix.shape[1]
    units = act.shape[1]
    piece = units // (count * chips)
    for which in range(units // piece):
        slot = which // chips * piece
        acts[which % chips, :, slot : slot + piece] = act[:, which * piece : (which + 1) * piece]
    for which in range(chips):
        grad_pres[which] = grad_pre[:, which * span : (which + 1) * span]
    for by, out in enumerate(middle):
        index = ids[1] ^ by
        out[:, :width] = mix[...]
        out[:, width : width + span] = acts[index]
        out[:, width + span :] = grad_pres[index]


def middle_pack(call, mix, act, grad_pre, count, chips):
    tokens, width = mix.shape
    span = act.shape[1] // chips
    return call(
        functools.partial(middle_pack_kernel, count=count), "middle_pack", (shape(tokens, width + 2 * span),) * chips,
        (mix, act, grad_pre), 16, [pltpu.VMEM((chips, tokens, span), BF)] * 2, "ivvv",
    )


def feed_forward(call, after_self, cotangent, gain_ffn, w_co, w_in, w_out, packed):
    tokens, width = after_self.shape
    units = w_in.shape[1]
    return call(
        functools.partial(feed_forward_kernel, count=len(packed), chunks=4),
        "feed_forward",
        (shape(tokens, width), shape32(tokens, width), shape(tokens, width),
         shape(tokens + few_rows(tokens, width), width), shape32(1, width), shape(tokens, width),
         shape(tokens, units), shape(tokens, units)),
        (after_self, cotangent, gain_ffn, w_co, w_in, w_out) + tuple(packed),
        28,
        (),
        "vvvvvv" + "v" * len(packed),
    )


def cross_backward_kernel(ids, lengths, keys, values, queries, grads, grad_queries, grad_keys, grad_values, *, step):
    tokens, width = queries.shape
    key_count = grad_keys.shape[0]
    factor = (width // HEADS) ** -0.5
    rows = key_rows(ids, key_count, step)
    size = (key_count, LANES)
    hidden_key = jnp.where(rows_of(size) < lengths[ids[0] ^ step], 0.0, NEG)
    key_more = jnp.where(lanes_of(size) == LANES - 1, hidden_key, minus_slots(key_count, 0)).astype(BF)
    value_more = minus_slots(key_count, 2).astype(BF)
    extra = from_rows(grads[tokens:], tokens)
    one = last_lane(2 * tokens, 1.0)
    pair_width = 2 * width // HEADS
    for pair in range(HEADS // 2):
        part = slice(pair * pair_width, (pair + 1) * pair_width)
        grad_q, grad_k, grad_v = attend_pair_back(
            queries[:, part] * factor, keys[rows, part], values[rows, part], grads[:tokens, part],
            pair_of_slots(extra, pair, 0, one), key_more, pair_of_slots(extra, pair, 2), value_more,
        )
        grad_queries[:, part] = low(grad_q * factor)
        grad_keys[:, part] = low(grad_k)
        grad_values[:, part] = low(grad_v)


def cross_backward(call, lengths, queries, grads, keys, values, step):
    tokens, width = queries.shape
    key_count = keys.shape[0] // lengths.shape[0]
    return call(
        functools.partial(cross_backward_kernel, step=step),
        "cross_backward",
        (shape(tokens, width), shape(key_count, width), shape(key_count, width)),
        (lengths, keys, values, queries, grads), 20, (), "isvvvv",
    )


def extra_rows(four, width):
    return -(-6 * width // four // 8) * 8


def gain_block(gains, four, width_out):
    count = gains.shape[1] // four
    few = extra_rows(four, gains.shape[1])
    high = low(gains).astype(F32)
    rows = [part[i : i + 1, v * four : (v + 1) * four] for part in (high, gains - high) for i in range(3) for v in range(count)]
    block = jnp.concatenate(rows + [jnp.zeros((few - len(rows), four), F32)], 0)
    return low(jnp.concatenate([block, jnp.zeros((few, width_out - four), F32)], 1))


def gain_values(block, four, width):
    count = width // four
    rows = []
    for i in range(3):
        pieces = [
            block[i * count + v : i * count + v + 1, :four] + block[(3 + i) * count + v : (3 + i) * count + v + 1, :four]
            for v in range(count)
        ]
        rows.append(jnp.concatenate(pieces, 1))
    return jnp.concatenate(rows, 0)


def self_backward_kernel(
    ids, grad_after_cross, after_self, hidden, gain_self, gain_cross, grad_gain_ffn, g_cross,
    self_q, self_k, self_v, mixture, logs, *refs, count, chips
):
    weights, partial, refs = refs[:5], refs[5 : 5 + count], refs[5 + count :]
    hidden_out, late = refs[0], refs[1 : 1 + chips]
    fours, twos = refs[1 + chips :]
    tokens, width = after_self.shape
    factor = (width // HEADS) ** -0.5
    four, two = 4 * width // chips, 2 * width // chips
    grad_cq = low(sum(item[...].astype(F32) for item in partial))
    grad_values, grad_gain_cross = norm_back(nt(grad_cq, weights[0][...]), after_self[...], row(gain_cross))
    grad_after = grad_after_cross[...] + grad_values
    g_self = low(grad_after)
    grad_mix = low(nt(g_self, weights[1][...]))
    delta = head_sums(grad_mix.astype(F32) * mixture[...], gather_matrix(width))
    extra = low(in_slots(logs[...]) + in_slots(delta, 2))
    valid = causal_mask(tokens)
    key_more = minus_slots(tokens, 0).astype(BF)
    value_more = minus_slots(tokens, 2).astype(BF)
    pair_width = 2 * width // HEADS
    found = []
    for pair in range(HEADS // 2):
        part = slice(pair * pair_width, (pair + 1) * pair_width)
        grad_q, grad_k, grad_v = attend_pair_back(
            self_q[:, part] * factor, self_k[:, part], self_v[:, part], grad_mix[:, part],
            pair_of_slots(extra, pair, 0), key_more, pair_of_slots(extra, pair, 2), value_more, valid,
        )
        found.append((low(grad_q * factor), low(grad_k), low(grad_v)))
    grads = [jnp.concatenate([item[i] for item in found], 1) for i in range(3)]
    grad_x = jnp.zeros((tokens, width), F32)
    for i in range(3):
        grad_x = grad_x + nt(grads[i], weights[2 + i][...])
    grad_values, grad_gain_self = norm_back(grad_x, hidden[...].astype(F32), row(gain_self))
    hidden_out[...] = low(grad_after + grad_values)
    gains = jnp.concatenate([grad_gain_self, grad_gain_cross, grad_gain_ffn[...]], 0)
    block = gain_block(gains, four, four + two)
    for i, item in enumerate(grads + [g_self]):
        for v in range(width // four):
            fours[i * (width // four) + v] = item[:, v * four : (v + 1) * four]
    for i, item in enumerate((g_cross[...], grad_cq)):
        for v in range(width // two):
            twos[i * (width // two) + v] = item[:, v * two : (v + 1) * two]
    chip = ids[1]
    for by, out in enumerate(late):
        out[:tokens, :four] = fours[chip ^ by]
        out[:tokens, four:] = twos[chip ^ by]
        out[tokens:] = block


def self_backward(call, first, weights, partial, chips):
    tokens, width = first[1].shape
    four, two = 4 * width // chips, 2 * width // chips
    return call(
        functools.partial(self_backward_kernel, count=len(partial), chips=chips),
        "self_backward",
        (shape(tokens, width),) + (shape(tokens + extra_rows(four, width), four + two),) * chips,
        tuple(first) + tuple(weights) + tuple(partial),
        20,
        [pltpu.VMEM((chips, tokens, four), BF), pltpu.VMEM((chips, tokens, two), BF)],
        "i" + "v" * (len(first) + 5 + len(partial)),
    )


def stacked(refs, rows, lanes):
    return jnp.concatenate([item[rows, lanes] for item in refs], 0)


def hand_out(ids, held, keep, give):
    core = ids[2]
    keep[...] = held[core]
    give[...] = held[1 - core]


def ffn_grads_kernel(ids, w_co, gain_ffn, *refs, chips):
    early, middle, (keep, give, held) = refs[:chips], refs[chips : 2 * chips], refs[2 * chips :]
    _, ring, half, both = held.shape
    span = both // 2
    width = early[0].shape[1] // 3
    every = slice(None)
    mix = stacked(middle, every, slice(0, width))
    after_cross = stacked(early, every, slice(2 * width, 3 * width)).astype(F32) + nn(mix, w_co[...])
    x_ffn = low(after_cross * inverse_rms(after_cross) * row(gain_ffn))
    grad_in = low(tn(x_ffn, stacked(middle, every, slice(width + span, width + 2 * span))))
    for z in range(ring):
        for c in range(2):
            at = (2 * z + c) * half
            held[c, z, :, :span] = grad_in[at : at + half]
    grad_out = low(
        tn(stacked(middle, every, slice(width, width + span)), stacked(early, every, slice(width, 2 * width)))
    )
    few = span // (2 * ring)
    for z in range(ring):
        for c in range(2):
            at = (2 * z + c) * few
            block = grad_out[at : at + few]
            held[c, z, :, span:] = jnp.concatenate([block[:, v : v + span] for v in range(0, width, span)], 0)
    hand_out(ids, held, keep, give)


def ffn_grads(call, w_co, gain_ffn, early, middle, ring, units):
    chips = len(early)
    width = early[0].shape[1] // 3
    part = (ring, width // (2 * ring), 2 * units // chips)
    return call(
        functools.partial(ffn_grads_kernel, chips=chips), "ffn_grads", (shape(*part),) * 2,
        (w_co, gain_ffn) + tuple(early) + tuple(middle), 28, [pltpu.VMEM((2,) + part, BF)], "ivv" + "v" * (2 * chips),
    )


def key_grads_kernel(ids, encoder, *refs):
    grads, (keep, give, held) = refs[:-3], refs[-3:]
    count = len(grads) // 2
    _, ring, half, both = held.shape
    width = both // 2
    key_count = grads[0].shape[0]
    rows = jnp.concatenate([encoder[key_rows(ids, key_count, step), :] for step in range(count)], 0)
    for i in range(2):
        grad = low(tn(rows, stacked(grads[i * count : (i + 1) * count], slice(None), slice(None))))
        for z in range(ring):
            for c in range(2):
                at = (2 * z + c) * half
                held[c, z, :, i * width : (i + 1) * width] = grad[at : at + half]
    hand_out(ids, held, keep, give)


def key_grads(call, encoder, grad_keys, grad_values, ring):
    width = encoder.shape[1]
    part = (ring, width // (2 * ring), 2 * width)
    return call(
        key_grads_kernel, "key_grads", (shape(*part),) * 2, (encoder,) + tuple(grad_keys) + tuple(grad_values), 32,
        [pltpu.VMEM((2,) + part, BF)], "iv" + "v" * (2 * len(grad_keys)),
    )


def encoder_grad_kernel(ids, w_ck, w_cv, *refs):
    grads, out, held = refs[:-2], refs[-2], refs[-1]
    count = len(grads) // 2
    key_count = grads[0].shape[0]
    for index, item in enumerate(grads):
        held[index] = item[...]

    def step(index, carry):
        rows = pl.ds(pl.multiple_of((ids[0] ^ index) * key_count, LANES), key_count)
        out[rows, :] = low(nt(held[index], w_ck[...]) + nt(held[count + index], w_cv[...]))
        return carry

    lax.fori_loop(0, count, step, 0)


def encoder_grad(call, w_ck, w_cv, grad_keys, grad_values):
    key_count, width = grad_keys[0].shape
    return call(
        encoder_grad_kernel, "encoder_grad", shape(key_count * len(grad_keys), width),
        (w_ck, w_cv) + tuple(grad_keys) + tuple(grad_values), 12 + 3 * len(grad_keys),
        [pltpu.VMEM((2 * len(grad_keys), key_count, width), BF)], "ivv" + "v" * (2 * len(grad_keys)),
    )


def key_sum_kernel(ids, keep, came, even, odd, held):
    chips, two = held.shape[0], held.shape[3]
    summed = low(keep[...].astype(F32) + came[...].astype(F32))
    for j in range(chips):
        held[j] = summed[:, :, j * two : (j + 1) * two]
    for by in range(chips):
        (even, odd)[by % 2][by // 2] = held[ids[1] ^ by]


def key_sum(call, keep, came, chips):
    ring, half, both = keep.shape
    part = (ring, half, both // chips)
    return call(
        key_sum_kernel, "key_sum", (shape(chips // 2, *part),) * 2, (keep, came), 20, [pltpu.VMEM((chips,) + part, BF)],
        "ivv",
    )


def first_sum_kernel(ids, keep, came, *outs):
    for by in range(keep.shape[0]):
        z = ids[0] ^ by
        outs[by % 2][by // 2] = low(keep[z].astype(F32) + came[z].astype(F32))


def first_sum(call, keep, came):
    part = (keep.shape[0] // 2,) + keep.shape[1:]
    return call(first_sum_kernel, "first_sum", (shape(*part),) * 2, (keep, came), 16, (), "ivv")


def hold_kernel(item, out):
    out[...] = item[...]


def hold(call, item):
    return call(hold_kernel, "hold", shape(*item.shape), (item,), 8, (), "v")


def pack_kernel(*refs):
    for at, item in enumerate(refs[:-1]):
        refs[-1][at] = item[...]


def pack(call, parts):
    return call(pack_kernel, "pack", shape(len(parts), *parts[0].shape), tuple(parts), 16, (), "v" * len(parts))


def add_halves_kernel(*refs, count, inner):
    keep, came, outs = refs[: 1 if inner else count], refs[1 if inner else count], refs[2 if inner else count + 1 :]
    for at in range(count):
        mine = keep[0][at] if inner else keep[at][...]
        outs[at % 2][at // 2] = low(mine.astype(F32) + came[at].astype(F32))


def add_halves(call, name, keep, came):
    inner = not isinstance(keep, (tuple, list))
    count = came.shape[0]
    part = (count // 2,) + came.shape[1:]
    args = (keep,) if inner else tuple(keep)
    return call(
        functools.partial(add_halves_kernel, count=count, inner=inner), name, (shape(*part),) * 2, args + (came,), 16, (),
        "v" * (len(args) + 1),
    )


def halve(call, name, axis, keep, give, by):
    came = swap(give, axis, by)
    if came.shape[0] == 1:
        return keep, came
    keep, give = add_halves(call, name, keep, came)
    return halve(call, name, axis, keep, give, 2 * by)


def tail_grads_kernel(ids, gain_cross, *refs, chips):
    early, middle, late = refs[:chips], refs[chips : 2 * chips], refs[2 * chips : 3 * chips]
    keep, give, held, chosen = refs[3 * chips :]
    _, ring, more, both = held.shape
    four = both // 3 * 2
    width = early[0].shape[1] // 3
    half = more - extra_rows(four, width)
    tokens = early[0].shape[0]
    every, rows = slice(None), slice(0, tokens)
    first = lax.div(ids[1] * 2, chips) == 0

    @pl.when(first)
    def _():
        chosen[...] = stacked(middle, every, slice(0, width))

    @pl.when(jnp.logical_not(first))
    def _():
        after_self = stacked(early, every, slice(2 * width, 3 * width)).astype(F32)
        chosen[...] = low(after_self * inverse_rms(after_self) * row(gain_cross))

    grads = (
        (low(tn(stacked(early, every, slice(0, width)), stacked(late, rows, slice(0, four)))), slice(0, four)),
        (low(tn(chosen[...], stacked(late, rows, slice(four, both)))), slice(four, both)),
    )
    gains = sum(gain_values(item[tokens:].astype(F32), four, width) for item in late)
    block = gain_block(gains, four, both)
    for z in range(ring):
        for c in range(2):
            at = (2 * z + c) * half
            for grad, lanes in grads:
                held[c, z, :half, lanes] = grad[at : at + half]
            held[c, z, half:, :] = block
    hand_out(ids, held, keep, give)


def tail_grads(call, gain_cross, early, middle, late, ring):
    chips = len(early)
    width = early[0].shape[1] // 3
    both = late[0].shape[1]
    part = (ring, width // (2 * ring) + extra_rows(both // 3 * 2, width), both)
    return call(
        functools.partial(tail_grads_kernel, chips=chips), "tail_grads", (shape(*part),) * 2,
        (gain_cross,) + tuple(early) + tuple(middle) + tuple(late), 28,
        [pltpu.VMEM((2,) + part, BF), pltpu.VMEM((chips * early[0].shape[0], width), BF)], "iv" + "v" * (3 * chips),
    )


def tail_sum_kernel(ids, keep, came, part, more, *outs, chips):
    both = keep.shape[2]
    four = both // 3 * 2
    width = four * chips // 4
    half = keep.shape[1] - extra_rows(four, width)
    gains = gain_values(keep[0, half:].astype(F32), four, width) + gain_values(came[0, half:].astype(F32), four, width)
    block = gain_block(gains, four, outs[0].shape[1])
    for by, out in enumerate(outs):
        z = ids[0] ^ by
        out[:half, :both] = low(keep[z, :half].astype(F32) + came[z, :half].astype(F32))
        out[:half, both:] = low(part[0, z].astype(F32) + more[0, z].astype(F32))
        out[half:] = block


def tail_sum(call, keep, came, parts, chips):
    ring, more, both = keep.shape
    return call(
        functools.partial(tail_sum_kernel, chips=chips), "tail_sum",
        (shape(more, both + parts[0].shape[3]),) * ring, (keep, came) + tuple(parts), 16, (), "ivvvv",
    )


def ring_sum_kernel(keep, came, out):
    out[...] = low(keep[0].astype(F32) + came[0].astype(F32))


def ring_sum(call, parts):
    return call(ring_sum_kernel, "ring_sum", shape(*parts[0].shape[1:]), tuple(parts), 16, (), "vv")


def last_sum_kernel(ids, *refs):
    parts, (out, *gain_outs, held) = refs[:-5], refs[-5:]
    half, both = out.shape
    ring, _, rows = held.shape
    four = both // 2
    out[...] = low(sum(item[:half].astype(F32) for item in parts))
    gains = sum(gain_values(item[half:].astype(F32), four, ring * rows) for item in parts)
    for z in range(ring):
        held[z] = gains[:, z * rows : (z + 1) * rows]
    for i, gain_out in enumerate(gain_outs):
        gain_out[...] = held[ids[0], i]


def last_sum(call, parts, rows):
    more, both = parts[0].shape
    half = rows // 2
    return call(
        last_sum_kernel, "last_sum", (shape(half, both),) + (shape32(rows),) * 3, tuple(parts), 16,
        [pltpu.VMEM((len(parts), 3, rows), F32)], "i" + "v" * len(parts),
    )


def place_pieces(ids, own, other, held):
    for by in range(own.shape[0]):
        held[ids[1] ^ by, ids[2]] = own[by]
        held[ids[1] ^ by, 1 - ids[2]] = other[by]


def first_out_kernel(ids, *refs, chips):
    own, other, in_out, out_out, held = refs
    place_pieces(ids, own, other, held)
    half, wide = held.shape[2:]
    span = wide // 2
    width = out_out.shape[1]
    few = half * span // width
    for j in range(chips):
        for c in range(2):
            rows = slice(c * half, (c + 1) * half)
            in_out[rows, j * span : (j + 1) * span] = held[j, c, :, :span].astype(F32)
            for v in range(width // span):
                at = (2 * j + c) * few
                out_out[at : at + few, v * span : (v + 1) * span] = held[
                    j, c, v * few : (v + 1) * few, span : 2 * span
                ].astype(F32)


def first_out(call, own, other, units, width):
    chips, half, wide = own.shape
    rows = 2 * half
    return call(
        functools.partial(first_out_kernel, chips=chips), "first_out",
        (shape32(rows, units), shape32(rows * units // width, width)),
        (own, other), 24, [pltpu.VMEM((chips, 2, half, wide), BF)], "ivv",
    )


def last_out_kernel(ids, *refs, chips):
    own, other, outs, held = refs[0], refs[1], refs[2:-1], refs[-1]
    place_pieces(ids, own, other, held)
    half, both = held.shape[2:]
    four, two = both // 2, both // 4
    for j in range(chips):
        for c in range(2):
            rows = slice(c * half, (c + 1) * half)
            at = j % (chips // 4) * four
            outs[j * 4 // chips][rows, at : at + four] = held[j, c, :, :four].astype(F32)
            at = j % (chips // 2) * two
            outs[4 + j * 2 // chips][rows, at : at + two] = held[j, c, :, four : four + two].astype(F32)
            outs[6 + j * 2 // chips][rows, at : at + two] = held[j, c, :, four + two :].astype(F32)


def last_out(call, own, other, width):
    chips, half, both = own.shape
    return call(
        functools.partial(last_out_kernel, chips=chips), "last_out", (shape32(2 * half, width),) * 8,
        (own, other), 24, [pltpu.VMEM((chips, 2, half, both), BF)], "ivv",
    )


def swap(values, axis, by):
    peers = lax.axis_size(axis)
    return lax.ppermute(values, axis, [(i, i ^ by) for i in range(peers)])


def over_chips(blocks):
    return [blocks[0]] + [swap(item, "pb", 2 * by) for by, item in enumerate(blocks) if by]


def over_ring(blocks):
    return [blocks[0]] + [swap(item, "pa", by) for by, item in enumerate(blocks) if by]


def over_core(blocks):
    return [swap(item, "pb", 1) for item in blocks]


def body(
    hidden, encoder, lengths, w_sq, w_sk, w_sv, w_so, w_cq, w_ck, w_cv, w_co, w_in, w_out,
    gain_self, gain_cross, gain_ffn, cotangent,
):
    _, tokens, width = hidden.shape
    questions, _, passage_len, _ = encoder.shape
    units = w_in.shape[1]
    ring = lax.axis_size("pa")
    chips = lax.axis_size("pb") // 2
    true_len = lengths.reshape(questions)
    hidden2 = hidden.reshape(tokens, width)
    cot = cotangent.reshape(tokens, width)
    enc = encoder.reshape(questions * passage_len, width)

    call = Line()
    x_self, self_q, self_k, self_v, self_mix, mixture, logs, after_self, x_cross, cross_q = self_forward(
        call, hidden2, gain_self, gain_cross, (w_sq, w_sk, w_sv, w_so, w_cq)
    )
    asked = over_ring([cross_q] * ring)
    keys, values = key_values(call, enc, w_ck, w_cv, passage_len)
    near = chips - 1
    partial = []
    for step in range(ring):
        last = step == ring - 1
        if step == 1:
            early = list(early_pack(call, x_self, self_mix, cot, after_self, chips))
        partial.append(
            cross_forward(call, true_len, asked[step], keys, values, step, (), 10 if last else None)
        )
    early[near] = hold(call, early[near])
    early = over_chips(early)
    packed = over_ring(partial)
    call.meet(0, packed[1 : ring - 1])
    call.meet(3)
    found = feed_forward(call, after_self, cot, gain_ffn, w_co, w_in, w_out, packed)
    result, grad_after_cross, g_cross, sent, grad_gain_ffn, cross_mix, activated, grad_pre = found
    given = over_ring([sent] * ring)
    middle = list(middle_pack(call, cross_mix, activated, grad_pre, ring, chips))
    call.meet(0, early[1:])
    back = {}
    for step in range(ring):
        back[step] = cross_backward(call, true_len, asked[step], given[step], keys, values, step)
        if step == min(0, ring - 1):
            middle[near] = hold(call, middle[near])
    middle = over_chips(middle)
    partial = over_ring([back[step][0] for step in range(ring)])
    grad_keys, grad_values = [back[step][1] for step in range(ring)], [back[step][2] for step in range(ring)]
    key_keep, key_give = key_grads(call, enc, grad_keys, grad_values, ring)
    ffn_keep, ffn_give = ffn_grads(call, w_co, gain_ffn, early, middle, ring, units)
    call.meet(0, partial[2:])
    call.meet(20, ())
    key_parts = key_sum(call, key_keep, swap(key_give, "pb", 1), chips)
    first = first_sum(call, ffn_keep, swap(ffn_give, "pb", 1))
    found = self_backward(
        call,
        (grad_after_cross, after_self, hidden2, gain_self, gain_cross, grad_gain_ffn, g_cross,
         self_q, self_k, self_v, mixture, logs),
        (w_cq, w_so, w_sq, w_sk, w_sv),
        partial,
        chips,
    )
    grad_hidden = found[0]
    late = over_chips(found[1:])
    key_parts = halve(call, "key_add", "pb", *key_parts, 2)
    first = halve(call, "first_add", "pa", *first, 1)
    grad_encoder = encoder_grad(call, w_ck, w_cv, grad_keys, grad_values)
    call.meet(1, late[3:])
    keep, give = tail_grads(call, gain_cross, early, middle, late, ring)
    call.meet(0, [key_parts[1], first[1]])
    call.meet(12)
    last = over_ring(tail_sum(call, keep, swap(give, "pb", 1), key_parts, chips))
    first = over_chips([ring_sum(call, first)] * chips)
    call.meet(1, last[2:])
    last, *gains = last_sum(call, last, width // ring)
    last = over_chips([last] * chips)
    first = pack(call, first)
    last = pack(call, last)
    grad_in, grad_out = first_out(call, first, swap(first, "pb", 1), units, width)
    grad_sq, grad_sk, grad_sv, grad_so, grad_co, grad_cq, grad_ck, grad_cv = last_out(
        call, last, swap(last, "pb", 1), width
    )
    return (
        result.reshape(hidden.shape),
        grad_hidden.reshape(hidden.shape),
        grad_encoder.reshape(encoder.shape),
        grad_sq,
        grad_sk,
        grad_sv,
        grad_so,
        grad_cq,
        grad_ck,
        grad_cv,
        grad_co,
        grad_in,
        grad_out,
        gains[0],
        gains[1],
        gains[2],
    )


def solution(mesh):
    split = P(("pb", "pa"), None, None)
    passages = P("pb", "pa", None, None)
    return jax.shard_map(
        body,
        mesh=mesh,
        in_specs=(split, passages, P("pb", "pa")) + (P(),) * 13 + (split,),
        out_specs=(split, split, passages) + (P("pa", None),) * 10 + (P("pa"),) * 3,
        check_vma=False,
    )
```

```python
import functools

import jax
import jax.numpy as jnp
from jax import lax
from jax.experimental import pallas as pl
from jax.experimental.pallas import tpu as pltpu
from jax.sharding import PartitionSpec as P

HEADS = 12
EPS = 1e-06
NEG = -1000000000.0
F32 = jnp.float32
BF = jnp.bfloat16
SLOTS = 4
LANES = 128
MIB = 1 << 20


def dot(left, right, left_dim, right_dim, precision=None):
    return lax.dot_general(
        left,
        right,
        (((left_dim,), (right_dim,)), ((), ())),
        precision=precision,
        preferred_element_type=F32,
    )


def nn(left, right):
    return dot(left, right, 1, 0)


def nt(left, right):
    return dot(left, right, 1, 1)


def tn(left, right):
    return dot(left, right, 0, 0)


def low(values):
    return values.astype(BF)


def inverse_rms(values):
    return lax.rsqrt(jnp.mean(values * values, axis=-1, keepdims=True) + EPS)


def norm_back(grad, values, gain):
    inv = inverse_rms(values)
    scaled = gain * grad
    inner = jnp.mean(values * scaled, axis=-1, keepdims=True)
    grad_values = inv * scaled - values * (inv * inv * inv * inner)
    grad_gain = jnp.sum(grad * values * inv, axis=0, keepdims=True)
    return grad_values, grad_gain


def lanes_of(shape):
    return lax.broadcasted_iota(jnp.int32, shape, len(shape) - 1)


def rows_of(shape):
    return lax.broadcasted_iota(jnp.int32, shape, len(shape) - 2)


def ones_where(condition):
    return jnp.where(condition, 1.0, 0.0).astype(BF)


def spread_matrix(width):
    slot, lane = rows_of((LANES, width)), lanes_of((LANES, width))
    return ones_where((slot // SLOTS == lane // (width // HEADS)) & (slot % SLOTS < 2))


def compact_matrix():
    slot, lane = rows_of((LANES, LANES)), lanes_of((LANES, LANES))
    return ones_where((slot // SLOTS == lane // SLOTS) & (slot % SLOTS < 2))


def gather_matrix(width):
    feature, lane = rows_of((width, LANES)), lanes_of((width, LANES))
    return ones_where(feature // (width // HEADS) == lane // SLOTS)


def split_three(values):
    first = low(values).astype(F32)
    rest = values - first
    second = low(rest).astype(F32)
    third = low(rest - second).astype(F32)
    return first, second, third


def in_slots(values, start=0):
    first, second, _ = split_three(values)
    slot = lanes_of(values.shape) % SLOTS - start
    return jnp.where(slot == 0, first, jnp.where(slot == 1, second, 0.0))


def to_rows(extra, width):
    turned = jnp.transpose(extra)
    few = HEADS * SLOTS * extra.shape[0] // width
    return jnp.concatenate([turned[at : at + few] for at in range(0, HEADS * SLOTS, few)], 1)


def from_rows(rows, tokens):
    few = rows.shape[0]
    parts = [rows[:, at : at + tokens].astype(F32) for at in range(0, rows.shape[1], tokens)]
    parts.append(jnp.zeros((LANES - few * len(parts), tokens), F32))
    return low(jnp.transpose(jnp.concatenate(parts, 0)))


def few_rows(tokens, width):
    return HEADS * SLOTS * tokens // width


def head_sums(values, matrix):
    first, second, third = split_three(values)
    return nn(low(first), matrix) + nn(low(second), matrix) + nn(low(third), matrix)


def two_heads(block):
    first = lanes_of(block.shape) < block.shape[1] // 2
    zero = jnp.zeros_like(block)
    return jnp.concatenate([jnp.where(first, block, zero), jnp.where(first, zero, block)], 0)


def fold_heads(block):
    half = block.shape[0] // 2
    lane = lanes_of((half, block.shape[1]))
    return jnp.where(lane < block.shape[1] // 2, block[:half], block[half:])


def pair_of_slots(extra, pair, start, more=None):
    lane = lanes_of(extra.shape)
    slot = lane % SLOTS
    wanted = (slot >= start) & (slot < start + 2)
    halves = [
        jnp.where(wanted & (lane // SLOTS == 2 * pair + i), extra, jnp.zeros_like(extra)) for i in range(2)
    ]
    block = jnp.concatenate(halves, 0)
    return block if more is None else block + more


def last_lane(rows, value):
    return jnp.where(lanes_of((rows, LANES)) == LANES - 1, value, 0.0).astype(BF)


def attend_pair(queries, keys, values, valid=None):
    scores = nt(keys, queries)
    if valid is not None:
        scores = jnp.where(valid, scores, NEG)
    top = jnp.max(scores, axis=0, keepdims=True)
    weights = low(jnp.exp(scores - top))
    both = tn(weights, values)
    split = both.shape[1] - LANES
    mixture = fold_heads(both[:, :split]) * (1.0 / fold_heads(both[:, split:]))
    return mixture, both[:, split:], top


def log_totals(sums, tops):
    tokens = tops[0].shape[1] // 2
    lane = lanes_of((tokens, LANES)) // SLOTS
    found = jnp.ones((tokens, LANES), F32)
    rows = []
    for pair, (both, top) in enumerate(zip(sums, tops)):
        found = jnp.where(lane == 2 * pair, both[:tokens], jnp.where(lane == 2 * pair + 1, both[tokens:], found))
        rows += [jnp.broadcast_to(top[:, :tokens], (SLOTS, tokens)), jnp.broadcast_to(top[:, tokens:], (SLOTS, tokens))]
    rows.append(jnp.zeros((LANES - HEADS * SLOTS, tokens), F32))
    return jnp.transpose(jnp.concatenate(rows, 0)) + jnp.log(found)


def attend_pair_back(queries, keys, values, grad_mix, query_more, key_more, grad_more, value_more, valid=None):
    scaled = two_heads(queries)
    grad_two = two_heads(grad_mix)
    scores = nt(jnp.concatenate([keys, key_more], 1), jnp.concatenate([scaled, query_more], 1))
    probs = jnp.exp(scores)
    if valid is not None:
        probs = jnp.where(valid, probs, 0.0)
    grad_probs = nt(jnp.concatenate([values, value_more], 1), jnp.concatenate([grad_two, grad_more], 1))
    grad_scores = low(probs * grad_probs)
    grad_values = nn(low(probs), grad_two)
    grad_keys = nn(grad_scores, scaled)
    grad_queries = fold_heads(tn(grad_scores, keys))
    return grad_queries, grad_keys, grad_values


def minus_slots(rows, start):
    slot = lanes_of((rows, LANES)) % SLOTS
    return jnp.where((slot >= start) & (slot < start + 2), -1.0, 0.0)


def causal_mask(tokens):
    key = rows_of((tokens, 2 * tokens))
    token = lanes_of((tokens, 2 * tokens))
    return key <= jnp.where(token >= tokens, token - tokens, token)


WEIGHTS = {
    "self_forward": 0,
    "key_values": 5,
    "cross_forward": 1,
    "feed_forward": 5,
    "cross_backward": 4,
    "key_grads": 1,
    "ffn_grads": 0,
    "first_sum": 0,
    "self_backward": 20,
    "early_pack": 0,
    "middle_pack": 0,
    "encoder_grad": 0,
    "ring_sum": 0,
    "tail_grads": 0,
    "tail_sum": 0,
    "first_out": 0,
    "last_sum": 0,
    "last_out": 0,
    "meet": 0,
    "pack": 0,
    "hold": 0,
    "key_sum": 0,
    "key_add": 0,
    "first_add": 0,
}


class Line:
    def __init__(self):
        self.token = None

    def __call__(self, kernel, name, outs, args, mib, scratch=(), places="", after=(), weight=None):
        kinds = {"s": pltpu.SMEM, "h": pltpu.HBM, "v": pltpu.VMEM}
        placed = places[:1] == "i"
        specs = [pl.BlockSpec(memory_space=kinds[letter]) for letter in places[placed:]]
        count = len(args)
        single = not isinstance(outs, (tuple, list))
        outs = ((outs,) if single else tuple(outs)) + (shape32(8, LANES),)
        given = (() if self.token is None else (self.token,)) + tuple(after)
        homes = [pltpu.HBM if name == "self_forward" else pltpu.VMEM] * (len(outs) - 1) + [pltpu.VMEM]

        def run(*refs):
            at = count + len(given)
            made = refs[at : at + len(outs)]
            made[-1][...] = jnp.zeros((8, LANES), F32)
            here = ()
            if placed:
                lane = lax.axis_index("pb").astype(jnp.int32)
                here = ((lax.axis_index("pa").astype(jnp.int32), lane >> 1, lane & 1),)
            kernel(*here, *refs[:count], *made[:-1], *refs[at + len(outs) :])

        found = pl.pallas_call(
            run,
            out_shape=outs,
            in_specs=specs + [pl.BlockSpec(memory_space=pl.ANY)] * len(given),
            out_specs=[pl.BlockSpec(memory_space=home) for home in homes],
            scratch_shapes=scratch,
            compiler_params=pltpu.CompilerParams(vmem_limit_bytes=mib * MIB),
            cost_estimate=pl.CostEstimate(flops=int(1153000000 * (WEIGHTS[name] if weight is None else weight)), bytes_accessed=0, transcendentals=0),
            name=name,
        )(*args, *given)
        self.token = found[-1]
        return found[0] if single else found[:-1]

    def meet(self, weight, after=()):
        self(lambda *refs: None, "meet", (), (), 4, (), "", after, weight)


def shape(*dims):
    return jax.ShapeDtypeStruct(dims, BF)


def shape32(*dims):
    return jax.ShapeDtypeStruct(dims, F32)


def row(gain):
    return gain[...].reshape(1, gain.shape[0])


def self_forward_kernel(*refs):
    far, outs, refs = refs[:8], refs[8:18], refs[18:]
    held, made, (sems, out_sems) = refs[:8], refs[8:18], refs[18:]
    copies = [pltpu.make_async_copy(item, near, sems.at[i]) for i, (item, near) in enumerate(zip(far, held))]
    for item in copies:
        item.start()
    hidden, gain_self, gain_cross = held[:3]
    weights = held[3:]
    (x_self_out, q_out, k_out, v_out, mix_out, mixture_out, logs_out, after_out, x_cross_out, cross_q_out) = made
    pending = []

    def send(index):
        pending.append(pltpu.make_async_copy(made[index], outs[index], out_sems.at[index]))
        pending[-1].start()

    tokens, width = hidden.shape
    factor = (width // HEADS) ** -0.5
    copies[0].wait()
    copies[1].wait()
    stream = hidden[...].astype(F32)
    x_self = low(stream * inverse_rms(stream) * row(gain_self))
    x_self_out[...] = x_self
    send(0)
    for i in range(3):
        copies[3 + i].wait()
        made[1 + i][...] = low(nn(x_self, weights[i][...]))
        send(1 + i)
    queries, keys, values = (made[1 + i][...] for i in range(3))
    valid = causal_mask(tokens)
    pair_width = 2 * width // HEADS
    ones = jnp.ones((tokens, LANES), BF)
    mixtures, sums, tops = [], [], []
    for pair in range(HEADS // 2):
        part = slice(pair * pair_width, (pair + 1) * pair_width)
        mixture, both, top = attend_pair(
            two_heads(queries[:, part] * factor), keys[:, part], jnp.concatenate([values[:, part], ones], 1), valid
        )
        mixtures.append(mixture)
        sums.append(both)
        tops.append(top)
    mixture = jnp.concatenate(mixtures, 1)
    mixture_out[...] = mixture
    send(5)
    mix = low(mixture)
    mix_out[...] = mix
    send(4)
    logs_out[...] = log_totals(sums, tops)
    send(6)
    copies[2].wait()
    copies[6].wait()
    after_self = stream + nn(mix, weights[3][...])
    after_out[...] = after_self
    send(7)
    x_cross = low(after_self * inverse_rms(after_self) * row(gain_cross))
    x_cross_out[...] = x_cross
    send(8)
    copies[7].wait()
    cross_q_out[...] = low(nn(x_cross, weights[4][...]))
    send(9)
    for item in pending:
        item.wait()


def self_forward(call, hidden, gain_self, gain_cross, weights):
    tokens, width = hidden.shape
    low_one = shape(tokens, width)
    args = (hidden, gain_self, gain_cross) + tuple(weights)
    outs = (low_one,) * 5 + (
        shape32(tokens, width), shape32(tokens, LANES), shape32(tokens, width), low_one, low_one,
    )
    return call(
        self_forward_kernel, "self_forward", outs, args, 56,
        [pltpu.VMEM(item.shape, item.dtype) for item in args + outs]
        + [pltpu.SemaphoreType.DMA((size,)) for size in (len(args), len(outs))],
        "h" * len(args),
    )


def early_pack_kernel(ids, x_self, mix, cot, after_self, *early):
    chips = len(early)
    width = cot.shape[1]
    for by, out in enumerate(early):
        out[:, width : 2 * width] = cot[...]
        out[:, 2 * width :] = low(after_self[...])
        last = lax.div((ids[1] ^ by) * 4, chips) == 3

        @pl.when(last)
        def _():
            out[:, :width] = mix[...]

        @pl.when(jnp.logical_not(last))
        def _():
            out[:, :width] = x_self[...]


def early_pack(call, x_self, mix, cot, after_self, chips):
    tokens, width = cot.shape
    return call(
        early_pack_kernel, "early_pack", (shape(tokens, 3 * width),) * chips, (x_self, mix, cot, after_self), 12, (), "ivvvv"
    )


def key_values_kernel(encoder, w_ck, w_cv, keys, values, *, block):
    def step(index, carry):
        rows = pl.ds(pl.multiple_of(index * block, block), block)
        here = encoder[rows, :]
        keys[rows, :] = low(nn(here, w_ck[...]))
        values[rows, :] = low(nn(here, w_cv[...]))
        return carry

    lax.fori_loop(0, encoder.shape[0] // block, step, 0)


def key_values(call, encoder, w_ck, w_cv, block):
    return call(
        functools.partial(key_values_kernel, block=block), "key_values", (shape(*encoder.shape), shape(*encoder.shape)), (encoder, w_ck, w_cv), 24, (), "vvv"
    )


def key_rows(ids, count, step):
    key_count = count
    return pl.ds(pl.multiple_of((ids[0] ^ step) * key_count, LANES), key_count)


def cross_forward_kernel(ids, lengths, keys, values, queries, out, *, step, key_count):
    tokens, width = queries.shape
    factor = (width // HEADS) ** -0.5
    rows = key_rows(ids, key_count, step)
    size = (key_count, LANES)
    hidden_key = jnp.where(rows_of(size) < lengths[ids[0] ^ step], 0.0, NEG)
    key_more = jnp.where(lanes_of(size) == LANES - 1, hidden_key, 0.0).astype(BF)
    query_more = last_lane(2 * tokens, 1.0)
    ones = jnp.ones(size, BF)
    pair_width = 2 * width // HEADS
    sums, tops = [], []
    for pair in range(HEADS // 2):
        part = slice(pair * pair_width, (pair + 1) * pair_width)
        mixture, both, top = attend_pair(
            jnp.concatenate([two_heads(queries[:, part] * factor), query_more], 1),
            jnp.concatenate([keys[rows, part], key_more], 1),
            jnp.concatenate([values[rows, part], ones], 1),
        )
        out[:tokens, part] = low(mixture)
        sums.append(both)
        tops.append(top)
    out[tokens:] = low(to_rows(in_slots(log_totals(sums, tops)), width))


def cross_forward(call, lengths, queries, keys, values, step, after=(), weight=None):
    tokens, width = queries.shape
    key_count = keys.shape[0] // lengths.shape[0]
    return call(
        functools.partial(cross_forward_kernel, step=step, key_count=key_count),
        "cross_forward", shape(tokens + few_rows(tokens, width), width), (lengths, keys, values, queries), 16, (), "isvvv",
        after, weight,
    )


def feed_forward_kernel(
    after_self, cotangent, gain_ffn, w_co, w_in, w_out, *refs, count, chunks
):
    packed, refs = refs[:count], refs[count:]
    result_out, grad_after_out, g_cross_out, send_out, grad_gain_out, mix_out, act_held, grad_held = refs
    tokens, width = after_self.shape
    units = w_in.shape[1]
    wide = units // chunks
    compact, spread = compact_matrix(), spread_matrix(width)
    logs = [nn(from_rows(part[tokens:], tokens), compact) for part in packed]
    top = functools.reduce(jnp.maximum, logs)
    log_total = top + jnp.log(sum(jnp.exp(item - top) for item in logs))
    mixture = sum(
        nn(low(in_slots(jnp.exp(item - log_total))), spread) * part[:tokens].astype(F32)
        for item, part in zip(logs, packed)
    )
    mix = low(mixture)
    mix_out[...] = mix
    after_cross = after_self[...] + nn(mix, w_co[...])
    x_ffn = low(after_cross * inverse_rms(after_cross) * row(gain_ffn))
    grad_low = cotangent[...]
    slope = (2.0 / 3.141592653589793) ** 0.5

    def step(chunk, carry):
        part = pl.ds(pl.multiple_of(chunk * wide, LANES), wide)
        pre = nn(x_ffn, w_in[:, part])
        square = pre * pre
        bent = jnp.tanh(pre * (slope + (0.044715 * slope) * square))
        act_held[:, part] = low(0.5 * pre * (1.0 + bent))
        grad_act = nt(grad_low, w_out[part, :])
        bend = 0.5 * (1.0 + bent) + 0.5 * pre * (1.0 - bent * bent) * (slope + (3 * 0.044715 * slope) * square)
        grad_held[:, part] = low(grad_act * bend)
        return carry

    lax.fori_loop(0, chunks, step, 0, unroll=True)
    result = after_cross + nn(act_held[...], w_out[...])
    grad_x = nt(grad_held[...], w_in[...])
    result_out[...] = low(result)
    grad_values, grad_gain = norm_back(grad_x, after_cross, row(gain_ffn))
    grad_gain_out[...] = grad_gain
    grad_after = grad_low.astype(F32) + grad_values
    grad_after_out[...] = grad_after
    g_cross = low(grad_after)
    g_cross_out[...] = g_cross
    grad_mix = low(nt(g_cross, w_co[...]))
    delta = head_sums(grad_mix.astype(F32) * mixture, gather_matrix(width))
    send_out[:tokens] = grad_mix
    send_out[tokens:] = low(to_rows(in_slots(log_total) + in_slots(delta, 2), width))


def middle_pack_kernel(ids, mix, act, grad_pre, *refs, count):
    middle, acts, grad_pres = refs[:-2], refs[-2], refs[-1]
    chips, _, span = acts.shape
    width = mix.shape[1]
    units = act.shape[1]
    piece = units // (count * chips)
    for which in range(units // piece):
        slot = which // chips * piece
        acts[which % chips, :, slot : slot + piece] = act[:, which * piece : (which + 1) * piece]
    for which in range(chips):
        grad_pres[which] = grad_pre[:, which * span : (which + 1) * span]
    for by, out in enumerate(middle):
        index = ids[1] ^ by
        out[:, :width] = mix[...]
        out[:, width : width + span] = acts[index]
        out[:, width + span :] = grad_pres[index]


def middle_pack(call, mix, act, grad_pre, count, chips):
    tokens, width = mix.shape
    span = act.shape[1] // chips
    return call(
        functools.partial(middle_pack_kernel, count=count), "middle_pack", (shape(tokens, width + 2 * span),) * chips,
        (mix, act, grad_pre), 16, [pltpu.VMEM((chips, tokens, span), BF)] * 2, "ivvv",
    )


def feed_forward(call, after_self, cotangent, gain_ffn, w_co, w_in, w_out, packed):
    tokens, width = after_self.shape
    units = w_in.shape[1]
    return call(
        functools.partial(feed_forward_kernel, count=len(packed), chunks=4),
        "feed_forward",
        (shape(tokens, width), shape32(tokens, width), shape(tokens, width),
         shape(tokens + few_rows(tokens, width), width), shape32(1, width), shape(tokens, width),
         shape(tokens, units), shape(tokens, units)),
        (after_self, cotangent, gain_ffn, w_co, w_in, w_out) + tuple(packed),
        28,
        (),
        "vvvvvv" + "v" * len(packed),
    )


def cross_backward_kernel(ids, lengths, keys, values, queries, grads, grad_queries, grad_keys, grad_values, *, step):
    tokens, width = queries.shape
    key_count = grad_keys.shape[0]
    factor = (width // HEADS) ** -0.5
    rows = key_rows(ids, key_count, step)
    size = (key_count, LANES)
    hidden_key = jnp.where(rows_of(size) < lengths[ids[0] ^ step], 0.0, NEG)
    key_more = jnp.where(lanes_of(size) == LANES - 1, hidden_key, minus_slots(key_count, 0)).astype(BF)
    value_more = minus_slots(key_count, 2).astype(BF)
    extra = from_rows(grads[tokens:], tokens)
    one = last_lane(2 * tokens, 1.0)
    pair_width = 2 * width // HEADS
    for pair in range(HEADS // 2):
        part = slice(pair * pair_width, (pair + 1) * pair_width)
        grad_q, grad_k, grad_v = attend_pair_back(
            queries[:, part] * factor, keys[rows, part], values[rows, part], grads[:tokens, part],
            pair_of_slots(extra, pair, 0, one), key_more, pair_of_slots(extra, pair, 2), value_more,
        )
        grad_queries[:, part] = low(grad_q * factor)
        grad_keys[:, part] = low(grad_k)
        grad_values[:, part] = low(grad_v)


def cross_backward(call, lengths, queries, grads, keys, values, step):
    tokens, width = queries.shape
    key_count = keys.shape[0] // lengths.shape[0]
    return call(
        functools.partial(cross_backward_kernel, step=step),
        "cross_backward",
        (shape(tokens, width), shape(key_count, width), shape(key_count, width)),
        (lengths, keys, values, queries, grads), 20, (), "isvvvv",
    )


def extra_rows(four, width):
    return -(-6 * width // four // 8) * 8


def gain_block(gains, four, width_out):
    count = gains.shape[1] // four
    few = extra_rows(four, gains.shape[1])
    high = low(gains).astype(F32)
    rows = [part[i : i + 1, v * four : (v + 1) * four] for part in (high, gains - high) for i in range(3) for v in range(count)]
    block = jnp.concatenate(rows + [jnp.zeros((few - len(rows), four), F32)], 0)
    return low(jnp.concatenate([block, jnp.zeros((few, width_out - four), F32)], 1))


def gain_values(block, four, width):
    count = width // four
    rows = []
    for i in range(3):
        pieces = [
            block[i * count + v : i * count + v + 1, :four] + block[(3 + i) * count + v : (3 + i) * count + v + 1, :four]
            for v in range(count)
        ]
        rows.append(jnp.concatenate(pieces, 1))
    return jnp.concatenate(rows, 0)


def self_backward_kernel(
    ids, grad_after_cross, after_self, hidden, gain_self, gain_cross, grad_gain_ffn, g_cross,
    self_q, self_k, self_v, mixture, logs, *refs, count, chips
):
    weights, partial, refs = refs[:5], refs[5 : 5 + count], refs[5 + count :]
    hidden_out, late = refs[0], refs[1 : 1 + chips]
    fours, twos = refs[1 + chips :]
    tokens, width = after_self.shape
    factor = (width // HEADS) ** -0.5
    four, two = 4 * width // chips, 2 * width // chips
    grad_cq = low(sum(item[...].astype(F32) for item in partial))
    grad_values, grad_gain_cross = norm_back(nt(grad_cq, weights[0][...]), after_self[...], row(gain_cross))
    grad_after = grad_after_cross[...] + grad_values
    g_self = low(grad_after)
    grad_mix = low(nt(g_self, weights[1][...]))
    delta = head_sums(grad_mix.astype(F32) * mixture[...], gather_matrix(width))
    extra = low(in_slots(logs[...]) + in_slots(delta, 2))
    valid = causal_mask(tokens)
    key_more = minus_slots(tokens, 0).astype(BF)
    value_more = minus_slots(tokens, 2).astype(BF)
    pair_width = 2 * width // HEADS
    found = []
    for pair in range(HEADS // 2):
        part = slice(pair * pair_width, (pair + 1) * pair_width)
        grad_q, grad_k, grad_v = attend_pair_back(
            self_q[:, part] * factor, self_k[:, part], self_v[:, part], grad_mix[:, part],
            pair_of_slots(extra, pair, 0), key_more, pair_of_slots(extra, pair, 2), value_more, valid,
        )
        found.append((low(grad_q * factor), low(grad_k), low(grad_v)))
    grads = [jnp.concatenate([item[i] for item in found], 1) for i in range(3)]
    grad_x = jnp.zeros((tokens, width), F32)
    for i in range(3):
        grad_x = grad_x + nt(grads[i], weights[2 + i][...])
    grad_values, grad_gain_self = norm_back(grad_x, hidden[...].astype(F32), row(gain_self))
    hidden_out[...] = low(grad_after + grad_values)
    gains = jnp.concatenate([grad_gain_self, grad_gain_cross, grad_gain_ffn[...]], 0)
    block = gain_block(gains, four, four + two)
    for i, item in enumerate(grads + [g_self]):
        for v in range(width // four):
            fours[i * (width // four) + v] = item[:, v * four : (v + 1) * four]
    for i, item in enumerate((g_cross[...], grad_cq)):
        for v in range(width // two):
            twos[i * (width // two) + v] = item[:, v * two : (v + 1) * two]
    chip = ids[1]
    for by, out in enumerate(late):
        out[:tokens, :four] = fours[chip ^ by]
        out[:tokens, four:] = twos[chip ^ by]
        out[tokens:] = block


def self_backward(call, first, weights, partial, chips):
    tokens, width = first[1].shape
    four, two = 4 * width // chips, 2 * width // chips
    return call(
        functools.partial(self_backward_kernel, count=len(partial), chips=chips),
        "self_backward",
        (shape(tokens, width),) + (shape(tokens + extra_rows(four, width), four + two),) * chips,
        tuple(first) + tuple(weights) + tuple(partial),
        20,
        [pltpu.VMEM((chips, tokens, four), BF), pltpu.VMEM((chips, tokens, two), BF)],
        "i" + "v" * (len(first) + 5 + len(partial)),
    )


def stacked(refs, rows, lanes):
    return jnp.concatenate([item[rows, lanes] for item in refs], 0)


def hand_out(ids, held, keep, give):
    core = ids[2]
    keep[...] = held[core]
    give[...] = held[1 - core]


def ffn_grads_kernel(ids, w_co, gain_ffn, *refs, chips):
    early, middle, (keep, give, held) = refs[:chips], refs[chips : 2 * chips], refs[-3:]
    _, ring, half, both = held.shape
    span = both // 2
    width = early[0].shape[1] // 3
    every = slice(None)
    mix = stacked(middle, every, slice(0, width))
    after_cross = stacked(early, every, slice(2 * width, 3 * width)).astype(F32) + nn(mix, w_co[...])
    x_ffn = low(after_cross * inverse_rms(after_cross) * row(gain_ffn))
    grad_in = low(tn(x_ffn, stacked(middle, every, slice(width + span, width + 2 * span))))
    for z in range(ring):
        for c in range(2):
            at = (2 * z + c) * half
            held[c, z, :, :span] = grad_in[at : at + half]
    grad_out = low(
        tn(stacked(middle, every, slice(width, width + span)), stacked(early, every, slice(width, 2 * width)))
    )
    few = span // (2 * ring)
    for z in range(ring):
        for c in range(2):
            at = (2 * z + c) * few
            block = grad_out[at : at + few]
            held[c, z, :, span:] = jnp.concatenate([block[:, v : v + span] for v in range(0, width, span)], 0)
    hand_out(ids, held, keep, give)


def ffn_grads(call, w_co, gain_ffn, early, middle, ring, units, more):
    chips = len(early)
    width = early[0].shape[1] // 3
    part = (ring, width // (2 * ring), 2 * units // chips)
    return call(
        functools.partial(ffn_grads_kernel, chips=chips), "ffn_grads", (shape(*part),) * 2,
        (w_co, gain_ffn) + tuple(early) + tuple(middle) + tuple(more), 28, [pltpu.VMEM((2,) + part, BF)],
        "ivv" + "v" * (2 * chips + len(more)),
    )


def key_grads_kernel(ids, encoder, *refs):
    grads, (keep, give, held) = refs[:-3], refs[-3:]
    count = len(grads) // 2
    _, ring, half, both = held.shape
    width = both // 2
    key_count = grads[0].shape[0]
    rows = jnp.concatenate([encoder[key_rows(ids, key_count, step), :] for step in range(count)], 0)
    for i in range(2):
        grad = low(tn(rows, stacked(grads[i * count : (i + 1) * count], slice(None), slice(None))))
        for z in range(ring):
            for c in range(2):
                at = (2 * z + c) * half
                held[c, z, :, i * width : (i + 1) * width] = grad[at : at + half]
    hand_out(ids, held, keep, give)


def key_grads(call, encoder, grad_keys, grad_values, ring):
    width = encoder.shape[1]
    part = (ring, width // (2 * ring), 2 * width)
    return call(
        key_grads_kernel, "key_grads", (shape(*part),) * 2, (encoder,) + tuple(grad_keys) + tuple(grad_values), 32,
        [pltpu.VMEM((2,) + part, BF)], "iv" + "v" * (2 * len(grad_keys)),
    )


def encoder_grad_kernel(ids, w_ck, w_cv, *refs):
    grads, out, held = refs[:-2], refs[-2], refs[-1]
    count = len(grads) // 2
    key_count = grads[0].shape[0]
    for index, item in enumerate(grads):
        held[index] = item[...]

    def step(index, carry):
        rows = pl.ds(pl.multiple_of((ids[0] ^ index) * key_count, LANES), key_count)
        out[rows, :] = low(nt(held[index], w_ck[...]) + nt(held[count + index], w_cv[...]))
        return carry

    lax.fori_loop(0, count, step, 0)


def encoder_grad(call, w_ck, w_cv, grad_keys, grad_values):
    key_count, width = grad_keys[0].shape
    return call(
        encoder_grad_kernel, "encoder_grad", shape(key_count * len(grad_keys), width),
        (w_ck, w_cv) + tuple(grad_keys) + tuple(grad_values), 12 + 3 * len(grad_keys),
        [pltpu.VMEM((2 * len(grad_keys), key_count, width), BF)], "ivv" + "v" * (2 * len(grad_keys)),
    )


def key_sum_kernel(ids, keep, came, even, odd, held):
    chips, two = held.shape[0], held.shape[3]
    summed = low(keep[...].astype(F32) + came[...].astype(F32))
    for j in range(chips):
        held[j] = summed[:, :, j * two : (j + 1) * two]
    for by in range(chips):
        (even, odd)[by % 2][by // 2] = held[ids[1] ^ by]


def key_sum(call, keep, came, chips):
    ring, half, both = keep.shape
    part = (ring, half, both // chips)
    return call(
        key_sum_kernel, "key_sum", (shape(chips // 2, *part),) * 2, (keep, came), 20, [pltpu.VMEM((chips,) + part, BF)],
        "ivv",
    )


def first_sum_kernel(ids, keep, came, *outs):
    for by in range(keep.shape[0]):
        z = ids[0] ^ by
        outs[by % 2][by // 2] = low(keep[z].astype(F32) + came[z].astype(F32))


def first_sum(call, keep, came):
    part = (keep.shape[0] // 2,) + keep.shape[1:]
    return call(first_sum_kernel, "first_sum", (shape(*part),) * 2, (keep, came), 16, (), "ivv")


def hold_kernel(item, *refs):
    refs[-1][...] = item[...]


def hold(call, item, near=()):
    return call(hold_kernel, "hold", shape(*item.shape), (item, *near), 24, (), "v" * (1 + len(near)))


def pack_kernel(*refs):
    for at, item in enumerate(refs[:-1]):
        refs[-1][at] = item[...]


def pack(call, parts):
    return call(pack_kernel, "pack", shape(len(parts), *parts[0].shape), tuple(parts), 16, (), "v" * len(parts))


def add_halves_kernel(*refs, count, inner):
    keep, came, outs = refs[: 1 if inner else count], refs[1 if inner else count], refs[2 if inner else count + 1 :]
    for at in range(count):
        mine = keep[0][at] if inner else keep[at][...]
        outs[at % 2][at // 2] = low(mine.astype(F32) + came[at].astype(F32))


def add_halves(call, name, keep, came):
    inner = not isinstance(keep, (tuple, list))
    count = came.shape[0]
    part = (count // 2,) + came.shape[1:]
    args = (keep,) if inner else tuple(keep)
    return call(
        functools.partial(add_halves_kernel, count=count, inner=inner), name, (shape(*part),) * 2, args + (came,), 16, (),
        "v" * (len(args) + 1),
    )


def halve(call, name, axis, keep, give, by):
    came = swap(give, axis, by)
    if came.shape[0] == 1:
        return keep, came
    keep, give = add_halves(call, name, keep, came)
    return halve(call, name, axis, keep, give, 2 * by)


def tail_grads_kernel(ids, gain_cross, *refs, chips):
    early, middle, late = refs[:chips], refs[chips : 2 * chips], refs[2 * chips : 3 * chips]
    keep, give, held, chosen = refs[3 * chips :]
    _, ring, more, both = held.shape
    four = both // 3 * 2
    width = early[0].shape[1] // 3
    half = more - extra_rows(four, width)
    tokens = early[0].shape[0]
    every, rows = slice(None), slice(0, tokens)
    first = lax.div(ids[1] * 2, chips) == 0

    @pl.when(first)
    def _():
        chosen[...] = stacked(middle, every, slice(0, width))

    @pl.when(jnp.logical_not(first))
    def _():
        after_self = stacked(early, every, slice(2 * width, 3 * width)).astype(F32)
        chosen[...] = low(after_self * inverse_rms(after_self) * row(gain_cross))

    grads = (
        (low(tn(stacked(early, every, slice(0, width)), stacked(late, rows, slice(0, four)))), slice(0, four)),
        (low(tn(chosen[...], stacked(late, rows, slice(four, both)))), slice(four, both)),
    )
    gains = sum(gain_values(item[tokens:].astype(F32), four, width) for item in late)
    block = gain_block(gains, four, both)
    for z in range(ring):
        for c in range(2):
            at = (2 * z + c) * half
            for grad, lanes in grads:
                held[c, z, :half, lanes] = grad[at : at + half]
            held[c, z, half:, :] = block
    hand_out(ids, held, keep, give)


def tail_grads(call, gain_cross, early, middle, late, ring):
    chips = len(early)
    width = early[0].shape[1] // 3
    both = late[0].shape[1]
    part = (ring, width // (2 * ring) + extra_rows(both // 3 * 2, width), both)
    return call(
        functools.partial(tail_grads_kernel, chips=chips), "tail_grads", (shape(*part),) * 2,
        (gain_cross,) + tuple(early) + tuple(middle) + tuple(late), 28,
        [pltpu.VMEM((2,) + part, BF), pltpu.VMEM((chips * early[0].shape[0], width), BF)], "iv" + "v" * (3 * chips),
    )


def tail_sum_kernel(ids, keep, came, part, more, *outs, chips):
    both = keep.shape[2]
    four = both // 3 * 2
    width = four * chips // 4
    half = keep.shape[1] - extra_rows(four, width)
    gains = gain_values(keep[0, half:].astype(F32), four, width) + gain_values(came[0, half:].astype(F32), four, width)
    block = gain_block(gains, four, outs[0].shape[1])
    for by, out in enumerate(outs):
        z = ids[0] ^ by
        out[:half, :both] = low(keep[z, :half].astype(F32) + came[z, :half].astype(F32))
        out[:half, both:] = low(part[0, z].astype(F32) + more[0, z].astype(F32))
        out[half:] = block


def tail_sum(call, keep, came, parts, chips):
    ring, more, both = keep.shape
    return call(
        functools.partial(tail_sum_kernel, chips=chips), "tail_sum",
        (shape(more, both + parts[0].shape[3]),) * ring, (keep, came) + tuple(parts), 16, (), "ivvvv",
    )


def ring_sum_kernel(keep, came, out):
    out[...] = low(keep[0].astype(F32) + came[0].astype(F32))


def ring_sum(call, parts):
    return call(ring_sum_kernel, "ring_sum", shape(*parts[0].shape[1:]), tuple(parts), 16, (), "vv")


def last_sum_kernel(ids, *refs):
    parts, (out, *gain_outs, held) = refs[:-5], refs[-5:]
    half, both = out.shape
    ring, _, rows = held.shape
    four = both // 2
    out[...] = low(sum(item[:half].astype(F32) for item in parts))
    gains = sum(gain_values(item[half:].astype(F32), four, ring * rows) for item in parts)
    for z in range(ring):
        held[z] = gains[:, z * rows : (z + 1) * rows]
    for i, gain_out in enumerate(gain_outs):
        gain_out[...] = held[ids[0], i]


def last_sum(call, parts, rows):
    more, both = parts[0].shape
    half = rows // 2
    return call(
        last_sum_kernel, "last_sum", (shape(half, both),) + (shape32(rows),) * 3, tuple(parts), 16,
        [pltpu.VMEM((len(parts), 3, rows), F32)], "i" + "v" * len(parts),
    )


def place_pieces(ids, own, other, held):
    for by in range(own.shape[0]):
        held[ids[1] ^ by, ids[2]] = own[by]
        held[ids[1] ^ by, 1 - ids[2]] = other[by]


def first_out_kernel(ids, *refs, chips):
    own, other, in_out, out_out, held = refs
    place_pieces(ids, own, other, held)
    half, wide = held.shape[2:]
    span = wide // 2
    width = out_out.shape[1]
    few = half * span // width
    for j in range(chips):
        for c in range(2):
            rows = slice(c * half, (c + 1) * half)
            in_out[rows, j * span : (j + 1) * span] = held[j, c, :, :span].astype(F32)
            for v in range(width // span):
                at = (2 * j + c) * few
                out_out[at : at + few, v * span : (v + 1) * span] = held[
                    j, c, v * few : (v + 1) * few, span : 2 * span
                ].astype(F32)


def first_out(call, own, other, units, width):
    chips, half, wide = own.shape
    rows = 2 * half
    return call(
        functools.partial(first_out_kernel, chips=chips), "first_out",
        (shape32(rows, units), shape32(rows * units // width, width)),
        (own, other), 24, [pltpu.VMEM((chips, 2, half, wide), BF)], "ivv",
    )


def last_out_kernel(ids, *refs, chips):
    own, other, outs, held = refs[0], refs[1], refs[2:-1], refs[-1]
    place_pieces(ids, own, other, held)
    half, both = held.shape[2:]
    four, two = both // 2, both // 4
    for j in range(chips):
        for c in range(2):
            rows = slice(c * half, (c + 1) * half)
            at = j % (chips // 4) * four
            outs[j * 4 // chips][rows, at : at + four] = held[j, c, :, :four].astype(F32)
            at = j % (chips // 2) * two
            outs[4 + j * 2 // chips][rows, at : at + two] = held[j, c, :, four : four + two].astype(F32)
            outs[6 + j * 2 // chips][rows, at : at + two] = held[j, c, :, four + two :].astype(F32)


def last_out(call, own, other, width):
    chips, half, both = own.shape
    return call(
        functools.partial(last_out_kernel, chips=chips), "last_out", (shape32(2 * half, width),) * 8,
        (own, other), 24, [pltpu.VMEM((chips, 2, half, both), BF)], "ivv",
    )


def swap(values, axis, by):
    peers = lax.axis_size(axis)
    return lax.ppermute(values, axis, [(i, i ^ by) for i in range(peers)])


def over_chips(blocks):
    return [blocks[0]] + [swap(item, "pb", 2 * by) for by, item in enumerate(blocks) if by]


def over_ring(blocks):
    return [blocks[0]] + [swap(item, "pa", by) for by, item in enumerate(blocks) if by]


def over_core(blocks):
    return [swap(item, "pb", 1) for item in blocks]


def body(
    hidden, encoder, lengths, w_sq, w_sk, w_sv, w_so, w_cq, w_ck, w_cv, w_co, w_in, w_out,
    gain_self, gain_cross, gain_ffn, cotangent,
):
    _, tokens, width = hidden.shape
    questions, _, passage_len, _ = encoder.shape
    units = w_in.shape[1]
    ring = lax.axis_size("pa")
    chips = lax.axis_size("pb") // 2
    true_len = lengths.reshape(questions)
    hidden2 = hidden.reshape(tokens, width)
    cot = cotangent.reshape(tokens, width)
    enc = encoder.reshape(questions * passage_len, width)

    call = Line()
    x_self, self_q, self_k, self_v, self_mix, mixture, logs, after_self, x_cross, cross_q = self_forward(
        call, hidden2, gain_self, gain_cross, (w_sq, w_sk, w_sv, w_so, w_cq)
    )
    asked = over_ring([cross_q] * ring)
    keys, values = key_values(call, enc, w_ck, w_cv, passage_len)
    near = chips - 1
    partial = []
    for step in range(ring):
        last = step == ring - 1
        if step == 1:
            early = list(early_pack(call, x_self, self_mix, cot, after_self, chips))
        partial.append(
            cross_forward(call, true_len, asked[step], keys, values, step, (), 10 if last else None)
        )
    early[near] = hold(call, early[near], (w_co, w_in, w_out))
    early = over_chips(early)
    packed = over_ring(partial)
    call.meet(0, packed[1 : ring - 1])
    call.meet(3)
    found = feed_forward(call, after_self, cot, gain_ffn, w_co, w_in, w_out, packed)
    result, grad_after_cross, g_cross, sent, grad_gain_ffn, cross_mix, activated, grad_pre = found
    given = over_ring([sent] * ring)
    middle = list(middle_pack(call, cross_mix, activated, grad_pre, ring, chips))
    call.meet(0, early[1:])
    back = {}
    for step in [0] + list(range(2, ring)) + [1]:
        back[step] = cross_backward(call, true_len, asked[step], given[step], keys, values, step)
        if step == 0:
            sent = given[1] = swap(hold(call, sent), "pa", 1)
    middle = over_chips(middle)
    partial = over_ring([back[step][0] for step in range(ring)])
    grad_keys, grad_values = [back[step][1] for step in range(ring)], [back[step][2] for step in range(ring)]
    key_keep, key_give = key_grads(call, enc, grad_keys, grad_values, ring)
    ffn_keep, ffn_give = ffn_grads(
        call, w_co, gain_ffn, early, middle, ring, units, (hidden2, after_self, logs, mixture, gain_self, gain_cross)
    )
    call.meet(0, partial[2:])
    call.meet(20, ())
    key_parts = key_sum(call, key_keep, swap(key_give, "pb", 1), chips)
    first = first_sum(call, ffn_keep, swap(ffn_give, "pb", 1))
    found = self_backward(
        call,
        (grad_after_cross, after_self, hidden2, gain_self, gain_cross, grad_gain_ffn, g_cross,
         self_q, self_k, self_v, mixture, logs),
        (w_cq, w_so, w_sq, w_sk, w_sv),
        partial,
        chips,
    )
    grad_hidden = found[0]
    late = over_chips(found[1:])
    key_parts = halve(call, "key_add", "pb", *key_parts, 2)
    first = halve(call, "first_add", "pa", *first, 1)
    grad_encoder = encoder_grad(call, w_ck, w_cv, grad_keys, grad_values)
    call.meet(1, late[3:])
    keep, give = tail_grads(call, gain_cross, early, middle, late, ring)
    call.meet(0, [key_parts[1], first[1]])
    call.meet(12)
    last = over_ring(tail_sum(call, keep, swap(give, "pb", 1), key_parts, chips))
    first = over_chips([ring_sum(call, first)] * chips)
    call.meet(1, last[2:])
    last, *gains = last_sum(call, last, width // ring)
    last = over_chips([last] * chips)
    first = pack(call, first)
    last = pack(call, last)
    grad_in, grad_out = first_out(call, first, swap(first, "pb", 1), units, width)
    grad_sq, grad_sk, grad_sv, grad_so, grad_co, grad_cq, grad_ck, grad_cv = last_out(
        call, last, swap(last, "pb", 1), width
    )
    return (
        result.reshape(hidden.shape),
        grad_hidden.reshape(hidden.shape),
        grad_encoder.reshape(encoder.shape),
        grad_sq,
        grad_sk,
        grad_sv,
        grad_so,
        grad_cq,
        grad_ck,
        grad_cv,
        grad_co,
        grad_in,
        grad_out,
        gains[0],
        gains[1],
        gains[2],
    )


def solution(mesh):
    split = P(("pb", "pa"), None, None)
    passages = P("pb", "pa", None, None)
    return jax.shard_map(
        body,
        mesh=mesh,
        in_specs=(split, passages, P("pb", "pa")) + (P(),) * 13 + (split,),
        out_specs=(split, split, passages) + (P("pa", None),) * 10 + (P("pa"),) * 3,
        check_vma=False,
    )
```

```python
import functools

import jax
import jax.numpy as jnp
from jax import lax
from jax.experimental import pallas as pl
from jax.experimental.pallas import tpu as pltpu
from jax.sharding import PartitionSpec as P

HEADS = 12
EPS = 1e-06
NEG = -1000000000.0
F32 = jnp.float32
BF = jnp.bfloat16
SLOTS = 4
LANES = 128
MIB = 1 << 20


def dot(left, right, left_dim, right_dim, precision=None):
    return lax.dot_general(
        left,
        right,
        (((left_dim,), (right_dim,)), ((), ())),
        precision=precision,
        preferred_element_type=F32,
    )


def nn(left, right):
    return dot(left, right, 1, 0)


def nt(left, right):
    return dot(left, right, 1, 1)


def tn(left, right):
    return dot(left, right, 0, 0)


def low(values):
    return values.astype(BF)


def inverse_rms(values):
    return lax.rsqrt(jnp.mean(values * values, axis=-1, keepdims=True) + EPS)


def norm_back(grad, values, gain):
    inv = inverse_rms(values)
    scaled = gain * grad
    inner = jnp.mean(values * scaled, axis=-1, keepdims=True)
    grad_values = inv * scaled - values * (inv * inv * inv * inner)
    grad_gain = jnp.sum(grad * values * inv, axis=0, keepdims=True)
    return grad_values, grad_gain


def lanes_of(shape):
    return lax.broadcasted_iota(jnp.int32, shape, len(shape) - 1)


def rows_of(shape):
    return lax.broadcasted_iota(jnp.int32, shape, len(shape) - 2)


def ones_where(condition):
    return jnp.where(condition, 1.0, 0.0).astype(BF)


def spread_matrix(width):
    slot, lane = rows_of((LANES, width)), lanes_of((LANES, width))
    return ones_where((slot // SLOTS == lane // (width // HEADS)) & (slot % SLOTS < 2))


def compact_matrix():
    slot, lane = rows_of((LANES, LANES)), lanes_of((LANES, LANES))
    return ones_where((slot // SLOTS == lane // SLOTS) & (slot % SLOTS < 2))


def gather_matrix(width):
    feature, lane = rows_of((width, LANES)), lanes_of((width, LANES))
    return ones_where(feature // (width // HEADS) == lane // SLOTS)


def split_three(values):
    first = low(values).astype(F32)
    rest = values - first
    second = low(rest).astype(F32)
    third = low(rest - second).astype(F32)
    return first, second, third


def in_slots(values, start=0):
    first, second, _ = split_three(values)
    slot = lanes_of(values.shape) % SLOTS - start
    return jnp.where(slot == 0, first, jnp.where(slot == 1, second, 0.0))


def to_rows(extra, width):
    turned = jnp.transpose(extra)
    few = HEADS * SLOTS * extra.shape[0] // width
    return jnp.concatenate([turned[at : at + few] for at in range(0, HEADS * SLOTS, few)], 1)


def from_rows(rows, tokens):
    few = rows.shape[0]
    parts = [rows[:, at : at + tokens].astype(F32) for at in range(0, rows.shape[1], tokens)]
    parts.append(jnp.zeros((LANES - few * len(parts), tokens), F32))
    return low(jnp.transpose(jnp.concatenate(parts, 0)))


def few_rows(tokens, width):
    return HEADS * SLOTS * tokens // width


def head_sums(values, matrix):
    first, second, third = split_three(values)
    return nn(low(first), matrix) + nn(low(second), matrix) + nn(low(third), matrix)


def two_heads(block):
    first = lanes_of(block.shape) < block.shape[1] // 2
    zero = jnp.zeros_like(block)
    return jnp.concatenate([jnp.where(first, block, zero), jnp.where(first, zero, block)], 0)


def fold_heads(block):
    half = block.shape[0] // 2
    lane = lanes_of((half, block.shape[1]))
    return jnp.where(lane < block.shape[1] // 2, block[:half], block[half:])


def pair_of_slots(extra, pair, start, more=None):
    lane = lanes_of(extra.shape)
    slot = lane % SLOTS
    wanted = (slot >= start) & (slot < start + 2)
    halves = [
        jnp.where(wanted & (lane // SLOTS == 2 * pair + i), extra, jnp.zeros_like(extra)) for i in range(2)
    ]
    block = jnp.concatenate(halves, 0)
    return block if more is None else block + more


def last_lane(rows, value):
    return jnp.where(lanes_of((rows, LANES)) == LANES - 1, value, 0.0).astype(BF)


def attend_pair(queries, keys, values, valid=None):
    scores = nt(keys, queries)
    if valid is not None:
        scores = jnp.where(valid, scores, NEG)
    top = jnp.max(scores, axis=0, keepdims=True)
    weights = low(jnp.exp(scores - top))
    both = tn(weights, values)
    split = both.shape[1] - LANES
    mixture = fold_heads(both[:, :split]) * (1.0 / fold_heads(both[:, split:]))
    return mixture, both[:, split:], top


def log_totals(sums, tops):
    tokens = tops[0].shape[1] // 2
    lane = lanes_of((tokens, LANES)) // SLOTS
    found = jnp.ones((tokens, LANES), F32)
    rows = []
    for pair, (both, top) in enumerate(zip(sums, tops)):
        found = jnp.where(lane == 2 * pair, both[:tokens], jnp.where(lane == 2 * pair + 1, both[tokens:], found))
        rows += [jnp.broadcast_to(top[:, :tokens], (SLOTS, tokens)), jnp.broadcast_to(top[:, tokens:], (SLOTS, tokens))]
    rows.append(jnp.zeros((LANES - HEADS * SLOTS, tokens), F32))
    return jnp.transpose(jnp.concatenate(rows, 0)) + jnp.log(found)


def attend_pair_back(queries, keys, values, grad_mix, query_more, key_more, grad_more, value_more, valid=None):
    scaled = two_heads(queries)
    grad_two = two_heads(grad_mix)
    scores = nt(jnp.concatenate([keys, key_more], 1), jnp.concatenate([scaled, query_more], 1))
    probs = jnp.exp(scores)
    if valid is not None:
        probs = jnp.where(valid, probs, 0.0)
    grad_probs = nt(jnp.concatenate([values, value_more], 1), jnp.concatenate([grad_two, grad_more], 1))
    grad_scores = low(probs * grad_probs)
    grad_values = nn(low(probs), grad_two)
    grad_keys = nn(grad_scores, scaled)
    grad_queries = fold_heads(tn(grad_scores, keys))
    return grad_queries, grad_keys, grad_values


def minus_slots(rows, start):
    slot = lanes_of((rows, LANES)) % SLOTS
    return jnp.where((slot >= start) & (slot < start + 2), -1.0, 0.0)


def causal_mask(tokens):
    key = rows_of((tokens, 2 * tokens))
    token = lanes_of((tokens, 2 * tokens))
    return key <= jnp.where(token >= tokens, token - tokens, token)


WEIGHTS = {
    "self_forward": 0,
    "key_values": 5,
    "cross_forward": 1,
    "feed_forward": 5,
    "cross_backward": 4,
    "key_grads": 1,
    "ffn_grads": 0,
    "first_sum": 0,
    "self_backward": 20,
    "early_pack": 0,
    "middle_pack": 0,
    "encoder_grad": 0,
    "ring_sum": 0,
    "tail_grads": 0,
    "tail_sum": 0,
    "first_out": 0,
    "last_sum": 0,
    "last_out": 0,
    "meet": 0,
    "pack": 0,
    "hold": 0,
    "key_sum": 0,
    "key_add": 0,
    "first_add": 0,
}


class Line:
    def __init__(self):
        self.token = None

    def __call__(self, kernel, name, outs, args, mib, scratch=(), places="", after=(), weight=None):
        kinds = {"s": pltpu.SMEM, "h": pltpu.HBM, "v": pltpu.VMEM}
        placed = places[:1] == "i"
        specs = [pl.BlockSpec(memory_space=kinds[letter]) for letter in places[placed:]]
        count = len(args)
        single = not isinstance(outs, (tuple, list))
        outs = ((outs,) if single else tuple(outs)) + (shape32(8, LANES),)
        given = (() if self.token is None else (self.token,)) + tuple(after)
        homes = [pltpu.HBM if name == "self_forward" else pltpu.VMEM] * (len(outs) - 1) + [pltpu.VMEM]

        def run(*refs):
            at = count + len(given)
            made = refs[at : at + len(outs)]
            made[-1][...] = jnp.zeros((8, LANES), F32)
            here = ()
            if placed:
                lane = lax.axis_index("pb").astype(jnp.int32)
                here = ((lax.axis_index("pa").astype(jnp.int32), lane >> 1, lane & 1),)
            kernel(*here, *refs[:count], *made[:-1], *refs[at + len(outs) :])

        found = pl.pallas_call(
            run,
            out_shape=outs,
            in_specs=specs + [pl.BlockSpec(memory_space=pl.ANY)] * len(given),
            out_specs=[pl.BlockSpec(memory_space=home) for home in homes],
            scratch_shapes=scratch,
            compiler_params=pltpu.CompilerParams(vmem_limit_bytes=mib * MIB),
            cost_estimate=pl.CostEstimate(flops=int(1153000000 * (WEIGHTS[name] if weight is None else weight)), bytes_accessed=0, transcendentals=0),
            name=name,
        )(*args, *given)
        self.token = found[-1]
        return found[0] if single else found[:-1]

    def meet(self, weight, after=()):
        self(lambda *refs: None, "meet", (), (), 4, (), "", after, weight)


def shape(*dims):
    return jax.ShapeDtypeStruct(dims, BF)


def shape32(*dims):
    return jax.ShapeDtypeStruct(dims, F32)


def row(gain):
    return gain[...].reshape(1, gain.shape[0])


def self_forward_kernel(*refs):
    far, outs, refs = refs[:8], refs[8:18], refs[18:]
    held, made, (sems, out_sems) = refs[:8], refs[8:18], refs[18:]
    copies = [pltpu.make_async_copy(item, near, sems.at[i]) for i, (item, near) in enumerate(zip(far, held))]
    for item in copies:
        item.start()
    hidden, gain_self, gain_cross = held[:3]
    weights = held[3:]
    (x_self_out, q_out, k_out, v_out, mix_out, mixture_out, logs_out, after_out, x_cross_out, cross_q_out) = made
    pending = []

    def send(index):
        pending.append(pltpu.make_async_copy(made[index], outs[index], out_sems.at[index]))
        pending[-1].start()

    tokens, width = hidden.shape
    factor = (width // HEADS) ** -0.5
    copies[0].wait()
    copies[1].wait()
    stream = hidden[...].astype(F32)
    x_self = low(stream * inverse_rms(stream) * row(gain_self))
    x_self_out[...] = x_self
    send(0)
    for i in range(3):
        copies[3 + i].wait()
        made[1 + i][...] = low(nn(x_self, weights[i][...]))
        send(1 + i)
    queries, keys, values = (made[1 + i][...] for i in range(3))
    valid = causal_mask(tokens)
    pair_width = 2 * width // HEADS
    ones = jnp.ones((tokens, LANES), BF)
    mixtures, sums, tops = [], [], []
    for pair in range(HEADS // 2):
        part = slice(pair * pair_width, (pair + 1) * pair_width)
        mixture, both, top = attend_pair(
            two_heads(queries[:, part] * factor), keys[:, part], jnp.concatenate([values[:, part], ones], 1), valid
        )
        mixtures.append(mixture)
        sums.append(both)
        tops.append(top)
    mixture = jnp.concatenate(mixtures, 1)
    mixture_out[...] = mixture
    send(5)
    mix = low(mixture)
    mix_out[...] = mix
    send(4)
    logs_out[...] = log_totals(sums, tops)
    send(6)
    copies[2].wait()
    copies[6].wait()
    after_self = stream + nn(mix, weights[3][...])
    after_out[...] = after_self
    send(7)
    x_cross = low(after_self * inverse_rms(after_self) * row(gain_cross))
    x_cross_out[...] = x_cross
    send(8)
    copies[7].wait()
    cross_q_out[...] = low(nn(x_cross, weights[4][...]))
    send(9)
    for item in pending:
        item.wait()


def self_forward(call, hidden, gain_self, gain_cross, weights):
    tokens, width = hidden.shape
    low_one = shape(tokens, width)
    args = (hidden, gain_self, gain_cross) + tuple(weights)
    outs = (low_one,) * 5 + (
        shape32(tokens, width), shape32(tokens, LANES), shape32(tokens, width), low_one, low_one,
    )
    return call(
        self_forward_kernel, "self_forward", outs, args, 56,
        [pltpu.VMEM(item.shape, item.dtype) for item in args + outs]
        + [pltpu.SemaphoreType.DMA((size,)) for size in (len(args), len(outs))],
        "h" * len(args),
    )


def early_pack_kernel(ids, x_self, mix, cot, after_self, *early):
    chips = len(early)
    width = cot.shape[1]
    for by, out in enumerate(early):
        out[:, width : 2 * width] = cot[...]
        out[:, 2 * width :] = low(after_self[...])
        last = lax.div((ids[1] ^ by) * 4, chips) == 3

        @pl.when(last)
        def _():
            out[:, :width] = mix[...]

        @pl.when(jnp.logical_not(last))
        def _():
            out[:, :width] = x_self[...]


def early_pack(call, x_self, mix, cot, after_self, chips):
    tokens, width = cot.shape
    return call(
        early_pack_kernel, "early_pack", (shape(tokens, 3 * width),) * chips, (x_self, mix, cot, after_self), 12, (), "ivvvv"
    )


def key_values_kernel(encoder, w_ck, w_cv, keys, values, *, block):
    def step(index, carry):
        rows = pl.ds(pl.multiple_of(index * block, block), block)
        here = encoder[rows, :]
        keys[rows, :] = low(nn(here, w_ck[...]))
        values[rows, :] = low(nn(here, w_cv[...]))
        return carry

    lax.fori_loop(0, encoder.shape[0] // block, step, 0)


def key_values(call, encoder, w_ck, w_cv, block):
    return call(
        functools.partial(key_values_kernel, block=block), "key_values", (shape(*encoder.shape), shape(*encoder.shape)), (encoder, w_ck, w_cv), 24, (), "vvv"
    )


def key_rows(ids, count, step):
    key_count = count
    return pl.ds(pl.multiple_of((ids[0] ^ step) * key_count, LANES), key_count)


def cross_forward_kernel(ids, lengths, keys, values, queries, out, *, step, key_count):
    tokens, width = queries.shape
    factor = (width // HEADS) ** -0.5
    rows = key_rows(ids, key_count, step)
    size = (key_count, LANES)
    hidden_key = jnp.where(rows_of(size) < lengths[ids[0] ^ step], 0.0, NEG)
    key_more = jnp.where(lanes_of(size) == LANES - 1, hidden_key, 0.0).astype(BF)
    query_more = last_lane(2 * tokens, 1.0)
    ones = jnp.ones(size, BF)
    pair_width = 2 * width // HEADS
    sums, tops = [], []
    for pair in range(HEADS // 2):
        part = slice(pair * pair_width, (pair + 1) * pair_width)
        mixture, both, top = attend_pair(
            jnp.concatenate([two_heads(queries[:, part] * factor), query_more], 1),
            jnp.concatenate([keys[rows, part], key_more], 1),
            jnp.concatenate([values[rows, part], ones], 1),
        )
        out[:tokens, part] = low(mixture)
        sums.append(both)
        tops.append(top)
    out[tokens:] = low(to_rows(in_slots(log_totals(sums, tops)), width))


def cross_forward(call, lengths, queries, keys, values, step, after=(), weight=None):
    tokens, width = queries.shape
    key_count = keys.shape[0] // lengths.shape[0]
    return call(
        functools.partial(cross_forward_kernel, step=step, key_count=key_count),
        "cross_forward", shape(tokens + few_rows(tokens, width), width), (lengths, keys, values, queries), 16, (), "isvvv",
        after, weight,
    )


def feed_forward_kernel(
    after_self, cotangent, gain_ffn, w_co, w_in, w_out, *refs, count, chunks
):
    packed, refs = refs[:count], refs[count:]
    result_out, grad_after_out, g_cross_out, send_out, grad_gain_out, mix_out, act_held, grad_held = refs
    tokens, width = after_self.shape
    units = w_in.shape[1]
    wide = units // chunks
    compact, spread = compact_matrix(), spread_matrix(width)
    logs = [nn(from_rows(part[tokens:], tokens), compact) for part in packed]
    top = functools.reduce(jnp.maximum, logs)
    log_total = top + jnp.log(sum(jnp.exp(item - top) for item in logs))
    mixture = sum(
        nn(low(in_slots(jnp.exp(item - log_total))), spread) * part[:tokens].astype(F32)
        for item, part in zip(logs, packed)
    )
    mix = low(mixture)
    mix_out[...] = mix
    after_cross = after_self[...] + nn(mix, w_co[...])
    x_ffn = low(after_cross * inverse_rms(after_cross) * row(gain_ffn))
    grad_low = cotangent[...]
    slope = (2.0 / 3.141592653589793) ** 0.5

    def step(chunk, carry):
        part = pl.ds(pl.multiple_of(chunk * wide, LANES), wide)
        pre = nn(x_ffn, w_in[:, part])
        square = pre * pre
        bent = jnp.tanh(pre * (slope + (0.044715 * slope) * square))
        act_held[:, part] = low(0.5 * pre * (1.0 + bent))
        grad_act = nt(grad_low, w_out[part, :])
        bend = 0.5 * (1.0 + bent) + 0.5 * pre * (1.0 - bent * bent) * (slope + (3 * 0.044715 * slope) * square)
        grad_held[:, part] = low(grad_act * bend)
        return carry

    lax.fori_loop(0, chunks, step, 0, unroll=True)
    result = after_cross + nn(act_held[...], w_out[...])
    grad_x = nt(grad_held[...], w_in[...])
    result_out[...] = low(result)
    grad_values, grad_gain = norm_back(grad_x, after_cross, row(gain_ffn))
    grad_gain_out[...] = grad_gain
    grad_after = grad_low.astype(F32) + grad_values
    grad_after_out[...] = grad_after
    g_cross = low(grad_after)
    g_cross_out[...] = g_cross
    grad_mix = low(nt(g_cross, w_co[...]))
    delta = head_sums(grad_mix.astype(F32) * mixture, gather_matrix(width))
    send_out[:tokens] = grad_mix
    send_out[tokens:] = low(to_rows(in_slots(log_total) + in_slots(delta, 2), width))


def middle_pack_kernel(ids, mix, act, grad_pre, *refs, count):
    middle, acts, grad_pres = refs[:-2], refs[-2], refs[-1]
    chips, _, span = acts.shape
    width = mix.shape[1]
    units = act.shape[1]
    piece = units // (count * chips)
    for which in range(units // piece):
        slot = which // chips * piece
        acts[which % chips, :, slot : slot + piece] = act[:, which * piece : (which + 1) * piece]
    for which in range(chips):
        grad_pres[which] = grad_pre[:, which * span : (which + 1) * span]
    for by, out in enumerate(middle):
        index = ids[1] ^ by
        out[:, :width] = mix[...]
        out[:, width : width + span] = acts[index]
        out[:, width + span :] = grad_pres[index]


def middle_pack(call, mix, act, grad_pre, count, chips):
    tokens, width = mix.shape
    span = act.shape[1] // chips
    return call(
        functools.partial(middle_pack_kernel, count=count), "middle_pack", (shape(tokens, width + 2 * span),) * chips,
        (mix, act, grad_pre), 16, [pltpu.VMEM((chips, tokens, span), BF)] * 2, "ivvv",
    )


def feed_forward(call, after_self, cotangent, gain_ffn, w_co, w_in, w_out, packed):
    tokens, width = after_self.shape
    units = w_in.shape[1]
    return call(
        functools.partial(feed_forward_kernel, count=len(packed), chunks=4),
        "feed_forward",
        (shape(tokens, width), shape32(tokens, width), shape(tokens, width),
         shape(tokens + few_rows(tokens, width), width), shape32(1, width), shape(tokens, width),
         shape(tokens, units), shape(tokens, units)),
        (after_self, cotangent, gain_ffn, w_co, w_in, w_out) + tuple(packed),
        28,
        (),
        "vvvvvv" + "v" * len(packed),
    )


def cross_backward_kernel(ids, lengths, keys, values, queries, grads, grad_queries, grad_keys, grad_values, *, step):
    tokens, width = queries.shape
    key_count = grad_keys.shape[0]
    factor = (width // HEADS) ** -0.5
    rows = key_rows(ids, key_count, step)
    size = (key_count, LANES)
    hidden_key = jnp.where(rows_of(size) < lengths[ids[0] ^ step], 0.0, NEG)
    key_more = jnp.where(lanes_of(size) == LANES - 1, hidden_key, minus_slots(key_count, 0)).astype(BF)
    value_more = minus_slots(key_count, 2).astype(BF)
    extra = from_rows(grads[tokens:], tokens)
    one = last_lane(2 * tokens, 1.0)
    pair_width = 2 * width // HEADS
    for pair in range(HEADS // 2):
        part = slice(pair * pair_width, (pair + 1) * pair_width)
        grad_q, grad_k, grad_v = attend_pair_back(
            queries[:, part] * factor, keys[rows, part], values[rows, part], grads[:tokens, part],
            pair_of_slots(extra, pair, 0, one), key_more, pair_of_slots(extra, pair, 2), value_more,
        )
        grad_queries[:, part] = low(grad_q * factor)
        grad_keys[:, part] = low(grad_k)
        grad_values[:, part] = low(grad_v)


def cross_backward(call, lengths, queries, grads, keys, values, step):
    tokens, width = queries.shape
    key_count = keys.shape[0] // lengths.shape[0]
    return call(
        functools.partial(cross_backward_kernel, step=step),
        "cross_backward",
        (shape(tokens, width), shape(key_count, width), shape(key_count, width)),
        (lengths, keys, values, queries, grads), 20, (), "isvvvv",
    )


def extra_rows(four, width):
    return -(-6 * width // four // 8) * 8


def gain_block(gains, four, width_out):
    count = gains.shape[1] // four
    few = extra_rows(four, gains.shape[1])
    high = low(gains).astype(F32)
    rows = [part[i : i + 1, v * four : (v + 1) * four] for part in (high, gains - high) for i in range(3) for v in range(count)]
    block = jnp.concatenate(rows + [jnp.zeros((few - len(rows), four), F32)], 0)
    return low(jnp.concatenate([block, jnp.zeros((few, width_out - four), F32)], 1))


def gain_values(block, four, width):
    count = width // four
    rows = []
    for i in range(3):
        pieces = [
            block[i * count + v : i * count + v + 1, :four] + block[(3 + i) * count + v : (3 + i) * count + v + 1, :four]
            for v in range(count)
        ]
        rows.append(jnp.concatenate(pieces, 1))
    return jnp.concatenate(rows, 0)


def self_backward_kernel(
    ids, grad_after_cross, after_self, hidden, gain_self, gain_cross, grad_gain_ffn, g_cross,
    self_q, self_k, self_v, mixture, logs, *refs, count, chips
):
    weights, partial, refs = refs[:5], refs[5 : 5 + count], refs[5 + count :]
    hidden_out, late = refs[0], refs[1 : 1 + chips]
    fours, twos = refs[1 + chips :]
    tokens, width = after_self.shape
    factor = (width // HEADS) ** -0.5
    four, two = 4 * width // chips, 2 * width // chips
    grad_cq = low(sum(item[...].astype(F32) for item in partial))
    grad_values, grad_gain_cross = norm_back(nt(grad_cq, weights[0][...]), after_self[...], row(gain_cross))
    grad_after = grad_after_cross[...] + grad_values
    g_self = low(grad_after)
    grad_mix = low(nt(g_self, weights[1][...]))
    delta = head_sums(grad_mix.astype(F32) * mixture[...], gather_matrix(width))
    extra = low(in_slots(logs[...]) + in_slots(delta, 2))
    valid = causal_mask(tokens)
    key_more = minus_slots(tokens, 0).astype(BF)
    value_more = minus_slots(tokens, 2).astype(BF)
    pair_width = 2 * width // HEADS
    found = []
    for pair in range(HEADS // 2):
        part = slice(pair * pair_width, (pair + 1) * pair_width)
        grad_q, grad_k, grad_v = attend_pair_back(
            self_q[:, part] * factor, self_k[:, part], self_v[:, part], grad_mix[:, part],
            pair_of_slots(extra, pair, 0), key_more, pair_of_slots(extra, pair, 2), value_more, valid,
        )
        found.append((low(grad_q * factor), low(grad_k), low(grad_v)))
    grads = [jnp.concatenate([item[i] for item in found], 1) for i in range(3)]
    grad_x = jnp.zeros((tokens, width), F32)
    for i in range(3):
        grad_x = grad_x + nt(grads[i], weights[2 + i][...])
    grad_values, grad_gain_self = norm_back(grad_x, hidden[...].astype(F32), row(gain_self))
    hidden_out[...] = low(grad_after + grad_values)
    gains = jnp.concatenate([grad_gain_self, grad_gain_cross, grad_gain_ffn[...]], 0)
    block = gain_block(gains, four, four + two)
    for i, item in enumerate(grads + [g_self]):
        for v in range(width // four):
            fours[i * (width // four) + v] = item[:, v * four : (v + 1) * four]
    for i, item in enumerate((g_cross[...], grad_cq)):
        for v in range(width // two):
            twos[i * (width // two) + v] = item[:, v * two : (v + 1) * two]
    chip = ids[1]
    for by, out in enumerate(late):
        out[:tokens, :four] = fours[chip ^ by]
        out[:tokens, four:] = twos[chip ^ by]
        out[tokens:] = block


def self_backward(call, first, weights, partial, chips):
    tokens, width = first[1].shape
    four, two = 4 * width // chips, 2 * width // chips
    return call(
        functools.partial(self_backward_kernel, count=len(partial), chips=chips),
        "self_backward",
        (shape(tokens, width),) + (shape(tokens + extra_rows(four, width), four + two),) * chips,
        tuple(first) + tuple(weights) + tuple(partial),
        20,
        [pltpu.VMEM((chips, tokens, four), BF), pltpu.VMEM((chips, tokens, two), BF)],
        "i" + "v" * (len(first) + 5 + len(partial)),
    )


def stacked(refs, rows, lanes):
    return jnp.concatenate([item[rows, lanes] for item in refs], 0)


def hand_out(ids, held, keep, give):
    core = ids[2]
    keep[...] = held[core]
    give[...] = held[1 - core]


def ffn_grads_kernel(ids, w_co, gain_ffn, *refs, chips):
    early, middle, (keep, give, held) = refs[:chips], refs[chips : 2 * chips], refs[-3:]
    _, ring, half, both = held.shape
    span = both // 2
    width = early[0].shape[1] // 3
    every = slice(None)
    mix = stacked(middle, every, slice(0, width))
    after_cross = stacked(early, every, slice(2 * width, 3 * width)).astype(F32) + nn(mix, w_co[...])
    x_ffn = low(after_cross * inverse_rms(after_cross) * row(gain_ffn))
    grad_in = low(tn(x_ffn, stacked(middle, every, slice(width + span, width + 2 * span))))
    for z in range(ring):
        for c in range(2):
            at = (2 * z + c) * half
            held[c, z, :, :span] = grad_in[at : at + half]
    grad_out = low(
        tn(stacked(middle, every, slice(width, width + span)), stacked(early, every, slice(width, 2 * width)))
    )
    few = span // (2 * ring)
    for z in range(ring):
        for c in range(2):
            at = (2 * z + c) * few
            block = grad_out[at : at + few]
            held[c, z, :, span:] = jnp.concatenate([block[:, v : v + span] for v in range(0, width, span)], 0)
    hand_out(ids, held, keep, give)


def ffn_grads(call, w_co, gain_ffn, early, middle, ring, units, more):
    chips = len(early)
    width = early[0].shape[1] // 3
    part = (ring, width // (2 * ring), 2 * units // chips)
    return call(
        functools.partial(ffn_grads_kernel, chips=chips), "ffn_grads", (shape(*part),) * 2,
        (w_co, gain_ffn) + tuple(early) + tuple(middle) + tuple(more), 28, [pltpu.VMEM((2,) + part, BF)],
        "ivv" + "v" * (2 * chips + len(more)),
    )


def key_grads_kernel(ids, encoder, *refs):
    grads, (keep, give, held) = refs[:-3], refs[-3:]
    count = len(grads) // 2
    _, ring, half, both = held.shape
    width = both // 2
    key_count = grads[0].shape[0]
    rows = jnp.concatenate([encoder[key_rows(ids, key_count, step), :] for step in range(count)], 0)
    for i in range(2):
        grad = low(tn(rows, stacked(grads[i * count : (i + 1) * count], slice(None), slice(None))))
        for z in range(ring):
            for c in range(2):
                at = (2 * z + c) * half
                held[c, z, :, i * width : (i + 1) * width] = grad[at : at + half]
    hand_out(ids, held, keep, give)


def key_grads(call, encoder, grad_keys, grad_values, ring):
    width = encoder.shape[1]
    part = (ring, width // (2 * ring), 2 * width)
    return call(
        key_grads_kernel, "key_grads", (shape(*part),) * 2, (encoder,) + tuple(grad_keys) + tuple(grad_values), 32,
        [pltpu.VMEM((2,) + part, BF)], "iv" + "v" * (2 * len(grad_keys)),
    )


def encoder_grad_kernel(ids, w_ck, w_cv, *refs):
    grads, out, held = refs[:-2], refs[-2], refs[-1]
    count = len(grads) // 2
    key_count = grads[0].shape[0]
    for index, item in enumerate(grads):
        held[index] = item[...]

    def step(index, carry):
        rows = pl.ds(pl.multiple_of((ids[0] ^ index) * key_count, LANES), key_count)
        out[rows, :] = low(nt(held[index], w_ck[...]) + nt(held[count + index], w_cv[...]))
        return carry

    lax.fori_loop(0, count, step, 0)


def encoder_grad(call, w_ck, w_cv, grad_keys, grad_values):
    key_count, width = grad_keys[0].shape
    return call(
        encoder_grad_kernel, "encoder_grad", shape(key_count * len(grad_keys), width),
        (w_ck, w_cv) + tuple(grad_keys) + tuple(grad_values), 12 + 3 * len(grad_keys),
        [pltpu.VMEM((2 * len(grad_keys), key_count, width), BF)], "ivv" + "v" * (2 * len(grad_keys)),
    )


def key_sum_kernel(ids, keep, came, even, odd, held):
    chips, two = held.shape[0], held.shape[3]
    summed = low(keep[...].astype(F32) + came[...].astype(F32))
    for j in range(chips):
        held[j] = summed[:, :, j * two : (j + 1) * two]
    for by in range(chips):
        (even, odd)[by % 2][by // 2] = held[ids[1] ^ by]


def key_sum(call, keep, came, chips):
    ring, half, both = keep.shape
    part = (ring, half, both // chips)
    return call(
        key_sum_kernel, "key_sum", (shape(chips // 2, *part),) * 2, (keep, came), 20, [pltpu.VMEM((chips,) + part, BF)],
        "ivv",
    )


def first_sum_kernel(ids, keep, came, *outs):
    for by in range(keep.shape[0]):
        z = ids[0] ^ by
        outs[by % 2][by // 2] = low(keep[z].astype(F32) + came[z].astype(F32))


def first_sum(call, keep, came):
    part = (keep.shape[0] // 2,) + keep.shape[1:]
    return call(first_sum_kernel, "first_sum", (shape(*part),) * 2, (keep, came), 16, (), "ivv")


def hold_kernel(item, *refs):
    refs[-1][...] = item[...]


def hold(call, item, near=()):
    return call(hold_kernel, "hold", shape(*item.shape), (item, *near), 24, (), "v" * (1 + len(near)))


def pack_kernel(*refs):
    for at, item in enumerate(refs[:-1]):
        refs[-1][at] = item[...]


def pack(call, parts):
    return call(pack_kernel, "pack", shape(len(parts), *parts[0].shape), tuple(parts), 16, (), "v" * len(parts))


def add_halves_kernel(*refs, count, inner):
    keep, came, outs = refs[: 1 if inner else count], refs[1 if inner else count], refs[2 if inner else count + 1 :]
    for at in range(count):
        mine = keep[0][at] if inner else keep[at][...]
        outs[at % 2][at // 2] = low(mine.astype(F32) + came[at].astype(F32))


def add_halves(call, name, keep, came):
    inner = not isinstance(keep, (tuple, list))
    count = came.shape[0]
    part = (count // 2,) + came.shape[1:]
    args = (keep,) if inner else tuple(keep)
    return call(
        functools.partial(add_halves_kernel, count=count, inner=inner), name, (shape(*part),) * 2, args + (came,), 16, (),
        "v" * (len(args) + 1),
    )


def halve(call, name, axis, keep, give, by):
    came = swap(give, axis, by)
    if came.shape[0] == 1:
        return keep, came
    keep, give = add_halves(call, name, keep, came)
    return halve(call, name, axis, keep, give, 2 * by)


def tail_grads_kernel(ids, gain_cross, *refs, chips):
    early, middle, late = refs[:chips], refs[chips : 2 * chips], refs[2 * chips : 3 * chips]
    keep, give, held, chosen = refs[3 * chips :]
    _, ring, more, both = held.shape
    four = both // 3 * 2
    width = early[0].shape[1] // 3
    half = more - extra_rows(four, width)
    tokens = early[0].shape[0]
    every, rows = slice(None), slice(0, tokens)
    first = lax.div(ids[1] * 2, chips) == 0

    @pl.when(first)
    def _():
        chosen[...] = stacked(middle, every, slice(0, width))

    @pl.when(jnp.logical_not(first))
    def _():
        after_self = stacked(early, every, slice(2 * width, 3 * width)).astype(F32)
        chosen[...] = low(after_self * inverse_rms(after_self) * row(gain_cross))

    grads = (
        (low(tn(stacked(early, every, slice(0, width)), stacked(late, rows, slice(0, four)))), slice(0, four)),
        (low(tn(chosen[...], stacked(late, rows, slice(four, both)))), slice(four, both)),
    )
    gains = sum(gain_values(item[tokens:].astype(F32), four, width) for item in late)
    block = gain_block(gains, four, both)
    for z in range(ring):
        for c in range(2):
            at = (2 * z + c) * half
            for grad, lanes in grads:
                held[c, z, :half, lanes] = grad[at : at + half]
            held[c, z, half:, :] = block
    hand_out(ids, held, keep, give)


def tail_grads(call, gain_cross, early, middle, late, ring):
    chips = len(early)
    width = early[0].shape[1] // 3
    both = late[0].shape[1]
    part = (ring, width // (2 * ring) + extra_rows(both // 3 * 2, width), both)
    return call(
        functools.partial(tail_grads_kernel, chips=chips), "tail_grads", (shape(*part),) * 2,
        (gain_cross,) + tuple(early) + tuple(middle) + tuple(late), 28,
        [pltpu.VMEM((2,) + part, BF), pltpu.VMEM((chips * early[0].shape[0], width), BF)], "iv" + "v" * (3 * chips),
    )


def tail_sum_kernel(ids, keep, came, part, more, *outs, chips):
    both = keep.shape[2]
    four = both // 3 * 2
    width = four * chips // 4
    half = keep.shape[1] - extra_rows(four, width)
    gains = gain_values(keep[0, half:].astype(F32), four, width) + gain_values(came[0, half:].astype(F32), four, width)
    block = gain_block(gains, four, outs[0].shape[1])
    for by, out in enumerate(outs):
        z = ids[0] ^ by
        out[:half, :both] = low(keep[z, :half].astype(F32) + came[z, :half].astype(F32))
        out[:half, both:] = low(part[0, z].astype(F32) + more[0, z].astype(F32))
        out[half:] = block


def tail_sum(call, keep, came, parts, chips):
    ring, more, both = keep.shape
    return call(
        functools.partial(tail_sum_kernel, chips=chips), "tail_sum",
        (shape(more, both + parts[0].shape[3]),) * ring, (keep, came) + tuple(parts), 16, (), "ivvvv",
    )


def ring_sum_kernel(keep, came, out):
    out[...] = low(keep[0].astype(F32) + came[0].astype(F32))


def ring_sum(call, parts):
    return call(ring_sum_kernel, "ring_sum", shape(*parts[0].shape[1:]), tuple(parts), 16, (), "vv")


def last_sum_kernel(ids, *refs):
    parts, (out, *gain_outs, held) = refs[:-5], refs[-5:]
    half, both = out.shape
    ring, _, rows = held.shape
    four = both // 2
    out[...] = low(sum(item[:half].astype(F32) for item in parts))
    gains = sum(gain_values(item[half:].astype(F32), four, ring * rows) for item in parts)
    for z in range(ring):
        held[z] = gains[:, z * rows : (z + 1) * rows]
    for i, gain_out in enumerate(gain_outs):
        gain_out[...] = held[ids[0], i]


def last_sum(call, parts, rows):
    more, both = parts[0].shape
    half = rows // 2
    return call(
        last_sum_kernel, "last_sum", (shape(half, both),) + (shape32(rows),) * 3, tuple(parts), 16,
        [pltpu.VMEM((len(parts), 3, rows), F32)], "i" + "v" * len(parts),
    )


def place_pieces(ids, own, other, held):
    for by in range(own.shape[0]):
        held[ids[1] ^ by, ids[2]] = own[by]
        held[ids[1] ^ by, 1 - ids[2]] = other[by]


def first_out_kernel(ids, *refs, chips):
    own, other, in_out, out_out, held = refs
    place_pieces(ids, own, other, held)
    half, wide = held.shape[2:]
    span = wide // 2
    width = out_out.shape[1]
    few = half * span // width
    for j in range(chips):
        for c in range(2):
            rows = slice(c * half, (c + 1) * half)
            in_out[rows, j * span : (j + 1) * span] = held[j, c, :, :span].astype(F32)
            for v in range(width // span):
                at = (2 * j + c) * few
                out_out[at : at + few, v * span : (v + 1) * span] = held[
                    j, c, v * few : (v + 1) * few, span : 2 * span
                ].astype(F32)


def first_out(call, own, other, units, width):
    chips, half, wide = own.shape
    rows = 2 * half
    return call(
        functools.partial(first_out_kernel, chips=chips), "first_out",
        (shape32(rows, units), shape32(rows * units // width, width)),
        (own, other), 24, [pltpu.VMEM((chips, 2, half, wide), BF)], "ivv",
    )


def last_out_kernel(ids, *refs, chips):
    own, other, outs, held = refs[0], refs[1], refs[2:-1], refs[-1]
    place_pieces(ids, own, other, held)
    half, both = held.shape[2:]
    four, two = both // 2, both // 4
    for j in range(chips):
        for c in range(2):
            rows = slice(c * half, (c + 1) * half)
            at = j % (chips // 4) * four
            outs[j * 4 // chips][rows, at : at + four] = held[j, c, :, :four].astype(F32)
            at = j % (chips // 2) * two
            outs[4 + j * 2 // chips][rows, at : at + two] = held[j, c, :, four : four + two].astype(F32)
            outs[6 + j * 2 // chips][rows, at : at + two] = held[j, c, :, four + two :].astype(F32)


def last_out(call, own, other, width):
    chips, half, both = own.shape
    return call(
        functools.partial(last_out_kernel, chips=chips), "last_out", (shape32(2 * half, width),) * 8,
        (own, other), 24, [pltpu.VMEM((chips, 2, half, both), BF)], "ivv",
    )


def swap(values, axis, by):
    peers = lax.axis_size(axis)
    return lax.ppermute(values, axis, [(i, i ^ by) for i in range(peers)])


def over_chips(blocks):
    return [blocks[0]] + [swap(item, "pb", 2 * by) for by, item in enumerate(blocks) if by]


def over_ring(blocks):
    return [blocks[0]] + [swap(item, "pa", by) for by, item in enumerate(blocks) if by]


def over_core(blocks):
    return [swap(item, "pb", 1) for item in blocks]


def body(
    hidden, encoder, lengths, w_sq, w_sk, w_sv, w_so, w_cq, w_ck, w_cv, w_co, w_in, w_out,
    gain_self, gain_cross, gain_ffn, cotangent,
):
    _, tokens, width = hidden.shape
    questions, _, passage_len, _ = encoder.shape
    units = w_in.shape[1]
    ring = lax.axis_size("pa")
    chips = lax.axis_size("pb") // 2
    true_len = lengths.reshape(questions)
    hidden2 = hidden.reshape(tokens, width)
    cot = cotangent.reshape(tokens, width)
    enc = encoder.reshape(questions * passage_len, width)

    call = Line()
    x_self, self_q, self_k, self_v, self_mix, mixture, logs, after_self, x_cross, cross_q = self_forward(
        call, hidden2, gain_self, gain_cross, (w_sq, w_sk, w_sv, w_so, w_cq)
    )
    asked = over_ring([cross_q] * ring)
    keys, values = key_values(call, enc, w_ck, w_cv, passage_len)
    near = chips - 1
    order = [0] + list(range(2, ring)) + [1]
    partial = {}
    for step in order:
        last = step == order[-1]
        partial[step] = cross_forward(call, true_len, asked[step], keys, values, step, (), 1 if last else None)
        if step == 0:
            early = list(early_pack(call, x_self, self_mix, cot, after_self, chips))
    partial = [partial[step] for step in range(ring)]
    early[near] = hold(call, early[near], (w_co, w_in, w_out))
    early = over_chips(early)
    packed = over_ring(partial)
    call.meet(1, packed[2:3])
    call.meet(0, packed[3:])
    call.meet(3)
    found = feed_forward(call, after_self, cot, gain_ffn, w_co, w_in, w_out, packed)
    result, grad_after_cross, g_cross, sent, grad_gain_ffn, cross_mix, activated, grad_pre = found
    given = over_ring([sent] * ring)
    middle = list(middle_pack(call, cross_mix, activated, grad_pre, ring, chips))
    call.meet(0, early[1:])
    back = {}
    for step in [0] + list(range(2, ring)) + [1]:
        back[step] = cross_backward(call, true_len, asked[step], given[step], keys, values, step)
        if step == 0:
            sent = given[1] = swap(hold(call, sent), "pa", 1)
    middle = over_chips(middle)
    partial = over_ring([back[step][0] for step in range(ring)])
    grad_keys, grad_values = [back[step][1] for step in range(ring)], [back[step][2] for step in range(ring)]
    key_keep, key_give = key_grads(call, enc, grad_keys, grad_values, ring)
    ffn_keep, ffn_give = ffn_grads(
        call, w_co, gain_ffn, early, middle, ring, units, (hidden2, after_self, logs, mixture, gain_self, gain_cross)
    )
    call.meet(0, partial[2:])
    call.meet(20, ())
    key_parts = key_sum(call, key_keep, swap(key_give, "pb", 1), chips)
    first = first_sum(call, ffn_keep, swap(ffn_give, "pb", 1))
    found = self_backward(
        call,
        (grad_after_cross, after_self, hidden2, gain_self, gain_cross, grad_gain_ffn, g_cross,
         self_q, self_k, self_v, mixture, logs),
        (w_cq, w_so, w_sq, w_sk, w_sv),
        partial,
        chips,
    )
    grad_hidden = found[0]
    late = over_chips(found[1:])
    key_parts = halve(call, "key_add", "pb", *key_parts, 2)
    first = halve(call, "first_add", "pa", *first, 1)
    grad_encoder = encoder_grad(call, w_ck, w_cv, grad_keys, grad_values)
    call.meet(1, late[3:])
    keep, give = tail_grads(call, gain_cross, early, middle, late, ring)
    call.meet(0, [key_parts[1], first[1]])
    call.meet(12)
    last = over_ring(tail_sum(call, keep, swap(give, "pb", 1), key_parts, chips))
    first = over_chips([ring_sum(call, first)] * chips)
    call.meet(1, last[2:])
    last, *gains = last_sum(call, last, width // ring)
    last = over_chips([last] * chips)
    first = pack(call, first)
    last = pack(call, last)
    grad_in, grad_out = first_out(call, first, swap(first, "pb", 1), units, width)
    grad_sq, grad_sk, grad_sv, grad_so, grad_co, grad_cq, grad_ck, grad_cv = last_out(
        call, last, swap(last, "pb", 1), width
    )
    return (
        result.reshape(hidden.shape),
        grad_hidden.reshape(hidden.shape),
        grad_encoder.reshape(encoder.shape),
        grad_sq,
        grad_sk,
        grad_sv,
        grad_so,
        grad_cq,
        grad_ck,
        grad_cv,
        grad_co,
        grad_in,
        grad_out,
        gains[0],
        gains[1],
        gains[2],
    )


def solution(mesh):
    split = P(("pb", "pa"), None, None)
    passages = P("pb", "pa", None, None)
    return jax.shard_map(
        body,
        mesh=mesh,
        in_specs=(split, passages, P("pb", "pa")) + (P(),) * 13 + (split,),
        out_specs=(split, split, passages) + (P("pa", None),) * 10 + (P("pa"),) * 3,
        check_vma=False,
    )
```

```python
import functools

import jax
import jax.numpy as jnp
from jax import lax
from jax.experimental import pallas as pl
from jax.experimental.pallas import tpu as pltpu
from jax.sharding import PartitionSpec as P

HEADS = 12
EPS = 1e-06
NEG = -1000000000.0
F32 = jnp.float32
BF = jnp.bfloat16
SLOTS = 4
LANES = 128
MIB = 1 << 20


def dot(left, right, left_dim, right_dim, precision=None):
    return lax.dot_general(
        left,
        right,
        (((left_dim,), (right_dim,)), ((), ())),
        precision=precision,
        preferred_element_type=F32,
    )


def nn(left, right):
    return dot(left, right, 1, 0)


def nt(left, right):
    return dot(left, right, 1, 1)


def tn(left, right):
    return dot(left, right, 0, 0)


def low(values):
    return values.astype(BF)


def inverse_rms(values):
    return lax.rsqrt(jnp.mean(values * values, axis=-1, keepdims=True) + EPS)


def norm_back(grad, values, gain):
    inv = inverse_rms(values)
    scaled = gain * grad
    inner = jnp.mean(values * scaled, axis=-1, keepdims=True)
    grad_values = inv * scaled - values * (inv * inv * inv * inner)
    grad_gain = jnp.sum(grad * values * inv, axis=0, keepdims=True)
    return grad_values, grad_gain


def lanes_of(shape):
    return lax.broadcasted_iota(jnp.int32, shape, len(shape) - 1)


def rows_of(shape):
    return lax.broadcasted_iota(jnp.int32, shape, len(shape) - 2)


def ones_where(condition):
    return jnp.where(condition, 1.0, 0.0).astype(BF)


def spread_matrix(width):
    slot, lane = rows_of((LANES, width)), lanes_of((LANES, width))
    return ones_where((slot // SLOTS == lane // (width // HEADS)) & (slot % SLOTS < 2))


def compact_matrix():
    slot, lane = rows_of((LANES, LANES)), lanes_of((LANES, LANES))
    return ones_where((slot // SLOTS == lane // SLOTS) & (slot % SLOTS < 2))


def gather_matrix(width):
    feature, lane = rows_of((width, LANES)), lanes_of((width, LANES))
    return ones_where(feature // (width // HEADS) == lane // SLOTS)


def split_three(values):
    first = low(values).astype(F32)
    rest = values - first
    second = low(rest).astype(F32)
    third = low(rest - second).astype(F32)
    return first, second, third


def in_slots(values, start=0):
    first, second, _ = split_three(values)
    slot = lanes_of(values.shape) % SLOTS - start
    return jnp.where(slot == 0, first, jnp.where(slot == 1, second, 0.0))


def to_rows(extra, width):
    turned = jnp.transpose(extra)
    few = HEADS * SLOTS * extra.shape[0] // width
    return jnp.concatenate([turned[at : at + few] for at in range(0, HEADS * SLOTS, few)], 1)


def from_rows(rows, tokens):
    few = rows.shape[0]
    parts = [rows[:, at : at + tokens].astype(F32) for at in range(0, rows.shape[1], tokens)]
    parts.append(jnp.zeros((LANES - few * len(parts), tokens), F32))
    return low(jnp.transpose(jnp.concatenate(parts, 0)))


def few_rows(tokens, width):
    return HEADS * SLOTS * tokens // width


def head_sums(values, matrix):
    first, second, third = split_three(values)
    return nn(low(first), matrix) + nn(low(second), matrix) + nn(low(third), matrix)


def two_heads(block):
    first = lanes_of(block.shape) < block.shape[1] // 2
    zero = jnp.zeros_like(block)
    return jnp.concatenate([jnp.where(first, block, zero), jnp.where(first, zero, block)], 0)


def fold_heads(block):
    half = block.shape[0] // 2
    lane = lanes_of((half, block.shape[1]))
    return jnp.where(lane < block.shape[1] // 2, block[:half], block[half:])


def pair_of_slots(extra, pair, start, more=None):
    lane = lanes_of(extra.shape)
    slot = lane % SLOTS
    wanted = (slot >= start) & (slot < start + 2)
    halves = [
        jnp.where(wanted & (lane // SLOTS == 2 * pair + i), extra, jnp.zeros_like(extra)) for i in range(2)
    ]
    block = jnp.concatenate(halves, 0)
    return block if more is None else block + more


def last_lane(rows, value):
    return jnp.where(lanes_of((rows, LANES)) == LANES - 1, value, 0.0).astype(BF)


def attend_pair(queries, keys, values, valid=None):
    scores = nt(keys, queries)
    if valid is not None:
        scores = jnp.where(valid, scores, NEG)
    top = jnp.max(scores, axis=0, keepdims=True)
    weights = low(jnp.exp(scores - top))
    both = tn(weights, values)
    split = both.shape[1] - LANES
    mixture = fold_heads(both[:, :split]) * (1.0 / fold_heads(both[:, split:]))
    return mixture, both[:, split:], top


def log_totals(sums, tops):
    tokens = tops[0].shape[1] // 2
    lane = lanes_of((tokens, LANES)) // SLOTS
    found = jnp.ones((tokens, LANES), F32)
    rows = []
    for pair, (both, top) in enumerate(zip(sums, tops)):
        found = jnp.where(lane == 2 * pair, both[:tokens], jnp.where(lane == 2 * pair + 1, both[tokens:], found))
        rows += [jnp.broadcast_to(top[:, :tokens], (SLOTS, tokens)), jnp.broadcast_to(top[:, tokens:], (SLOTS, tokens))]
    rows.append(jnp.zeros((LANES - HEADS * SLOTS, tokens), F32))
    return jnp.transpose(jnp.concatenate(rows, 0)) + jnp.log(found)


def attend_pair_back(queries, keys, values, grad_mix, query_more, key_more, grad_more, value_more, valid=None):
    scaled = two_heads(queries)
    grad_two = two_heads(grad_mix)
    scores = nt(jnp.concatenate([keys, key_more], 1), jnp.concatenate([scaled, query_more], 1))
    probs = jnp.exp(scores)
    if valid is not None:
        probs = jnp.where(valid, probs, 0.0)
    grad_probs = nt(jnp.concatenate([values, value_more], 1), jnp.concatenate([grad_two, grad_more], 1))
    grad_scores = low(probs * grad_probs)
    grad_values = nn(low(probs), grad_two)
    grad_keys = nn(grad_scores, scaled)
    grad_queries = fold_heads(tn(grad_scores, keys))
    return grad_queries, grad_keys, grad_values


def minus_slots(rows, start):
    slot = lanes_of((rows, LANES)) % SLOTS
    return jnp.where((slot >= start) & (slot < start + 2), -1.0, 0.0)


def causal_mask(tokens):
    key = rows_of((tokens, 2 * tokens))
    token = lanes_of((tokens, 2 * tokens))
    return key <= jnp.where(token >= tokens, token - tokens, token)


WEIGHTS = {
    "self_forward": 0,
    "key_values": 5,
    "cross_forward": 1,
    "feed_forward": 5,
    "cross_backward": 4,
    "key_grads": 1,
    "ffn_grads": 0,
    "first_sum": 0,
    "self_backward": 20,
    "early_pack": 0,
    "middle_pack": 0,
    "encoder_grad": 0,
    "ring_sum": 0,
    "tail_grads": 0,
    "tail_sum": 0,
    "first_out": 0,
    "last_sum": 0,
    "last_out": 0,
    "meet": 0,
    "pack": 0,
    "hold": 0,
    "key_sum": 0,
    "key_add": 0,
    "first_add": 0,
}


class Line:
    def __init__(self):
        self.token = None

    def __call__(self, kernel, name, outs, args, mib, scratch=(), places="", after=(), weight=None):
        kinds = {"s": pltpu.SMEM, "h": pltpu.HBM, "v": pltpu.VMEM}
        placed = places[:1] == "i"
        specs = [pl.BlockSpec(memory_space=kinds[letter]) for letter in places[placed:]]
        count = len(args)
        single = not isinstance(outs, (tuple, list))
        outs = ((outs,) if single else tuple(outs)) + (shape32(8, LANES),)
        given = (() if self.token is None else (self.token,)) + tuple(after)
        homes = [pltpu.HBM if name == "self_forward" else pltpu.VMEM] * (len(outs) - 1) + [pltpu.VMEM]

        def run(*refs):
            at = count + len(given)
            made = refs[at : at + len(outs)]
            made[-1][...] = jnp.zeros((8, LANES), F32)
            here = ()
            if placed:
                lane = lax.axis_index("pb").astype(jnp.int32)
                here = ((lax.axis_index("pa").astype(jnp.int32), lane >> 1, lane & 1),)
            kernel(*here, *refs[:count], *made[:-1], *refs[at + len(outs) :])

        found = pl.pallas_call(
            run,
            out_shape=outs,
            in_specs=specs + [pl.BlockSpec(memory_space=pl.ANY)] * len(given),
            out_specs=[pl.BlockSpec(memory_space=home) for home in homes],
            scratch_shapes=scratch,
            compiler_params=pltpu.CompilerParams(vmem_limit_bytes=mib * MIB),
            cost_estimate=pl.CostEstimate(flops=int(1153000000 * (WEIGHTS[name] if weight is None else weight)), bytes_accessed=0, transcendentals=0),
            name=name,
        )(*args, *given)
        self.token = found[-1]
        return found[0] if single else found[:-1]

    def meet(self, weight, after=()):
        self(lambda *refs: None, "meet", (), (), 4, (), "", after, weight)


def shape(*dims):
    return jax.ShapeDtypeStruct(dims, BF)


def shape32(*dims):
    return jax.ShapeDtypeStruct(dims, F32)


def row(gain):
    return gain[...].reshape(1, gain.shape[0])


def self_forward_kernel(*refs):
    far, outs, refs = refs[:8], refs[8:18], refs[18:]
    held, made, (sems, out_sems) = refs[:8], refs[8:18], refs[18:]
    copies = [pltpu.make_async_copy(item, near, sems.at[i]) for i, (item, near) in enumerate(zip(far, held))]
    for item in copies:
        item.start()
    hidden, gain_self, gain_cross = held[:3]
    weights = held[3:]
    (x_self_out, q_out, k_out, v_out, mix_out, mixture_out, logs_out, after_out, x_cross_out, cross_q_out) = made
    pending = []

    def send(index):
        pending.append(pltpu.make_async_copy(made[index], outs[index], out_sems.at[index]))
        pending[-1].start()

    tokens, width = hidden.shape
    factor = (width // HEADS) ** -0.5
    copies[0].wait()
    copies[1].wait()
    stream = hidden[...].astype(F32)
    x_self = low(stream * inverse_rms(stream) * row(gain_self))
    x_self_out[...] = x_self
    send(0)
    for i in range(3):
        copies[3 + i].wait()
        made[1 + i][...] = low(nn(x_self, weights[i][...]))
        send(1 + i)
    queries, keys, values = (made[1 + i][...] for i in range(3))
    valid = causal_mask(tokens)
    pair_width = 2 * width // HEADS
    ones = jnp.ones((tokens, LANES), BF)
    mixtures, sums, tops = [], [], []
    for pair in range(HEADS // 2):
        part = slice(pair * pair_width, (pair + 1) * pair_width)
        mixture, both, top = attend_pair(
            two_heads(queries[:, part] * factor), keys[:, part], jnp.concatenate([values[:, part], ones], 1), valid
        )
        mixtures.append(mixture)
        sums.append(both)
        tops.append(top)
    mixture = jnp.concatenate(mixtures, 1)
    mixture_out[...] = mixture
    send(5)
    mix = low(mixture)
    mix_out[...] = mix
    send(4)
    logs_out[...] = log_totals(sums, tops)
    send(6)
    copies[2].wait()
    copies[6].wait()
    after_self = stream + nn(mix, weights[3][...])
    after_out[...] = after_self
    send(7)
    x_cross = low(after_self * inverse_rms(after_self) * row(gain_cross))
    x_cross_out[...] = x_cross
    send(8)
    copies[7].wait()
    cross_q_out[...] = low(nn(x_cross, weights[4][...]))
    send(9)
    for item in pending:
        item.wait()


def self_forward(call, hidden, gain_self, gain_cross, weights):
    tokens, width = hidden.shape
    low_one = shape(tokens, width)
    args = (hidden, gain_self, gain_cross) + tuple(weights)
    outs = (low_one,) * 5 + (
        shape32(tokens, width), shape32(tokens, LANES), shape32(tokens, width), low_one, low_one,
    )
    return call(
        self_forward_kernel, "self_forward", outs, args, 56,
        [pltpu.VMEM(item.shape, item.dtype) for item in args + outs]
        + [pltpu.SemaphoreType.DMA((size,)) for size in (len(args), len(outs))],
        "h" * len(args),
    )


def early_pack_kernel(ids, x_self, mix, cot, after_self, *early):
    chips = len(early)
    width = cot.shape[1]
    for by, out in enumerate(early):
        out[:, width : 2 * width] = cot[...]
        out[:, 2 * width :] = low(after_self[...])
        last = lax.div((ids[1] ^ by) * 4, chips) == 3

        @pl.when(last)
        def _():
            out[:, :width] = mix[...]

        @pl.when(jnp.logical_not(last))
        def _():
            out[:, :width] = x_self[...]


def early_pack(call, x_self, mix, cot, after_self, chips):
    tokens, width = cot.shape
    return call(
        early_pack_kernel, "early_pack", (shape(tokens, 3 * width),) * chips, (x_self, mix, cot, after_self), 12, (), "ivvvv"
    )


def key_values_kernel(encoder, w_ck, w_cv, keys, values, *, block):
    def step(index, carry):
        rows = pl.ds(pl.multiple_of(index * block, block), block)
        here = encoder[rows, :]
        keys[rows, :] = low(nn(here, w_ck[...]))
        values[rows, :] = low(nn(here, w_cv[...]))
        return carry

    lax.fori_loop(0, encoder.shape[0] // block, step, 0)


def key_values(call, encoder, w_ck, w_cv, block):
    return call(
        functools.partial(key_values_kernel, block=block), "key_values", (shape(*encoder.shape), shape(*encoder.shape)), (encoder, w_ck, w_cv), 24, (), "vvv"
    )


def key_rows(ids, count, step):
    key_count = count
    return pl.ds(pl.multiple_of((ids[0] ^ step) * key_count, LANES), key_count)


def cross_forward_kernel(ids, lengths, keys, values, queries, out, *, step, key_count):
    tokens, width = queries.shape
    factor = (width // HEADS) ** -0.5
    rows = key_rows(ids, key_count, step)
    size = (key_count, LANES)
    hidden_key = jnp.where(rows_of(size) < lengths[ids[0] ^ step], 0.0, NEG)
    key_more = jnp.where(lanes_of(size) == LANES - 1, hidden_key, 0.0).astype(BF)
    query_more = last_lane(2 * tokens, 1.0)
    ones = jnp.ones(size, BF)
    pair_width = 2 * width // HEADS
    sums, tops = [], []
    for pair in range(HEADS // 2):
        part = slice(pair * pair_width, (pair + 1) * pair_width)
        mixture, both, top = attend_pair(
            jnp.concatenate([two_heads(queries[:, part] * factor), query_more], 1),
            jnp.concatenate([keys[rows, part], key_more], 1),
            jnp.concatenate([values[rows, part], ones], 1),
        )
        out[:tokens, part] = low(mixture)
        sums.append(both)
        tops.append(top)
    out[tokens:] = low(to_rows(in_slots(log_totals(sums, tops)), width))


def cross_forward(call, lengths, queries, keys, values, step, after=(), weight=None):
    tokens, width = queries.shape
    key_count = keys.shape[0] // lengths.shape[0]
    return call(
        functools.partial(cross_forward_kernel, step=step, key_count=key_count),
        "cross_forward", shape(tokens + few_rows(tokens, width), width), (lengths, keys, values, queries), 16, (), "isvvv",
        after, weight,
    )


def feed_forward_kernel(
    after_self, cotangent, gain_ffn, w_co, w_in, w_out, *refs, count, chunks
):
    packed, refs = refs[:count], refs[count:]
    result_out, grad_after_out, g_cross_out, send_out, grad_gain_out, mix_out, act_held, grad_held = refs
    tokens, width = after_self.shape
    units = w_in.shape[1]
    wide = units // chunks
    compact, spread = compact_matrix(), spread_matrix(width)
    logs = [nn(from_rows(part[tokens:], tokens), compact) for part in packed]
    top = functools.reduce(jnp.maximum, logs)
    log_total = top + jnp.log(sum(jnp.exp(item - top) for item in logs))
    mixture = sum(
        nn(low(in_slots(jnp.exp(item - log_total))), spread) * part[:tokens].astype(F32)
        for item, part in zip(logs, packed)
    )
    mix = low(mixture)
    mix_out[...] = mix
    after_cross = after_self[...] + nn(mix, w_co[...])
    x_ffn = low(after_cross * inverse_rms(after_cross) * row(gain_ffn))
    grad_low = cotangent[...]
    slope = (2.0 / 3.141592653589793) ** 0.5

    def step(chunk, carry):
        part = pl.ds(pl.multiple_of(chunk * wide, LANES), wide)
        pre = nn(x_ffn, w_in[:, part])
        square = pre * pre
        bent = jnp.tanh(pre * (slope + (0.044715 * slope) * square))
        act_held[:, part] = low(0.5 * pre * (1.0 + bent))
        grad_act = nt(grad_low, w_out[part, :])
        bend = 0.5 * (1.0 + bent) + 0.5 * pre * (1.0 - bent * bent) * (slope + (3 * 0.044715 * slope) * square)
        grad_held[:, part] = low(grad_act * bend)
        return carry

    lax.fori_loop(0, chunks, step, 0, unroll=True)
    result = after_cross + nn(act_held[...], w_out[...])
    grad_x = nt(grad_held[...], w_in[...])
    result_out[...] = low(result)
    grad_values, grad_gain = norm_back(grad_x, after_cross, row(gain_ffn))
    grad_gain_out[...] = grad_gain
    grad_after = grad_low.astype(F32) + grad_values
    grad_after_out[...] = grad_after
    g_cross = low(grad_after)
    g_cross_out[...] = g_cross
    grad_mix = low(nt(g_cross, w_co[...]))
    delta = head_sums(grad_mix.astype(F32) * mixture, gather_matrix(width))
    send_out[:tokens] = grad_mix
    send_out[tokens:] = low(to_rows(in_slots(log_total) + in_slots(delta, 2), width))


def middle_pack_kernel(ids, mix, act, grad_pre, *refs, count):
    middle, acts, grad_pres = refs[:-2], refs[-2], refs[-1]
    chips, _, span = acts.shape
    width = mix.shape[1]
    units = act.shape[1]
    piece = units // (count * chips)
    for which in range(units // piece):
        slot = which // chips * piece
        acts[which % chips, :, slot : slot + piece] = act[:, which * piece : (which + 1) * piece]
    for which in range(chips):
        grad_pres[which] = grad_pre[:, which * span : (which + 1) * span]
    for by, out in enumerate(middle):
        index = ids[1] ^ by
        out[:, :width] = mix[...]
        out[:, width : width + span] = acts[index]
        out[:, width + span :] = grad_pres[index]


def middle_pack(call, mix, act, grad_pre, count, chips):
    tokens, width = mix.shape
    span = act.shape[1] // chips
    return call(
        functools.partial(middle_pack_kernel, count=count), "middle_pack", (shape(tokens, width + 2 * span),) * chips,
        (mix, act, grad_pre), 16, [pltpu.VMEM((chips, tokens, span), BF)] * 2, "ivvv",
    )


def feed_forward(call, after_self, cotangent, gain_ffn, w_co, w_in, w_out, packed):
    tokens, width = after_self.shape
    units = w_in.shape[1]
    return call(
        functools.partial(feed_forward_kernel, count=len(packed), chunks=4),
        "feed_forward",
        (shape(tokens, width), shape32(tokens, width), shape(tokens, width),
         shape(tokens + few_rows(tokens, width), width), shape32(1, width), shape(tokens, width),
         shape(tokens, units), shape(tokens, units)),
        (after_self, cotangent, gain_ffn, w_co, w_in, w_out) + tuple(packed),
        28,
        (),
        "vvvvvv" + "v" * len(packed),
    )


def cross_backward_kernel(ids, lengths, keys, values, queries, grads, grad_queries, grad_keys, grad_values, *, step):
    tokens, width = queries.shape
    key_count = grad_keys.shape[0]
    factor = (width // HEADS) ** -0.5
    rows = key_rows(ids, key_count, step)
    size = (key_count, LANES)
    hidden_key = jnp.where(rows_of(size) < lengths[ids[0] ^ step], 0.0, NEG)
    key_more = jnp.where(lanes_of(size) == LANES - 1, hidden_key, minus_slots(key_count, 0)).astype(BF)
    value_more = minus_slots(key_count, 2).astype(BF)
    extra = from_rows(grads[tokens:], tokens)
    one = last_lane(2 * tokens, 1.0)
    pair_width = 2 * width // HEADS
    for pair in range(HEADS // 2):
        part = slice(pair * pair_width, (pair + 1) * pair_width)
        grad_q, grad_k, grad_v = attend_pair_back(
            queries[:, part] * factor, keys[rows, part], values[rows, part], grads[:tokens, part],
            pair_of_slots(extra, pair, 0, one), key_more, pair_of_slots(extra, pair, 2), value_more,
        )
        grad_queries[:, part] = low(grad_q * factor)
        grad_keys[:, part] = low(grad_k)
        grad_values[:, part] = low(grad_v)


def cross_backward(call, lengths, queries, grads, keys, values, step):
    tokens, width = queries.shape
    key_count = keys.shape[0] // lengths.shape[0]
    return call(
        functools.partial(cross_backward_kernel, step=step),
        "cross_backward",
        (shape(tokens, width), shape(key_count, width), shape(key_count, width)),
        (lengths, keys, values, queries, grads), 20, (), "isvvvv",
    )


def extra_rows(four, width):
    return -(-6 * width // four // 8) * 8


def gain_block(gains, four, width_out):
    count = gains.shape[1] // four
    few = extra_rows(four, gains.shape[1])
    high = low(gains).astype(F32)
    rows = [part[i : i + 1, v * four : (v + 1) * four] for part in (high, gains - high) for i in range(3) for v in range(count)]
    block = jnp.concatenate(rows + [jnp.zeros((few - len(rows), four), F32)], 0)
    return low(jnp.concatenate([block, jnp.zeros((few, width_out - four), F32)], 1))


def gain_values(block, four, width):
    count = width // four
    rows = []
    for i in range(3):
        pieces = [
            block[i * count + v : i * count + v + 1, :four] + block[(3 + i) * count + v : (3 + i) * count + v + 1, :four]
            for v in range(count)
        ]
        rows.append(jnp.concatenate(pieces, 1))
    return jnp.concatenate(rows, 0)


def self_backward_kernel(
    ids, grad_after_cross, after_self, hidden, gain_self, gain_cross, grad_gain_ffn, g_cross,
    self_q, self_k, self_v, mixture, logs, *refs, count, chips
):
    weights, partial, refs = refs[:5], refs[5 : 5 + count], refs[5 + count :]
    hidden_out, late = refs[0], refs[1 : 1 + chips]
    fours, twos = refs[1 + chips :]
    tokens, width = after_self.shape
    factor = (width // HEADS) ** -0.5
    four, two = 4 * width // chips, 2 * width // chips
    grad_cq = low(sum(item[...].astype(F32) for item in partial))
    grad_values, grad_gain_cross = norm_back(nt(grad_cq, weights[0][...]), after_self[...], row(gain_cross))
    grad_after = grad_after_cross[...] + grad_values
    g_self = low(grad_after)
    grad_mix = low(nt(g_self, weights[1][...]))
    delta = head_sums(grad_mix.astype(F32) * mixture[...], gather_matrix(width))
    extra = low(in_slots(logs[...]) + in_slots(delta, 2))
    valid = causal_mask(tokens)
    key_more = minus_slots(tokens, 0).astype(BF)
    value_more = minus_slots(tokens, 2).astype(BF)
    pair_width = 2 * width // HEADS
    found = []
    for pair in range(HEADS // 2):
        part = slice(pair * pair_width, (pair + 1) * pair_width)
        grad_q, grad_k, grad_v = attend_pair_back(
            self_q[:, part] * factor, self_k[:, part], self_v[:, part], grad_mix[:, part],
            pair_of_slots(extra, pair, 0), key_more, pair_of_slots(extra, pair, 2), value_more, valid,
        )
        found.append((low(grad_q * factor), low(grad_k), low(grad_v)))
    grads = [jnp.concatenate([item[i] for item in found], 1) for i in range(3)]
    grad_x = jnp.zeros((tokens, width), F32)
    for i in range(3):
        grad_x = grad_x + nt(grads[i], weights[2 + i][...])
    grad_values, grad_gain_self = norm_back(grad_x, hidden[...].astype(F32), row(gain_self))
    hidden_out[...] = low(grad_after + grad_values)
    gains = jnp.concatenate([grad_gain_self, grad_gain_cross, grad_gain_ffn[...]], 0)
    block = gain_block(gains, four, four + two)
    for i, item in enumerate(grads + [g_self]):
        for v in range(width // four):
            fours[i * (width // four) + v] = item[:, v * four : (v + 1) * four]
    for i, item in enumerate((g_cross[...], grad_cq)):
        for v in range(width // two):
            twos[i * (width // two) + v] = item[:, v * two : (v + 1) * two]
    chip = ids[1]
    for by, out in enumerate(late):
        out[:tokens, :four] = fours[chip ^ by]
        out[:tokens, four:] = twos[chip ^ by]
        out[tokens:] = block


def self_backward(call, first, weights, partial, chips):
    tokens, width = first[1].shape
    four, two = 4 * width // chips, 2 * width // chips
    return call(
        functools.partial(self_backward_kernel, count=len(partial), chips=chips),
        "self_backward",
        (shape(tokens, width),) + (shape(tokens + extra_rows(four, width), four + two),) * chips,
        tuple(first) + tuple(weights) + tuple(partial),
        20,
        [pltpu.VMEM((chips, tokens, four), BF), pltpu.VMEM((chips, tokens, two), BF)],
        "i" + "v" * (len(first) + 5 + len(partial)),
    )


def stacked(refs, rows, lanes):
    return jnp.concatenate([item[rows, lanes] for item in refs], 0)


def hand_out(ids, held, keep, give):
    core = ids[2]
    keep[...] = held[core]
    give[...] = held[1 - core]


def ffn_grads_kernel(ids, w_co, gain_ffn, *refs, chips):
    early, middle, (keep, give, held) = refs[:chips], refs[chips : 2 * chips], refs[-3:]
    _, ring, half, both = held.shape
    span = both // 2
    width = early[0].shape[1] // 3
    every = slice(None)
    mix = stacked(middle, every, slice(0, width))
    after_cross = stacked(early, every, slice(2 * width, 3 * width)).astype(F32) + nn(mix, w_co[...])
    x_ffn = low(after_cross * inverse_rms(after_cross) * row(gain_ffn))
    grad_in = low(tn(x_ffn, stacked(middle, every, slice(width + span, width + 2 * span))))
    for z in range(ring):
        for c in range(2):
            at = (2 * z + c) * half
            held[c, z, :, :span] = grad_in[at : at + half]
    grad_out = low(
        tn(stacked(middle, every, slice(width, width + span)), stacked(early, every, slice(width, 2 * width)))
    )
    few = span // (2 * ring)
    for z in range(ring):
        for c in range(2):
            at = (2 * z + c) * few
            block = grad_out[at : at + few]
            held[c, z, :, span:] = jnp.concatenate([block[:, v : v + span] for v in range(0, width, span)], 0)
    hand_out(ids, held, keep, give)


def ffn_grads(call, w_co, gain_ffn, early, middle, ring, units, more):
    chips = len(early)
    width = early[0].shape[1] // 3
    part = (ring, width // (2 * ring), 2 * units // chips)
    return call(
        functools.partial(ffn_grads_kernel, chips=chips), "ffn_grads", (shape(*part),) * 2,
        (w_co, gain_ffn) + tuple(early) + tuple(middle) + tuple(more), 28, [pltpu.VMEM((2,) + part, BF)],
        "ivv" + "v" * (2 * chips + len(more)),
    )


def key_grads_kernel(ids, encoder, *refs):
    grads, (keep, give, held) = refs[:-3], refs[-3:]
    count = len(grads) // 2
    _, ring, half, both = held.shape
    width = both // 2
    key_count = grads[0].shape[0]
    rows = jnp.concatenate([encoder[key_rows(ids, key_count, step), :] for step in range(count)], 0)
    for i in range(2):
        grad = low(tn(rows, stacked(grads[i * count : (i + 1) * count], slice(None), slice(None))))
        for z in range(ring):
            for c in range(2):
                at = (2 * z + c) * half
                held[c, z, :, i * width : (i + 1) * width] = grad[at : at + half]
    hand_out(ids, held, keep, give)


def key_grads(call, encoder, grad_keys, grad_values, ring):
    width = encoder.shape[1]
    part = (ring, width // (2 * ring), 2 * width)
    return call(
        key_grads_kernel, "key_grads", (shape(*part),) * 2, (encoder,) + tuple(grad_keys) + tuple(grad_values), 32,
        [pltpu.VMEM((2,) + part, BF)], "iv" + "v" * (2 * len(grad_keys)),
    )


def encoder_grad_kernel(ids, w_ck, w_cv, *refs):
    grads, out, held = refs[:-2], refs[-2], refs[-1]
    count = len(grads) // 2
    key_count = grads[0].shape[0]
    for index, item in enumerate(grads):
        held[index] = item[...]

    def step(index, carry):
        rows = pl.ds(pl.multiple_of((ids[0] ^ index) * key_count, LANES), key_count)
        out[rows, :] = low(nt(held[index], w_ck[...]) + nt(held[count + index], w_cv[...]))
        return carry

    lax.fori_loop(0, count, step, 0)


def encoder_grad(call, w_ck, w_cv, grad_keys, grad_values):
    key_count, width = grad_keys[0].shape
    return call(
        encoder_grad_kernel, "encoder_grad", shape(key_count * len(grad_keys), width),
        (w_ck, w_cv) + tuple(grad_keys) + tuple(grad_values), 12 + 3 * len(grad_keys),
        [pltpu.VMEM((2 * len(grad_keys), key_count, width), BF)], "ivv" + "v" * (2 * len(grad_keys)),
    )


def key_sum_kernel(ids, keep, came, even, odd, held):
    chips, two = held.shape[0], held.shape[3]
    summed = low(keep[...].astype(F32) + came[...].astype(F32))
    for j in range(chips):
        held[j] = summed[:, :, j * two : (j + 1) * two]
    for by in range(chips):
        (even, odd)[by % 2][by // 2] = held[ids[1] ^ by]


def key_sum(call, keep, came, chips):
    ring, half, both = keep.shape
    part = (ring, half, both // chips)
    return call(
        key_sum_kernel, "key_sum", (shape(chips // 2, *part),) * 2, (keep, came), 20, [pltpu.VMEM((chips,) + part, BF)],
        "ivv",
    )


def first_sum_kernel(ids, keep, came, *outs):
    for by in range(keep.shape[0]):
        z = ids[0] ^ by
        outs[by % 2][by // 2] = low(keep[z].astype(F32) + came[z].astype(F32))


def first_sum(call, keep, came):
    part = (keep.shape[0] // 2,) + keep.shape[1:]
    return call(first_sum_kernel, "first_sum", (shape(*part),) * 2, (keep, came), 16, (), "ivv")


def hold_kernel(item, *refs):
    refs[-1][...] = item[...]


def hold(call, item, near=()):
    return call(hold_kernel, "hold", shape(*item.shape), (item, *near), 24, (), "v" * (1 + len(near)))


def pack_kernel(*refs):
    for at, item in enumerate(refs[:-1]):
        refs[-1][at] = item[...]


def pack(call, parts):
    return call(pack_kernel, "pack", shape(len(parts), *parts[0].shape), tuple(parts), 16, (), "v" * len(parts))


def add_halves_kernel(*refs, count, inner):
    keep, came, outs = refs[: 1 if inner else count], refs[1 if inner else count], refs[2 if inner else count + 1 :]
    for at in range(count):
        mine = keep[0][at] if inner else keep[at][...]
        outs[at % 2][at // 2] = low(mine.astype(F32) + came[at].astype(F32))


def add_halves(call, name, keep, came):
    inner = not isinstance(keep, (tuple, list))
    count = came.shape[0]
    part = (count // 2,) + came.shape[1:]
    args = (keep,) if inner else tuple(keep)
    return call(
        functools.partial(add_halves_kernel, count=count, inner=inner), name, (shape(*part),) * 2, args + (came,), 16, (),
        "v" * (len(args) + 1),
    )


def halve(call, name, axis, keep, give, by):
    came = swap(give, axis, by)
    if came.shape[0] == 1:
        return keep, came
    keep, give = add_halves(call, name, keep, came)
    return halve(call, name, axis, keep, give, 2 * by)


def tail_grads_kernel(ids, gain_cross, *refs, chips):
    early, middle, late = refs[:chips], refs[chips : 2 * chips], refs[2 * chips : 3 * chips]
    keep, give, held, chosen = refs[3 * chips :]
    _, ring, more, both = held.shape
    four = both // 3 * 2
    width = early[0].shape[1] // 3
    half = more - extra_rows(four, width)
    tokens = early[0].shape[0]
    every, rows = slice(None), slice(0, tokens)
    first = lax.div(ids[1] * 2, chips) == 0

    @pl.when(first)
    def _():
        chosen[...] = stacked(middle, every, slice(0, width))

    @pl.when(jnp.logical_not(first))
    def _():
        after_self = stacked(early, every, slice(2 * width, 3 * width)).astype(F32)
        chosen[...] = low(after_self * inverse_rms(after_self) * row(gain_cross))

    grads = (
        (low(tn(stacked(early, every, slice(0, width)), stacked(late, rows, slice(0, four)))), slice(0, four)),
        (low(tn(chosen[...], stacked(late, rows, slice(four, both)))), slice(four, both)),
    )
    gains = sum(gain_values(item[tokens:].astype(F32), four, width) for item in late)
    block = gain_block(gains, four, both)
    for z in range(ring):
        for c in range(2):
            at = (2 * z + c) * half
            for grad, lanes in grads:
                held[c, z, :half, lanes] = grad[at : at + half]
            held[c, z, half:, :] = block
    hand_out(ids, held, keep, give)


def tail_grads(call, gain_cross, early, middle, late, ring):
    chips = len(early)
    width = early[0].shape[1] // 3
    both = late[0].shape[1]
    part = (ring, width // (2 * ring) + extra_rows(both // 3 * 2, width), both)
    return call(
        functools.partial(tail_grads_kernel, chips=chips), "tail_grads", (shape(*part),) * 2,
        (gain_cross,) + tuple(early) + tuple(middle) + tuple(late), 28,
        [pltpu.VMEM((2,) + part, BF), pltpu.VMEM((chips * early[0].shape[0], width), BF)], "iv" + "v" * (3 * chips),
    )


def tail_sum_kernel(ids, keep, came, part, more, *outs, chips):
    both = keep.shape[2]
    four = both // 3 * 2
    width = four * chips // 4
    half = keep.shape[1] - extra_rows(four, width)
    gains = gain_values(keep[0, half:].astype(F32), four, width) + gain_values(came[0, half:].astype(F32), four, width)
    block = gain_block(gains, four, outs[0].shape[1])
    for by, out in enumerate(outs):
        z = ids[0] ^ by
        out[:half, :both] = low(keep[z, :half].astype(F32) + came[z, :half].astype(F32))
        out[:half, both:] = low(part[0, z].astype(F32) + more[0, z].astype(F32))
        out[half:] = block


def tail_sum(call, keep, came, parts, chips):
    ring, more, both = keep.shape
    return call(
        functools.partial(tail_sum_kernel, chips=chips), "tail_sum",
        (shape(more, both + parts[0].shape[3]),) * ring, (keep, came) + tuple(parts), 16, (), "ivvvv",
    )


def ring_sum_kernel(keep, came, out):
    out[...] = low(keep[0].astype(F32) + came[0].astype(F32))


def ring_sum(call, parts):
    return call(ring_sum_kernel, "ring_sum", shape(*parts[0].shape[1:]), tuple(parts), 16, (), "vv")


def last_sum_kernel(ids, *refs):
    parts, (out, *gain_outs, held) = refs[:-5], refs[-5:]
    half, both = out.shape
    ring, _, rows = held.shape
    four = both // 2
    out[...] = low(sum(item[:half].astype(F32) for item in parts))
    gains = sum(gain_values(item[half:].astype(F32), four, ring * rows) for item in parts)
    for z in range(ring):
        held[z] = gains[:, z * rows : (z + 1) * rows]
    for i, gain_out in enumerate(gain_outs):
        gain_out[...] = held[ids[0], i]


def last_sum(call, parts, rows):
    more, both = parts[0].shape
    half = rows // 2
    return call(
        last_sum_kernel, "last_sum", (shape(half, both),) + (shape32(rows),) * 3, tuple(parts), 16,
        [pltpu.VMEM((len(parts), 3, rows), F32)], "i" + "v" * len(parts),
    )


def place_pieces(ids, own, other, held):
    for by in range(own.shape[0]):
        held[ids[1] ^ by, ids[2]] = own[by]
        held[ids[1] ^ by, 1 - ids[2]] = other[by]


def first_out_kernel(ids, *refs, chips):
    own, other, in_out, out_out, held = refs
    place_pieces(ids, own, other, held)
    half, wide = held.shape[2:]
    span = wide // 2
    width = out_out.shape[1]
    few = half * span // width
    for j in range(chips):
        for c in range(2):
            rows = slice(c * half, (c + 1) * half)
            in_out[rows, j * span : (j + 1) * span] = held[j, c, :, :span].astype(F32)
            for v in range(width // span):
                at = (2 * j + c) * few
                out_out[at : at + few, v * span : (v + 1) * span] = held[
                    j, c, v * few : (v + 1) * few, span : 2 * span
                ].astype(F32)


def first_out(call, own, other, units, width):
    chips, half, wide = own.shape
    rows = 2 * half
    return call(
        functools.partial(first_out_kernel, chips=chips), "first_out",
        (shape32(rows, units), shape32(rows * units // width, width)),
        (own, other), 24, [pltpu.VMEM((chips, 2, half, wide), BF)], "ivv",
    )


def last_out_kernel(ids, *refs, chips):
    own, other, outs, held = refs[0], refs[1], refs[2:-1], refs[-1]
    place_pieces(ids, own, other, held)
    half, both = held.shape[2:]
    four, two = both // 2, both // 4
    for j in range(chips):
        for c in range(2):
            rows = slice(c * half, (c + 1) * half)
            at = j % (chips // 4) * four
            outs[j * 4 // chips][rows, at : at + four] = held[j, c, :, :four].astype(F32)
            at = j % (chips // 2) * two
            outs[4 + j * 2 // chips][rows, at : at + two] = held[j, c, :, four : four + two].astype(F32)
            outs[6 + j * 2 // chips][rows, at : at + two] = held[j, c, :, four + two :].astype(F32)


def last_out(call, own, other, width):
    chips, half, both = own.shape
    return call(
        functools.partial(last_out_kernel, chips=chips), "last_out", (shape32(2 * half, width),) * 8,
        (own, other), 24, [pltpu.VMEM((chips, 2, half, both), BF)], "ivv",
    )


def swap(values, axis, by):
    peers = lax.axis_size(axis)
    return lax.ppermute(values, axis, [(i, i ^ by) for i in range(peers)])


def over_chips(blocks):
    return [blocks[0]] + [swap(item, "pb", 2 * by) for by, item in enumerate(blocks) if by]


def over_ring(blocks):
    return [blocks[0]] + [swap(item, "pa", by) for by, item in enumerate(blocks) if by]


def over_core(blocks):
    return [swap(item, "pb", 1) for item in blocks]


def body(
    hidden, encoder, lengths, w_sq, w_sk, w_sv, w_so, w_cq, w_ck, w_cv, w_co, w_in, w_out,
    gain_self, gain_cross, gain_ffn, cotangent,
):
    _, tokens, width = hidden.shape
    questions, _, passage_len, _ = encoder.shape
    units = w_in.shape[1]
    ring = lax.axis_size("pa")
    chips = lax.axis_size("pb") // 2
    true_len = lengths.reshape(questions)
    hidden2 = hidden.reshape(tokens, width)
    cot = cotangent.reshape(tokens, width)
    enc = encoder.reshape(questions * passage_len, width)

    call = Line()
    x_self, self_q, self_k, self_v, self_mix, mixture, logs, after_self, x_cross, cross_q = self_forward(
        call, hidden2, gain_self, gain_cross, (w_sq, w_sk, w_sv, w_so, w_cq)
    )
    asked = over_ring([cross_q] * ring)
    keys, values = key_values(call, enc, w_ck, w_cv, passage_len)
    near = chips - 1
    order = [0] + list(range(2, ring)) + [1]
    partial = {}
    for step in order:
        last = step == order[-1]
        partial[step] = cross_forward(call, true_len, asked[step], keys, values, step, (), 1 if last else None)
        if step == 0:
            early = list(early_pack(call, x_self, self_mix, cot, after_self, chips))
    partial = [partial[step] for step in range(ring)]
    early[near] = hold(call, early[near], (w_co, w_in, w_out, after_self, cot, gain_ffn))
    early = over_chips(early)
    packed = over_ring(partial)
    call.meet(1, packed[2:3])
    call.meet(0, packed[3:])
    call.meet(3)
    found = feed_forward(call, after_self, cot, gain_ffn, w_co, w_in, w_out, packed)
    result, grad_after_cross, g_cross, sent, grad_gain_ffn, cross_mix, activated, grad_pre = found
    given = over_ring([sent] * ring)
    middle = list(middle_pack(call, cross_mix, activated, grad_pre, ring, chips))
    call.meet(0, early[1:])
    back = {}
    for step in [0] + list(range(2, ring)) + [1]:
        back[step] = cross_backward(call, true_len, asked[step], given[step], keys, values, step)
        if step == 0:
            sent = given[1] = swap(hold(call, sent), "pa", 1)
    middle = over_chips(middle)
    partial = over_ring([back[step][0] for step in range(ring)])
    grad_keys, grad_values = [back[step][1] for step in range(ring)], [back[step][2] for step in range(ring)]
    key_keep, key_give = key_grads(call, enc, grad_keys, grad_values, ring)
    ffn_keep, ffn_give = ffn_grads(
        call, w_co, gain_ffn, early, middle, ring, units, (hidden2, after_self, logs, mixture, gain_self, gain_cross)
    )
    call.meet(0, partial[2:])
    call.meet(20, ())
    key_parts = key_sum(call, key_keep, swap(key_give, "pb", 1), chips)
    first = first_sum(call, ffn_keep, swap(ffn_give, "pb", 1))
    found = self_backward(
        call,
        (grad_after_cross, after_self, hidden2, gain_self, gain_cross, grad_gain_ffn, g_cross,
         self_q, self_k, self_v, mixture, logs),
        (w_cq, w_so, w_sq, w_sk, w_sv),
        partial,
        chips,
    )
    grad_hidden = found[0]
    late = over_chips(found[1:])
    key_parts = halve(call, "key_add", "pb", *key_parts, 2)
    first = halve(call, "first_add", "pa", *first, 1)
    call.meet(1, late[3:])
    keep, give = tail_grads(call, gain_cross, early, middle, late, ring)
    call.meet(0, [key_parts[1], first[1]])
    call.meet(12)
    last = over_ring(tail_sum(call, keep, swap(give, "pb", 1), key_parts, chips))
    first = over_chips([ring_sum(call, first)] * chips)
    grad_encoder = encoder_grad(call, w_ck, w_cv, grad_keys, grad_values)
    call.meet(1, last[2:])
    last, *gains = last_sum(call, last, width // ring)
    last = over_chips([last] * chips)
    first = pack(call, first)
    last = pack(call, last)
    grad_in, grad_out = first_out(call, first, swap(first, "pb", 1), units, width)
    grad_sq, grad_sk, grad_sv, grad_so, grad_co, grad_cq, grad_ck, grad_cv = last_out(
        call, last, swap(last, "pb", 1), width
    )
    return (
        result.reshape(hidden.shape),
        grad_hidden.reshape(hidden.shape),
        grad_encoder.reshape(encoder.shape),
        grad_sq,
        grad_sk,
        grad_sv,
        grad_so,
        grad_cq,
        grad_ck,
        grad_cv,
        grad_co,
        grad_in,
        grad_out,
        gains[0],
        gains[1],
        gains[2],
    )


def solution(mesh):
    split = P(("pb", "pa"), None, None)
    passages = P("pb", "pa", None, None)
    return jax.shard_map(
        body,
        mesh=mesh,
        in_specs=(split, passages, P("pb", "pa")) + (P(),) * 13 + (split,),
        out_specs=(split, split, passages) + (P("pa", None),) * 10 + (P("pa"),) * 3,
        check_vma=False,
    )
```

```python
import functools

import jax
import jax.numpy as jnp
from jax import lax
from jax.experimental import pallas as pl
from jax.experimental.pallas import tpu as pltpu
from jax.sharding import PartitionSpec as P

HEADS = 12
EPS = 1e-06
NEG = -1000000000.0
F32 = jnp.float32
BF = jnp.bfloat16
SLOTS = 4
LANES = 128
MIB = 1 << 20


def dot(left, right, left_dim, right_dim, precision=None):
    return lax.dot_general(
        left,
        right,
        (((left_dim,), (right_dim,)), ((), ())),
        precision=precision,
        preferred_element_type=F32,
    )


def nn(left, right):
    return dot(left, right, 1, 0)


def nt(left, right):
    return dot(left, right, 1, 1)


def tn(left, right):
    return dot(left, right, 0, 0)


def low(values):
    return values.astype(BF)


def inverse_rms(values):
    return lax.rsqrt(jnp.mean(values * values, axis=-1, keepdims=True) + EPS)


def norm_back(grad, values, gain):
    inv = inverse_rms(values)
    scaled = gain * grad
    inner = jnp.mean(values * scaled, axis=-1, keepdims=True)
    grad_values = inv * scaled - values * (inv * inv * inv * inner)
    grad_gain = jnp.sum(grad * values * inv, axis=0, keepdims=True)
    return grad_values, grad_gain


def lanes_of(shape):
    return lax.broadcasted_iota(jnp.int32, shape, len(shape) - 1)


def rows_of(shape):
    return lax.broadcasted_iota(jnp.int32, shape, len(shape) - 2)


def ones_where(condition):
    return jnp.where(condition, 1.0, 0.0).astype(BF)


def spread_matrix(width):
    slot, lane = rows_of((LANES, width)), lanes_of((LANES, width))
    return ones_where((slot // SLOTS == lane // (width // HEADS)) & (slot % SLOTS < 2))


def compact_matrix():
    slot, lane = rows_of((LANES, LANES)), lanes_of((LANES, LANES))
    return ones_where((slot // SLOTS == lane // SLOTS) & (slot % SLOTS < 2))


def gather_matrix(width):
    feature, lane = rows_of((width, LANES)), lanes_of((width, LANES))
    return ones_where(feature // (width // HEADS) == lane // SLOTS)


def split_three(values):
    first = low(values).astype(F32)
    rest = values - first
    second = low(rest).astype(F32)
    third = low(rest - second).astype(F32)
    return first, second, third


def in_slots(values, start=0):
    first, second, _ = split_three(values)
    slot = lanes_of(values.shape) % SLOTS - start
    return jnp.where(slot == 0, first, jnp.where(slot == 1, second, 0.0))


def to_rows(extra, width):
    turned = jnp.transpose(extra)
    few = HEADS * SLOTS * extra.shape[0] // width
    return jnp.concatenate([turned[at : at + few] for at in range(0, HEADS * SLOTS, few)], 1)


def from_rows(rows, tokens):
    few = rows.shape[0]
    parts = [rows[:, at : at + tokens].astype(F32) for at in range(0, rows.shape[1], tokens)]
    parts.append(jnp.zeros((LANES - few * len(parts), tokens), F32))
    return low(jnp.transpose(jnp.concatenate(parts, 0)))


def few_rows(tokens, width):
    return HEADS * SLOTS * tokens // width


def head_sums(values, matrix):
    first, second, third = split_three(values)
    return nn(low(first), matrix) + nn(low(second), matrix) + nn(low(third), matrix)


def two_heads(block):
    first = lanes_of(block.shape) < block.shape[1] // 2
    zero = jnp.zeros_like(block)
    return jnp.concatenate([jnp.where(first, block, zero), jnp.where(first, zero, block)], 0)


def fold_heads(block):
    half = block.shape[0] // 2
    lane = lanes_of((half, block.shape[1]))
    return jnp.where(lane < block.shape[1] // 2, block[:half], block[half:])


def pair_of_slots(extra, pair, start, more=None):
    lane = lanes_of(extra.shape)
    slot = lane % SLOTS
    wanted = (slot >= start) & (slot < start + 2)
    halves = [
        jnp.where(wanted & (lane // SLOTS == 2 * pair + i), extra, jnp.zeros_like(extra)) for i in range(2)
    ]
    block = jnp.concatenate(halves, 0)
    return block if more is None else block + more


def last_lane(rows, value):
    return jnp.where(lanes_of((rows, LANES)) == LANES - 1, value, 0.0).astype(BF)


def attend_pair(queries, keys, values, valid=None):
    scores = nt(keys, queries)
    if valid is not None:
        scores = jnp.where(valid, scores, NEG)
    top = jnp.max(scores, axis=0, keepdims=True)
    weights = low(jnp.exp(scores - top))
    both = tn(weights, values)
    split = both.shape[1] - LANES
    mixture = fold_heads(both[:, :split]) * (1.0 / fold_heads(both[:, split:]))
    return mixture, both[:, split:], top


def log_totals(sums, tops):
    tokens = tops[0].shape[1] // 2
    lane = lanes_of((tokens, LANES)) // SLOTS
    found = jnp.ones((tokens, LANES), F32)
    rows = []
    for pair, (both, top) in enumerate(zip(sums, tops)):
        found = jnp.where(lane == 2 * pair, both[:tokens], jnp.where(lane == 2 * pair + 1, both[tokens:], found))
        rows += [jnp.broadcast_to(top[:, :tokens], (SLOTS, tokens)), jnp.broadcast_to(top[:, tokens:], (SLOTS, tokens))]
    rows.append(jnp.zeros((LANES - HEADS * SLOTS, tokens), F32))
    return jnp.transpose(jnp.concatenate(rows, 0)) + jnp.log(found)


def attend_pair_back(queries, keys, values, grad_mix, query_more, key_more, grad_more, value_more, valid=None):
    scaled = two_heads(queries)
    grad_two = two_heads(grad_mix)
    scores = nt(jnp.concatenate([keys, key_more], 1), jnp.concatenate([scaled, query_more], 1))
    probs = jnp.exp(scores)
    if valid is not None:
        probs = jnp.where(valid, probs, 0.0)
    grad_probs = nt(jnp.concatenate([values, value_more], 1), jnp.concatenate([grad_two, grad_more], 1))
    grad_scores = low(probs * grad_probs)
    grad_values = nn(low(probs), grad_two)
    grad_keys = nn(grad_scores, scaled)
    grad_queries = fold_heads(tn(grad_scores, keys))
    return grad_queries, grad_keys, grad_values


def minus_slots(rows, start):
    slot = lanes_of((rows, LANES)) % SLOTS
    return jnp.where((slot >= start) & (slot < start + 2), -1.0, 0.0)


def causal_mask(tokens):
    key = rows_of((tokens, 2 * tokens))
    token = lanes_of((tokens, 2 * tokens))
    return key <= jnp.where(token >= tokens, token - tokens, token)


WEIGHTS = {
    "self_forward": 0,
    "key_values": 5,
    "cross_forward": 1,
    "feed_forward": 5,
    "cross_backward": 4,
    "key_grads": 1,
    "ffn_grads": 0,
    "first_sum": 0,
    "self_backward": 20,
    "early_pack": 0,
    "middle_pack": 0,
    "encoder_grad": 0,
    "ring_sum": 0,
    "tail_grads": 0,
    "tail_sum": 0,
    "first_out": 0,
    "last_sum": 0,
    "last_out": 0,
    "meet": 0,
    "pack": 0,
    "hold": 0,
    "key_sum": 0,
    "key_add": 0,
    "first_add": 0,
}


class Line:
    def __init__(self):
        self.token = None

    def __call__(self, kernel, name, outs, args, mib, scratch=(), places="", after=(), weight=None):
        kinds = {"s": pltpu.SMEM, "h": pltpu.HBM, "v": pltpu.VMEM}
        placed = places[:1] == "i"
        specs = [pl.BlockSpec(memory_space=kinds[letter]) for letter in places[placed:]]
        count = len(args)
        single = not isinstance(outs, (tuple, list))
        outs = ((outs,) if single else tuple(outs)) + (shape32(8, LANES),)
        given = (() if self.token is None else (self.token,)) + tuple(after)
        homes = [pltpu.HBM if name == "self_forward" else pltpu.VMEM] * (len(outs) - 1) + [pltpu.VMEM]

        def run(*refs):
            at = count + len(given)
            made = refs[at : at + len(outs)]
            made[-1][...] = jnp.zeros((8, LANES), F32)
            here = ()
            if placed:
                lane = lax.axis_index("pb").astype(jnp.int32)
                here = ((lax.axis_index("pa").astype(jnp.int32), lane >> 1, lane & 1),)
            kernel(*here, *refs[:count], *made[:-1], *refs[at + len(outs) :])

        found = pl.pallas_call(
            run,
            out_shape=outs,
            in_specs=specs + [pl.BlockSpec(memory_space=pl.ANY)] * len(given),
            out_specs=[pl.BlockSpec(memory_space=home) for home in homes],
            scratch_shapes=scratch,
            compiler_params=pltpu.CompilerParams(vmem_limit_bytes=mib * MIB),
            cost_estimate=pl.CostEstimate(flops=int(1153000000 * (WEIGHTS[name] if weight is None else weight)), bytes_accessed=0, transcendentals=0),
            name=name,
        )(*args, *given)
        self.token = found[-1]
        return found[0] if single else found[:-1]

    def meet(self, weight, after=()):
        self(lambda *refs: None, "meet", (), (), 4, (), "", after, weight)


def shape(*dims):
    return jax.ShapeDtypeStruct(dims, BF)


def shape32(*dims):
    return jax.ShapeDtypeStruct(dims, F32)


def row(gain):
    return gain[...].reshape(1, gain.shape[0])


def self_forward_kernel(*refs):
    far, outs, refs = refs[:8], refs[8:18], refs[18:]
    held, made, (sems, out_sems) = refs[:8], refs[8:18], refs[18:]
    copies = [pltpu.make_async_copy(item, near, sems.at[i]) for i, (item, near) in enumerate(zip(far, held))]
    for item in copies:
        item.start()
    hidden, gain_self, gain_cross = held[:3]
    weights = held[3:]
    (x_self_out, q_out, k_out, v_out, mix_out, mixture_out, logs_out, after_out, x_cross_out, cross_q_out) = made
    pending = []

    def send(index):
        pending.append(pltpu.make_async_copy(made[index], outs[index], out_sems.at[index]))
        pending[-1].start()

    tokens, width = hidden.shape
    factor = (width // HEADS) ** -0.5
    copies[0].wait()
    copies[1].wait()
    stream = hidden[...].astype(F32)
    x_self = low(stream * inverse_rms(stream) * row(gain_self))
    x_self_out[...] = x_self
    send(0)
    for i in range(3):
        copies[3 + i].wait()
        made[1 + i][...] = low(nn(x_self, weights[i][...]))
        send(1 + i)
    queries, keys, values = (made[1 + i][...] for i in range(3))
    valid = causal_mask(tokens)
    pair_width = 2 * width // HEADS
    ones = jnp.ones((tokens, LANES), BF)
    mixtures, sums, tops = [], [], []
    for pair in range(HEADS // 2):
        part = slice(pair * pair_width, (pair + 1) * pair_width)
        mixture, both, top = attend_pair(
            two_heads(queries[:, part] * factor), keys[:, part], jnp.concatenate([values[:, part], ones], 1), valid
        )
        mixtures.append(mixture)
        sums.append(both)
        tops.append(top)
    mixture = jnp.concatenate(mixtures, 1)
    mixture_out[...] = mixture
    send(5)
    mix = low(mixture)
    mix_out[...] = mix
    send(4)
    logs_out[...] = log_totals(sums, tops)
    send(6)
    copies[2].wait()
    copies[6].wait()
    after_self = stream + nn(mix, weights[3][...])
    after_out[...] = after_self
    send(7)
    x_cross = low(after_self * inverse_rms(after_self) * row(gain_cross))
    x_cross_out[...] = x_cross
    send(8)
    copies[7].wait()
    cross_q_out[...] = low(nn(x_cross, weights[4][...]))
    send(9)
    for item in pending:
        item.wait()


def self_forward(call, hidden, gain_self, gain_cross, weights):
    tokens, width = hidden.shape
    low_one = shape(tokens, width)
    args = (hidden, gain_self, gain_cross) + tuple(weights)
    outs = (low_one,) * 5 + (
        shape32(tokens, width), shape32(tokens, LANES), shape32(tokens, width), low_one, low_one,
    )
    return call(
        self_forward_kernel, "self_forward", outs, args, 56,
        [pltpu.VMEM(item.shape, item.dtype) for item in args + outs]
        + [pltpu.SemaphoreType.DMA((size,)) for size in (len(args), len(outs))],
        "h" * len(args),
    )


def early_pack_kernel(ids, x_self, mix, cot, after_self, *early):
    chips = len(early)
    width = cot.shape[1]
    for by, out in enumerate(early):
        out[:, width : 2 * width] = cot[...]
        out[:, 2 * width :] = low(after_self[...])
        last = lax.div((ids[1] ^ by) * 4, chips) == 3

        @pl.when(last)
        def _():
            out[:, :width] = mix[...]

        @pl.when(jnp.logical_not(last))
        def _():
            out[:, :width] = x_self[...]


def early_pack(call, x_self, mix, cot, after_self, chips):
    tokens, width = cot.shape
    return call(
        early_pack_kernel, "early_pack", (shape(tokens, 3 * width),) * chips, (x_self, mix, cot, after_self), 12, (), "ivvvv"
    )


def key_values_kernel(encoder, w_ck, w_cv, keys, values, *, block):
    def step(index, carry):
        rows = pl.ds(pl.multiple_of(index * block, block), block)
        here = encoder[rows, :]
        keys[rows, :] = low(nn(here, w_ck[...]))
        values[rows, :] = low(nn(here, w_cv[...]))
        return carry

    lax.fori_loop(0, encoder.shape[0] // block, step, 0, unroll=2)


def key_values(call, encoder, w_ck, w_cv, block):
    return call(
        functools.partial(key_values_kernel, block=block), "key_values", (shape(*encoder.shape), shape(*encoder.shape)), (encoder, w_ck, w_cv), 24, (), "vvv"
    )


def key_rows(ids, count, step):
    key_count = count
    return pl.ds(pl.multiple_of((ids[0] ^ step) * key_count, LANES), key_count)


def cross_forward_kernel(ids, lengths, keys, values, queries, out, *, step, key_count):
    tokens, width = queries.shape
    factor = (width // HEADS) ** -0.5
    rows = key_rows(ids, key_count, step)
    size = (key_count, LANES)
    hidden_key = jnp.where(rows_of(size) < lengths[ids[0] ^ step], 0.0, NEG)
    key_more = jnp.where(lanes_of(size) == LANES - 1, hidden_key, 0.0).astype(BF)
    query_more = last_lane(2 * tokens, 1.0)
    ones = jnp.ones(size, BF)
    pair_width = 2 * width // HEADS
    sums, tops = [], []
    for pair in range(HEADS // 2):
        part = slice(pair * pair_width, (pair + 1) * pair_width)
        mixture, both, top = attend_pair(
            jnp.concatenate([two_heads(queries[:, part] * factor), query_more], 1),
            jnp.concatenate([keys[rows, part], key_more], 1),
            jnp.concatenate([values[rows, part], ones], 1),
        )
        out[:tokens, part] = low(mixture)
        sums.append(both)
        tops.append(top)
    out[tokens:] = low(to_rows(in_slots(log_totals(sums, tops)), width))


def cross_forward(call, lengths, queries, keys, values, step, after=(), weight=None):
    tokens, width = queries.shape
    key_count = keys.shape[0] // lengths.shape[0]
    return call(
        functools.partial(cross_forward_kernel, step=step, key_count=key_count),
        "cross_forward", shape(tokens + few_rows(tokens, width), width), (lengths, keys, values, queries), 16, (), "isvvv",
        after, weight,
    )


def feed_forward_kernel(
    after_self, cotangent, gain_ffn, w_co, w_in, w_out, *refs, count, chunks
):
    packed, refs = refs[:count], refs[count:]
    result_out, grad_after_out, g_cross_out, send_out, grad_gain_out, mix_out, act_held, grad_held = refs
    tokens, width = after_self.shape
    units = w_in.shape[1]
    wide = units // chunks
    compact, spread = compact_matrix(), spread_matrix(width)
    logs = [nn(from_rows(part[tokens:], tokens), compact) for part in packed]
    top = functools.reduce(jnp.maximum, logs)
    log_total = top + jnp.log(sum(jnp.exp(item - top) for item in logs))
    mixture = sum(
        nn(low(in_slots(jnp.exp(item - log_total))), spread) * part[:tokens].astype(F32)
        for item, part in zip(logs, packed)
    )
    mix = low(mixture)
    mix_out[...] = mix
    after_cross = after_self[...] + nn(mix, w_co[...])
    x_ffn = low(after_cross * inverse_rms(after_cross) * row(gain_ffn))
    grad_low = cotangent[...]
    slope = (2.0 / 3.141592653589793) ** 0.5

    def step(chunk, carry):
        part = pl.ds(pl.multiple_of(chunk * wide, LANES), wide)
        pre = nn(x_ffn, w_in[:, part])
        square = pre * pre
        bent = jnp.tanh(pre * (slope + (0.044715 * slope) * square))
        act_held[:, part] = low(0.5 * pre * (1.0 + bent))
        grad_act = nt(grad_low, w_out[part, :])
        bend = 0.5 * (1.0 + bent) + 0.5 * pre * (1.0 - bent * bent) * (slope + (3 * 0.044715 * slope) * square)
        grad_held[:, part] = low(grad_act * bend)
        return carry

    lax.fori_loop(0, chunks, step, 0, unroll=True)
    result = after_cross + nn(act_held[...], w_out[...])
    grad_x = nt(grad_held[...], w_in[...])
    result_out[...] = low(result)
    grad_values, grad_gain = norm_back(grad_x, after_cross, row(gain_ffn))
    grad_gain_out[...] = grad_gain
    grad_after = grad_low.astype(F32) + grad_values
    grad_after_out[...] = grad_after
    g_cross = low(grad_after)
    g_cross_out[...] = g_cross
    grad_mix = low(nt(g_cross, w_co[...]))
    delta = head_sums(grad_mix.astype(F32) * mixture, gather_matrix(width))
    send_out[:tokens] = grad_mix
    send_out[tokens:] = low(to_rows(in_slots(log_total) + in_slots(delta, 2), width))


def middle_pack_kernel(ids, mix, act, grad_pre, *refs, count):
    middle, acts, grad_pres = refs[:-2], refs[-2], refs[-1]
    chips, _, span = acts.shape
    width = mix.shape[1]
    units = act.shape[1]
    piece = units // (count * chips)
    for which in range(units // piece):
        slot = which // chips * piece
        acts[which % chips, :, slot : slot + piece] = act[:, which * piece : (which + 1) * piece]
    for which in range(chips):
        grad_pres[which] = grad_pre[:, which * span : (which + 1) * span]
    for by, out in enumerate(middle):
        index = ids[1] ^ by
        out[:, :width] = mix[...]
        out[:, width : width + span] = acts[index]
        out[:, width + span :] = grad_pres[index]


def middle_pack(call, mix, act, grad_pre, count, chips):
    tokens, width = mix.shape
    span = act.shape[1] // chips
    return call(
        functools.partial(middle_pack_kernel, count=count), "middle_pack", (shape(tokens, width + 2 * span),) * chips,
        (mix, act, grad_pre), 16, [pltpu.VMEM((chips, tokens, span), BF)] * 2, "ivvv",
    )


def feed_forward(call, after_self, cotangent, gain_ffn, w_co, w_in, w_out, packed):
    tokens, width = after_self.shape
    units = w_in.shape[1]
    return call(
        functools.partial(feed_forward_kernel, count=len(packed), chunks=4),
        "feed_forward",
        (shape(tokens, width), shape32(tokens, width), shape(tokens, width),
         shape(tokens + few_rows(tokens, width), width), shape32(1, width), shape(tokens, width),
         shape(tokens, units), shape(tokens, units)),
        (after_self, cotangent, gain_ffn, w_co, w_in, w_out) + tuple(packed),
        28,
        (),
        "vvvvvv" + "v" * len(packed),
    )


def cross_backward_kernel(ids, lengths, keys, values, queries, grads, grad_queries, grad_keys, grad_values, *, step):
    tokens, width = queries.shape
    key_count = grad_keys.shape[0]
    factor = (width // HEADS) ** -0.5
    rows = key_rows(ids, key_count, step)
    size = (key_count, LANES)
    hidden_key = jnp.where(rows_of(size) < lengths[ids[0] ^ step], 0.0, NEG)
    key_more = jnp.where(lanes_of(size) == LANES - 1, hidden_key, minus_slots(key_count, 0)).astype(BF)
    value_more = minus_slots(key_count, 2).astype(BF)
    extra = from_rows(grads[tokens:], tokens)
    one = last_lane(2 * tokens, 1.0)
    pair_width = 2 * width // HEADS
    for pair in range(HEADS // 2):
        part = slice(pair * pair_width, (pair + 1) * pair_width)
        grad_q, grad_k, grad_v = attend_pair_back(
            queries[:, part] * factor, keys[rows, part], values[rows, part], grads[:tokens, part],
            pair_of_slots(extra, pair, 0, one), key_more, pair_of_slots(extra, pair, 2), value_more,
        )
        grad_queries[:, part] = low(grad_q * factor)
        grad_keys[:, part] = low(grad_k)
        grad_values[:, part] = low(grad_v)


def cross_backward(call, lengths, queries, grads, keys, values, step):
    tokens, width = queries.shape
    key_count = keys.shape[0] // lengths.shape[0]
    return call(
        functools.partial(cross_backward_kernel, step=step),
        "cross_backward",
        (shape(tokens, width), shape(key_count, width), shape(key_count, width)),
        (lengths, keys, values, queries, grads), 20, (), "isvvvv",
    )


def extra_rows(four, width):
    return -(-6 * width // four // 8) * 8


def gain_block(gains, four, width_out):
    count = gains.shape[1] // four
    few = extra_rows(four, gains.shape[1])
    high = low(gains).astype(F32)
    rows = [part[i : i + 1, v * four : (v + 1) * four] for part in (high, gains - high) for i in range(3) for v in range(count)]
    block = jnp.concatenate(rows + [jnp.zeros((few - len(rows), four), F32)], 0)
    return low(jnp.concatenate([block, jnp.zeros((few, width_out - four), F32)], 1))


def gain_values(block, four, width):
    count = width // four
    rows = []
    for i in range(3):
        pieces = [
            block[i * count + v : i * count + v + 1, :four] + block[(3 + i) * count + v : (3 + i) * count + v + 1, :four]
            for v in range(count)
        ]
        rows.append(jnp.concatenate(pieces, 1))
    return jnp.concatenate(rows, 0)


def self_backward_kernel(
    ids, grad_after_cross, after_self, hidden, gain_self, gain_cross, grad_gain_ffn, g_cross,
    self_q, self_k, self_v, mixture, logs, *refs, count, chips
):
    weights, partial, refs = refs[:5], refs[5 : 5 + count], refs[5 + count :]
    hidden_out, late = refs[0], refs[1 : 1 + chips]
    fours, twos = refs[1 + chips :]
    tokens, width = after_self.shape
    factor = (width // HEADS) ** -0.5
    four, two = 4 * width // chips, 2 * width // chips
    grad_cq = low(sum(item[...].astype(F32) for item in partial))
    grad_values, grad_gain_cross = norm_back(nt(grad_cq, weights[0][...]), after_self[...], row(gain_cross))
    grad_after = grad_after_cross[...] + grad_values
    g_self = low(grad_after)
    grad_mix = low(nt(g_self, weights[1][...]))
    delta = head_sums(grad_mix.astype(F32) * mixture[...], gather_matrix(width))
    extra = low(in_slots(logs[...]) + in_slots(delta, 2))
    valid = causal_mask(tokens)
    key_more = minus_slots(tokens, 0).astype(BF)
    value_more = minus_slots(tokens, 2).astype(BF)
    pair_width = 2 * width // HEADS
    found = []
    for pair in range(HEADS // 2):
        part = slice(pair * pair_width, (pair + 1) * pair_width)
        grad_q, grad_k, grad_v = attend_pair_back(
            self_q[:, part] * factor, self_k[:, part], self_v[:, part], grad_mix[:, part],
            pair_of_slots(extra, pair, 0), key_more, pair_of_slots(extra, pair, 2), value_more, valid,
        )
        found.append((low(grad_q * factor), low(grad_k), low(grad_v)))
    grads = [jnp.concatenate([item[i] for item in found], 1) for i in range(3)]
    grad_x = jnp.zeros((tokens, width), F32)
    for i in range(3):
        grad_x = grad_x + nt(grads[i], weights[2 + i][...])
    grad_values, grad_gain_self = norm_back(grad_x, hidden[...].astype(F32), row(gain_self))
    hidden_out[...] = low(grad_after + grad_values)
    gains = jnp.concatenate([grad_gain_self, grad_gain_cross, grad_gain_ffn[...]], 0)
    block = gain_block(gains, four, four + two)
    for i, item in enumerate(grads + [g_self]):
        for v in range(width // four):
            fours[i * (width // four) + v] = item[:, v * four : (v + 1) * four]
    for i, item in enumerate((g_cross[...], grad_cq)):
        for v in range(width // two):
            twos[i * (width // two) + v] = item[:, v * two : (v + 1) * two]
    chip = ids[1]
    for by, out in enumerate(late):
        out[:tokens, :four] = fours[chip ^ by]
        out[:tokens, four:] = twos[chip ^ by]
        out[tokens:] = block


def self_backward(call, first, weights, partial, chips):
    tokens, width = first[1].shape
    four, two = 4 * width // chips, 2 * width // chips
    return call(
        functools.partial(self_backward_kernel, count=len(partial), chips=chips),
        "self_backward",
        (shape(tokens, width),) + (shape(tokens + extra_rows(four, width), four + two),) * chips,
        tuple(first) + tuple(weights) + tuple(partial),
        20,
        [pltpu.VMEM((chips, tokens, four), BF), pltpu.VMEM((chips, tokens, two), BF)],
        "i" + "v" * (len(first) + 5 + len(partial)),
    )


def stacked(refs, rows, lanes):
    return jnp.concatenate([item[rows, lanes] for item in refs], 0)


def hand_out(ids, held, keep, give):
    core = ids[2]
    keep[...] = held[core]
    give[...] = held[1 - core]


def ffn_grads_kernel(ids, w_co, gain_ffn, *refs, chips):
    early, middle, (keep, give, held) = refs[:chips], refs[chips : 2 * chips], refs[-3:]
    _, ring, half, both = held.shape
    span = both // 2
    width = early[0].shape[1] // 3
    every = slice(None)
    mix = stacked(middle, every, slice(0, width))
    after_cross = stacked(early, every, slice(2 * width, 3 * width)).astype(F32) + nn(mix, w_co[...])
    x_ffn = low(after_cross * inverse_rms(after_cross) * row(gain_ffn))
    grad_in = low(tn(x_ffn, stacked(middle, every, slice(width + span, width + 2 * span))))
    for z in range(ring):
        for c in range(2):
            at = (2 * z + c) * half
            held[c, z, :, :span] = grad_in[at : at + half]
    grad_out = low(
        tn(stacked(middle, every, slice(width, width + span)), stacked(early, every, slice(width, 2 * width)))
    )
    few = span // (2 * ring)
    for z in range(ring):
        for c in range(2):
            at = (2 * z + c) * few
            block = grad_out[at : at + few]
            held[c, z, :, span:] = jnp.concatenate([block[:, v : v + span] for v in range(0, width, span)], 0)
    hand_out(ids, held, keep, give)


def ffn_grads(call, w_co, gain_ffn, early, middle, ring, units, more):
    chips = len(early)
    width = early[0].shape[1] // 3
    part = (ring, width // (2 * ring), 2 * units // chips)
    return call(
        functools.partial(ffn_grads_kernel, chips=chips), "ffn_grads", (shape(*part),) * 2,
        (w_co, gain_ffn) + tuple(early) + tuple(middle) + tuple(more), 28, [pltpu.VMEM((2,) + part, BF)],
        "ivv" + "v" * (2 * chips + len(more)),
    )


def key_grads_kernel(ids, encoder, *refs):
    grads, (keep, give, held) = refs[:-3], refs[-3:]
    count = len(grads) // 2
    _, ring, half, both = held.shape
    width = both // 2
    key_count = grads[0].shape[0]
    rows = jnp.concatenate([encoder[key_rows(ids, key_count, step), :] for step in range(count)], 0)
    for i in range(2):
        grad = low(tn(rows, stacked(grads[i * count : (i + 1) * count], slice(None), slice(None))))
        for z in range(ring):
            for c in range(2):
                at = (2 * z + c) * half
                held[c, z, :, i * width : (i + 1) * width] = grad[at : at + half]
    hand_out(ids, held, keep, give)


def key_grads(call, encoder, grad_keys, grad_values, ring):
    width = encoder.shape[1]
    part = (ring, width // (2 * ring), 2 * width)
    return call(
        key_grads_kernel, "key_grads", (shape(*part),) * 2, (encoder,) + tuple(grad_keys) + tuple(grad_values), 32,
        [pltpu.VMEM((2,) + part, BF)], "iv" + "v" * (2 * len(grad_keys)),
    )


def encoder_grad_kernel(ids, w_ck, w_cv, *refs):
    grads, out, held = refs[:-2], refs[-2], refs[-1]
    count = len(grads) // 2
    key_count = grads[0].shape[0]
    for index, item in enumerate(grads):
        held[index] = item[...]

    def step(index, carry):
        rows = pl.ds(pl.multiple_of((ids[0] ^ index) * key_count, LANES), key_count)
        out[rows, :] = low(nt(held[index], w_ck[...]) + nt(held[count + index], w_cv[...]))
        return carry

    lax.fori_loop(0, count, step, 0)


def encoder_grad(call, w_ck, w_cv, grad_keys, grad_values):
    key_count, width = grad_keys[0].shape
    return call(
        encoder_grad_kernel, "encoder_grad", shape(key_count * len(grad_keys), width),
        (w_ck, w_cv) + tuple(grad_keys) + tuple(grad_values), 12 + 3 * len(grad_keys),
        [pltpu.VMEM((2 * len(grad_keys), key_count, width), BF)], "ivv" + "v" * (2 * len(grad_keys)),
    )


def key_sum_kernel(ids, keep, came, even, odd, held):
    chips, two = held.shape[0], held.shape[3]
    summed = low(keep[...].astype(F32) + came[...].astype(F32))
    for j in range(chips):
        held[j] = summed[:, :, j * two : (j + 1) * two]
    for by in range(chips):
        (even, odd)[by % 2][by // 2] = held[ids[1] ^ by]


def key_sum(call, keep, came, chips):
    ring, half, both = keep.shape
    part = (ring, half, both // chips)
    return call(
        key_sum_kernel, "key_sum", (shape(chips // 2, *part),) * 2, (keep, came), 20, [pltpu.VMEM((chips,) + part, BF)],
        "ivv",
    )


def first_sum_kernel(ids, keep, came, *outs):
    for by in range(keep.shape[0]):
        z = ids[0] ^ by
        outs[by % 2][by // 2] = low(keep[z].astype(F32) + came[z].astype(F32))


def first_sum(call, keep, came):
    part = (keep.shape[0] // 2,) + keep.shape[1:]
    return call(first_sum_kernel, "first_sum", (shape(*part),) * 2, (keep, came), 16, (), "ivv")


def hold_kernel(item, *refs):
    refs[-1][...] = item[...]


def hold(call, item, near=()):
    return call(hold_kernel, "hold", shape(*item.shape), (item, *near), 24, (), "v" * (1 + len(near)))


def pack_kernel(*refs):
    for at, item in enumerate(refs[:-1]):
        refs[-1][at] = item[...]


def pack(call, parts):
    return call(pack_kernel, "pack", shape(len(parts), *parts[0].shape), tuple(parts), 16, (), "v" * len(parts))


def add_halves_kernel(*refs, count, inner):
    keep, came, outs = refs[: 1 if inner else count], refs[1 if inner else count], refs[2 if inner else count + 1 :]
    for at in range(count):
        mine = keep[0][at] if inner else keep[at][...]
        outs[at % 2][at // 2] = low(mine.astype(F32) + came[at].astype(F32))


def add_halves(call, name, keep, came):
    inner = not isinstance(keep, (tuple, list))
    count = came.shape[0]
    part = (count // 2,) + came.shape[1:]
    args = (keep,) if inner else tuple(keep)
    return call(
        functools.partial(add_halves_kernel, count=count, inner=inner), name, (shape(*part),) * 2, args + (came,), 16, (),
        "v" * (len(args) + 1),
    )


def halve(call, name, axis, keep, give, by):
    came = swap(give, axis, by)
    if came.shape[0] == 1:
        return keep, came
    keep, give = add_halves(call, name, keep, came)
    return halve(call, name, axis, keep, give, 2 * by)


def tail_grads_kernel(ids, gain_cross, *refs, chips):
    early, middle, late = refs[:chips], refs[chips : 2 * chips], refs[2 * chips : 3 * chips]
    keep, give, held, chosen = refs[3 * chips :]
    _, ring, more, both = held.shape
    four = both // 3 * 2
    width = early[0].shape[1] // 3
    half = more - extra_rows(four, width)
    tokens = early[0].shape[0]
    every, rows = slice(None), slice(0, tokens)
    first = lax.div(ids[1] * 2, chips) == 0

    @pl.when(first)
    def _():
        chosen[...] = stacked(middle, every, slice(0, width))

    @pl.when(jnp.logical_not(first))
    def _():
        after_self = stacked(early, every, slice(2 * width, 3 * width)).astype(F32)
        chosen[...] = low(after_self * inverse_rms(after_self) * row(gain_cross))

    grads = (
        (low(tn(stacked(early, every, slice(0, width)), stacked(late, rows, slice(0, four)))), slice(0, four)),
        (low(tn(chosen[...], stacked(late, rows, slice(four, both)))), slice(four, both)),
    )
    gains = sum(gain_values(item[tokens:].astype(F32), four, width) for item in late)
    block = gain_block(gains, four, both)
    for z in range(ring):
        for c in range(2):
            at = (2 * z + c) * half
            for grad, lanes in grads:
                held[c, z, :half, lanes] = grad[at : at + half]
            held[c, z, half:, :] = block
    hand_out(ids, held, keep, give)


def tail_grads(call, gain_cross, early, middle, late, ring):
    chips = len(early)
    width = early[0].shape[1] // 3
    both = late[0].shape[1]
    part = (ring, width // (2 * ring) + extra_rows(both // 3 * 2, width), both)
    return call(
        functools.partial(tail_grads_kernel, chips=chips), "tail_grads", (shape(*part),) * 2,
        (gain_cross,) + tuple(early) + tuple(middle) + tuple(late), 28,
        [pltpu.VMEM((2,) + part, BF), pltpu.VMEM((chips * early[0].shape[0], width), BF)], "iv" + "v" * (3 * chips),
    )


def tail_sum_kernel(ids, keep, came, part, more, *outs, chips):
    both = keep.shape[2]
    four = both // 3 * 2
    width = four * chips // 4
    half = keep.shape[1] - extra_rows(four, width)
    gains = gain_values(keep[0, half:].astype(F32), four, width) + gain_values(came[0, half:].astype(F32), four, width)
    block = gain_block(gains, four, outs[0].shape[1])
    for by, out in enumerate(outs):
        z = ids[0] ^ by
        out[:half, :both] = low(keep[z, :half].astype(F32) + came[z, :half].astype(F32))
        out[:half, both:] = low(part[0, z].astype(F32) + more[0, z].astype(F32))
        out[half:] = block


def tail_sum(call, keep, came, parts, chips):
    ring, more, both = keep.shape
    return call(
        functools.partial(tail_sum_kernel, chips=chips), "tail_sum",
        (shape(more, both + parts[0].shape[3]),) * ring, (keep, came) + tuple(parts), 16, (), "ivvvv",
    )


def ring_sum_kernel(keep, came, out):
    out[...] = low(keep[0].astype(F32) + came[0].astype(F32))


def ring_sum(call, parts):
    return call(ring_sum_kernel, "ring_sum", shape(*parts[0].shape[1:]), tuple(parts), 16, (), "vv")


def last_sum_kernel(ids, *refs):
    parts, (out, *gain_outs, held) = refs[:-5], refs[-5:]
    half, both = out.shape
    ring, _, rows = held.shape
    four = both // 2
    out[...] = low(sum(item[:half].astype(F32) for item in parts))
    gains = sum(gain_values(item[half:].astype(F32), four, ring * rows) for item in parts)
    for z in range(ring):
        held[z] = gains[:, z * rows : (z + 1) * rows]
    for i, gain_out in enumerate(gain_outs):
        gain_out[...] = held[ids[0], i]


def last_sum(call, parts, rows):
    more, both = parts[0].shape
    half = rows // 2
    return call(
        last_sum_kernel, "last_sum", (shape(half, both),) + (shape32(rows),) * 3, tuple(parts), 16,
        [pltpu.VMEM((len(parts), 3, rows), F32)], "i" + "v" * len(parts),
    )


def place_pieces(ids, own, other, held):
    for by in range(own.shape[0]):
        held[ids[1] ^ by, ids[2]] = own[by]
        held[ids[1] ^ by, 1 - ids[2]] = other[by]


def first_out_kernel(ids, *refs, chips):
    own, other, in_out, out_out, held = refs
    place_pieces(ids, own, other, held)
    half, wide = held.shape[2:]
    span = wide // 2
    width = out_out.shape[1]
    few = half * span // width
    for j in range(chips):
        for c in range(2):
            rows = slice(c * half, (c + 1) * half)
            in_out[rows, j * span : (j + 1) * span] = held[j, c, :, :span].astype(F32)
            for v in range(width // span):
                at = (2 * j + c) * few
                out_out[at : at + few, v * span : (v + 1) * span] = held[
                    j, c, v * few : (v + 1) * few, span : 2 * span
                ].astype(F32)


def first_out(call, own, other, units, width):
    chips, half, wide = own.shape
    rows = 2 * half
    return call(
        functools.partial(first_out_kernel, chips=chips), "first_out",
        (shape32(rows, units), shape32(rows * units // width, width)),
        (own, other), 24, [pltpu.VMEM((chips, 2, half, wide), BF)], "ivv",
    )


def last_out_kernel(ids, *refs, chips):
    own, other, outs, held = refs[0], refs[1], refs[2:-1], refs[-1]
    place_pieces(ids, own, other, held)
    half, both = held.shape[2:]
    four, two = both // 2, both // 4
    for j in range(chips):
        for c in range(2):
            rows = slice(c * half, (c + 1) * half)
            at = j % (chips // 4) * four
            outs[j * 4 // chips][rows, at : at + four] = held[j, c, :, :four].astype(F32)
            at = j % (chips // 2) * two
            outs[4 + j * 2 // chips][rows, at : at + two] = held[j, c, :, four : four + two].astype(F32)
            outs[6 + j * 2 // chips][rows, at : at + two] = held[j, c, :, four + two :].astype(F32)


def last_out(call, own, other, width):
    chips, half, both = own.shape
    return call(
        functools.partial(last_out_kernel, chips=chips), "last_out", (shape32(2 * half, width),) * 8,
        (own, other), 24, [pltpu.VMEM((chips, 2, half, both), BF)], "ivv",
    )


def swap(values, axis, by):
    peers = lax.axis_size(axis)
    return lax.ppermute(values, axis, [(i, i ^ by) for i in range(peers)])


def over_chips(blocks):
    return [blocks[0]] + [swap(item, "pb", 2 * by) for by, item in enumerate(blocks) if by]


def over_ring(blocks):
    return [blocks[0]] + [swap(item, "pa", by) for by, item in enumerate(blocks) if by]


def over_core(blocks):
    return [swap(item, "pb", 1) for item in blocks]


def body(
    hidden, encoder, lengths, w_sq, w_sk, w_sv, w_so, w_cq, w_ck, w_cv, w_co, w_in, w_out,
    gain_self, gain_cross, gain_ffn, cotangent,
):
    _, tokens, width = hidden.shape
    questions, _, passage_len, _ = encoder.shape
    units = w_in.shape[1]
    ring = lax.axis_size("pa")
    chips = lax.axis_size("pb") // 2
    true_len = lengths.reshape(questions)
    hidden2 = hidden.reshape(tokens, width)
    cot = cotangent.reshape(tokens, width)
    enc = encoder.reshape(questions * passage_len, width)

    call = Line()
    x_self, self_q, self_k, self_v, self_mix, mixture, logs, after_self, x_cross, cross_q = self_forward(
        call, hidden2, gain_self, gain_cross, (w_sq, w_sk, w_sv, w_so, w_cq)
    )
    asked = over_ring([cross_q] * ring)
    keys, values = key_values(call, enc, w_ck, w_cv, passage_len)
    near = chips - 1
    order = [0] + list(range(2, ring)) + [1]
    partial = {}
    for step in order:
        last = step == order[-1]
        partial[step] = cross_forward(call, true_len, asked[step], keys, values, step, (), 1 if last else None)
        if step == 0:
            early = list(early_pack(call, x_self, self_mix, cot, after_self, chips))
    partial = [partial[step] for step in range(ring)]
    early[near] = hold(call, early[near], (w_co, w_in, w_out, after_self, cot, gain_ffn))
    early = over_chips(early)
    packed = over_ring(partial)
    call.meet(1, packed[2:3])
    call.meet(0, packed[3:])
    call.meet(3)
    found = feed_forward(call, after_self, cot, gain_ffn, w_co, w_in, w_out, packed)
    result, grad_after_cross, g_cross, sent, grad_gain_ffn, cross_mix, activated, grad_pre = found
    given = over_ring([sent] * ring)
    middle = list(middle_pack(call, cross_mix, activated, grad_pre, ring, chips))
    call.meet(0, early[1:])
    back = {}
    for step in [0] + list(range(2, ring)) + [1]:
        back[step] = cross_backward(call, true_len, asked[step], given[step], keys, values, step)
        if step == 0:
            sent = given[1] = swap(hold(call, sent), "pa", 1)
    middle = over_chips(middle)
    partial = over_ring([back[step][0] for step in range(ring)])
    grad_keys, grad_values = [back[step][1] for step in range(ring)], [back[step][2] for step in range(ring)]
    key_keep, key_give = key_grads(call, enc, grad_keys, grad_values, ring)
    ffn_keep, ffn_give = ffn_grads(
        call, w_co, gain_ffn, early, middle, ring, units, (hidden2, after_self, logs, mixture, gain_self, gain_cross)
    )
    call.meet(0, partial[2:])
    call.meet(20, ())
    key_parts = key_sum(call, key_keep, swap(key_give, "pb", 1), chips)
    first = first_sum(call, ffn_keep, swap(ffn_give, "pb", 1))
    found = self_backward(
        call,
        (grad_after_cross, after_self, hidden2, gain_self, gain_cross, grad_gain_ffn, g_cross,
         self_q, self_k, self_v, mixture, logs),
        (w_cq, w_so, w_sq, w_sk, w_sv),
        partial,
        chips,
    )
    grad_hidden = found[0]
    late = over_chips(found[1:])
    key_parts = halve(call, "key_add", "pb", *key_parts, 2)
    first = halve(call, "first_add", "pa", *first, 1)
    call.meet(1, late[3:])
    keep, give = tail_grads(call, gain_cross, early, middle, late, ring)
    call.meet(0, [key_parts[1], first[1]])
    call.meet(12)
    last = over_ring(tail_sum(call, keep, swap(give, "pb", 1), key_parts, chips))
    first = over_chips([ring_sum(call, first)] * chips)
    grad_encoder = encoder_grad(call, w_ck, w_cv, grad_keys, grad_values)
    call.meet(1, last[2:])
    last, *gains = last_sum(call, last, width // ring)
    last = over_chips([last] * chips)
    first = pack(call, first)
    last = pack(call, last)
    grad_in, grad_out = first_out(call, first, swap(first, "pb", 1), units, width)
    grad_sq, grad_sk, grad_sv, grad_so, grad_co, grad_cq, grad_ck, grad_cv = last_out(
        call, last, swap(last, "pb", 1), width
    )
    return (
        result.reshape(hidden.shape),
        grad_hidden.reshape(hidden.shape),
        grad_encoder.reshape(encoder.shape),
        grad_sq,
        grad_sk,
        grad_sv,
        grad_so,
        grad_cq,
        grad_ck,
        grad_cv,
        grad_co,
        grad_in,
        grad_out,
        gains[0],
        gains[1],
        gains[2],
    )


def solution(mesh):
    split = P(("pb", "pa"), None, None)
    passages = P("pb", "pa", None, None)
    return jax.shard_map(
        body,
        mesh=mesh,
        in_specs=(split, passages, P("pb", "pa")) + (P(),) * 13 + (split,),
        out_specs=(split, split, passages) + (P("pa", None),) * 10 + (P("pa"),) * 3,
        check_vma=False,
    )
```
